32 devices in a mesh: grp: 2 (over y), wide: 4 (over z), narrow: 2 (over x), sub: 2 (over core).
Axes of the slice: x: 2, y: 2, z: 4, core: 2. Of those that a mesh axis runs over, the one named last changes fastest.
Arguments:
- inverse_slabs: bfloat16 [2, 384, 160000], P(None, 'wide', ('narrow', 'sub')), may hold values from -40 to 40
- potential_noise: bfloat16 [512, 160000], P(('grp', 'wide'), ('narrow', 'sub')), parts along dimension 0, may hold values from -6 to 6
- electrode_volts: float32 [512, 2], P(('grp', 'wide')), parts along dimension 0, may hold values from -3 to 3
- labels: int32 [160000], P(('narrow', 'sub')), may hold values from 0 to 1
- profile: float32 [2, 384], P(None, ('narrow', 'sub')), may hold values from 0.5 to 5
Outputs:
- neutral_charges: float32 [2, 384, 512], P(None, ('narrow', 'sub'), ('grp', 'wide')), parts along dimension 2
The draws below stay inside these ranges and needn't reach their ends.
There are 2 independent parts, one for each index of `grp`. The reference program is written for one: setup_inputs(seed, part) draws one part's arguments, and reference() takes and returns one part's arrays. A program takes and returns all parts, laid end to end along the dimension named above; an argument that names none is the same for every part. Nothing has to cross between parts.
All inputs are finite; a program needn't handle non-finite values.
Results may differ from the reference program's by a relative error of at most 0.003.
Values may be sent and summed in bfloat16 or wider, within the bound.
No kernel may reach another device: no remote copies, remote signals or barrier semaphores. Data moves between devices by JAX's collectives and lax.ppermute only.
A program may use at most 192 MiB of HBM per device.

```python
import math
import jax
import jax.numpy as jnp
from jax import lax

N = 160000
K = 2
PANELS = 2
PANEL = 384
FRM_DEV = 64
F = 256


def draw_inverse_slabs(key, part):
    key = jax.random.fold_in(key, 11)
    key_off, key_diag, key_row = jax.random.split(key, 3)
    shape = (PANELS, PANEL, N)
    spread = 0.6 / math.sqrt(N)
    offdiag = jax.random.normal(key_off, shape, jnp.float32) * spread
    diagonal = jax.random.uniform(key_diag, (PANELS, PANEL, 1), jnp.float32, 1.5, 3.0)
    scale = jnp.exp(jax.random.uniform(key_row, (PANELS, PANEL, 1), jnp.float32, 0.0, math.log(10.0)))
    site_index = (jnp.arange(PANELS, dtype=jnp.int32)[:, None] * PANEL + jnp.arange(PANEL, dtype=jnp.int32)[None, :])[:, :, None]
    on_diagonal = jnp.arange(N, dtype=jnp.int32)[None, None, :] == site_index
    return (scale * (offdiag + jnp.where(on_diagonal, diagonal, 0.0))).astype(jnp.bfloat16)


def set_ends(drawn, stream_key, least, largest):
    index_at = [jax.random.randint(jax.random.fold_in(stream_key, axis), (), 0, length) for axis, length in enumerate(drawn.shape)]
    longest = drawn.shape.index(max(drawn.shape))
    beside = index_at[:longest] + [(index_at[longest] + 1) % drawn.shape[longest]] + index_at[longest + 1:]
    return drawn.at[tuple(index_at)].set(least).at[tuple(beside)].set(largest)


def shard_levels(own_key, extent, shards, low, high):
    def one(axis_at, blocks):
        steps = jax.random.uniform(jax.random.fold_in(jax.random.fold_in(own_key, 6), axis_at), (blocks,), jnp.float32, low / len(shards), high / len(shards))
        return jnp.repeat(jnp.exp(steps), extent[axis_at] // blocks).reshape((-1,) + (1,) * (len(extent) - axis_at - 1))

    loudness = one(*shards[0])
    for cut in shards[1:]:
        loudness = loudness * one(*cut)
    return loudness


def noise(own_key, dims, scale, bound, shards=(), kind=jnp.bfloat16):
    array = jax.random.normal(own_key, dims, jnp.float32) * scale
    if len(shards) > 0:
        array = shard_levels(own_key, dims, shards, -0.22, 0.18) * array
    return jnp.clip(array, min=-bound, max=bound).astype(kind)


def setup_inputs(seed: int = 0, part: int = 0) -> dict:
    key_list = jax.random.split(jax.random.key(seed), 6)
    own_keys = jax.random.split(jax.random.fold_in(key_list[5], part), 6)
    return {
        "inverse_slabs": draw_inverse_slabs(jax.random.fold_in(key_list[5], 71), part),
        "potential_noise": noise(own_keys[1], (F, N), 1.0, 6.0, ((0, 4), (1, 4))),
        "electrode_volts": jnp.clip(jax.random.uniform(own_keys[2], (F, K), jnp.float32, -3.0, 3.0) * shard_levels(own_keys[2], (F, K), ((0, 4),), -0.4, 0.0), -3.0, 3.0),
        "labels": set_ends(jax.random.randint(key_list[3], (N,), 0, K), jax.random.fold_in(key_list[3], 1), 0, K - 1).astype(jnp.int32),
        "profile": jnp.clip(jnp.exp(math.log(5.0) - 2.3025851 * jax.random.uniform(key_list[4], (PANELS, PANEL), jnp.float32) ** shard_levels(key_list[4], (PANELS, PANEL), ((1, 4),), -0.2, 0.2)), 0.5, 5.0),
    }


def reference(inverse_slabs, potential_noise, electrode_volts, labels, profile):
    kind_ids = jnp.arange(K, dtype=jnp.int32)
    onehot = (labels[None, :] == kind_ids[:, None]).astype(jnp.float32)
    inverse_rows = inverse_slabs.reshape(PANELS * PANEL, N)

    def frame_products(frame_block):
        first_row = (frame_block * FRM_DEV).astype(jnp.int32)
        noise_block = lax.dynamic_slice_in_dim(potential_noise, first_row, FRM_DEV, 0)
        volt_block = lax.dynamic_slice_in_dim(electrode_volts, first_row, FRM_DEV, 0)
        potential = (jnp.dot(volt_block, onehot, precision=lax.Precision.HIGHEST)
                     + noise_block.astype(jnp.float32)).astype(jnp.bfloat16)
        return lax.dot_general(inverse_rows, potential, (((1,), (1,)), ((), ())),
                               preferred_element_type=jnp.float32)

    products = lax.map(frame_products, jnp.arange(F // FRM_DEV, dtype=jnp.int32))
    charges = jnp.transpose(products, (1, 0, 2)).reshape(PANELS, PANEL, F)
    charge_total = jnp.sum(charges, axis=(0, 1))
    weight_sum = jnp.sum(profile)
    return charges - profile[:, :, None] * (charge_total / weight_sum)[None, None, :]
```

```python
import jax
import jax.numpy as jnp
from jax import lax
from jax.sharding import PartitionSpec as P

SITES = ("narrow", "sub")
ALL = ("wide", "narrow", "sub")


def dot_t(a, b):
    return lax.dot_general(a, b, (((1,), (1,)), ((), ())), preferred_element_type=jnp.float32)


def potential_of(noise, volts, labels):
    value = volts[:, 0:1]
    for kind in range(1, volts.shape[1]):
        value = jnp.where(labels[None, :] == kind, volts[:, kind:kind + 1], value)
    return (value + noise.astype(jnp.float32)).astype(jnp.bfloat16)


def finish(charges, total, weight_sum, profile):
    return charges - profile[:, :, None] * (total / weight_sum)[None, None, :]


def gather_plan(slab, noise, volts, labels, profile, sizes):
    wide, owners = sizes
    panels, rows, _ = slab.shape
    frames = noise.shape[0]
    pot = lax.all_gather(potential_of(noise, volts, labels), "wide", axis=0, tiled=True)
    part = dot_t(slab.reshape(panels * rows, -1), pot).reshape(panels, rows, wide, frames)
    mine = lax.all_to_all(part, "wide", 2, 1, tiled=True).reshape(panels, wide * rows, frames)
    charges = lax.psum_scatter(mine, SITES, scatter_dimension=1, tiled=True)
    total, weight_sum = lax.psum((jnp.sum(charges, axis=(0, 1)), jnp.sum(profile)), SITES)
    return finish(charges, total, weight_sum, profile)


def line_plan(slab, noise, volts, labels, profile, sizes):
    wide, owners = sizes
    panels, rows, sites = slab.shape
    frames = noise.shape[0]
    nrows = panels * rows
    part_rows = nrows // 3
    third = sites // 3 // 128 * 128
    last = sites - 2 * third
    cuts = (0, third, 2 * third, sites)
    z = lax.axis_index("wide")
    slab = slab.reshape(nrows, sites)
    own = [potential_of(noise[:, cuts[s]:cuts[s + 1]], volts, labels[cuts[s]:cuts[s + 1]]) for s in range(3)]
    spare = [slab[part_rows * i:part_rows * (i + 1), cuts[2]:] for i in range(3)]

    def widen(x):
        return jnp.pad(x, ((0, 0), (0, last - x.shape[1])))

    def send(x, step):
        pairs = [(i, i + step) for i in range(wide) if 0 <= i + step < wide]
        return lax.ppermute(x, "wide", pairs)

    def rounds(step):
        place = z if step > 0 else wide - 1 - z
        first, second = place == 0, place == 1
        r1 = send(own[0], step)
        r2 = send(own[1], step)
        r3 = send(jnp.where(first, spare[0], widen(r1)), step)
        r4 = send(jnp.where(first, own[2], widen(r2)), step)
        r5 = send(jnp.where(first, spare[1], jnp.where(second, own[2], r3)), step)
        r6 = send(jnp.where(first, spare[2], r4), step)
        return r1, r2, r3, r4, r5, r6

    right, left = rounds(1), rounds(-1)

    def pieces(place, got):
        r1, r2, r3, r4, r5, r6 = got
        if place == 0:
            return [], []
        if place == 1:
            return [(1, 1, 0, r1), (2, 1, 1, r2), (4, 1, 2, r4)], [r3, r5, r6]
        if place == 2:
            return [(1, 1, 0, r1), (2, 1, 1, r2), (5, 1, 2, r5), (3, 2, 0, r3), (4, 2, 1, r4), (6, 2, 2, r6)], []
        return [(1, 1, 0, r1), (2, 1, 1, r2), (3, 2, 0, r3), (4, 2, 1, r4), (5, 3, 0, r5), (6, 3, 1, r6)], []

    def products(zz, low, high, right, left):
        parts = [jnp.zeros((nrows, frames), jnp.float32) for _ in range(wide)]
        at_right, rows_right = pieces(zz, right)
        at_left, rows_left = pieces(wide - 1 - zz, left)
        came = [(r, zz - d, s, x) for r, d, s, x in at_right] + [(r, zz + d, s, x) for r, d, s, x in at_left]
        if low <= 0:
            for s in range(3):
                parts[zz] += dot_t(slab[:, cuts[s]:cuts[s + 1]], own[s])
        for r, b, s, x in came:
            if low <= r <= high:
                parts[b] += dot_t(slab[:, cuts[s]:cuts[s + 1]], x[:, :cuts[s + 1] - cuts[s]])
        mine = jnp.concatenate(parts, axis=1)
        extra_rows = rows_right + rows_left
        if high < 6:
            return mine
        extra = jnp.zeros((nrows, wide * frames), jnp.float32)
        if extra_rows:
            lasts = {b: x for r, b, s, x in came if s == 2}
            lasts = jnp.concatenate([lasts[b] if b in lasts else (own[2] if b == zz else None)
                                     for b in range(wide) if b in lasts or b == zz], axis=0)
            extra_rows = jnp.concatenate(extra_rows, axis=0)
            missing = (rows_right and [0] or [wide - 1])[0]
            extra = dot_t(extra_rows, lasts)
            del missing
        return mine, extra

    early = lax.switch(z, [lambda r, l, zz=zz: products(zz, 0, 4, r, l) for zz in range(wide)], right[:4] + (None, None), left[:4] + (None, None))
    late, extra = lax.switch(z, [lambda r, l, zz=zz: products(zz, 5, 6, r, l) for zz in range(wide)], right, left)
    is_mid = (z == 1) | (z == wide - 2)
    end = jnp.where(z == 1, 0, wide - 1)
    block_of = jnp.arange(wide * frames) // frames
    extra = jnp.where((block_of == end)[None, :], 0.0, extra)
    mine = early + late
    mine_b = mine.reshape(nrows, wide, frames).transpose(1, 0, 2)
    extra_b = extra.reshape(nrows, wide, frames).transpose(1, 0, 2)
    total = lax.psum(jnp.sum(mine, axis=0) + jnp.sum(extra, axis=0), ALL)
    weight_sum = lax.psum(jnp.sum(profile), SITES)
    site = lax.axis_index(SITES)
    charges = 0.0
    for turn in range(wide):
        pairs = [(zz * owners + k, ((k + turn) % wide) * owners + zz) for zz in range(wide) for k in range(owners)]
        block = lax.dynamic_index_in_dim(mine_b, (site + turn) % wide, 0, False)
        charges += lax.ppermute(block, ALL, pairs)
        pairs = [(zz * owners + k, ((k + turn) % wide) * owners + e)
                 for zz, e in ((1, 0), (wide - 2, wide - 1)) for k in range(owners)]
        block = lax.dynamic_index_in_dim(extra_b, (site + turn) % wide, 0, False)
        charges += lax.ppermute(block, ALL, pairs)
    my_total = lax.dynamic_slice_in_dim(total, z * frames, frames, 0)
    return finish(charges.reshape(panels, rows, frames), my_total, weight_sum, profile)


def solution(mesh):
    wide = mesh.shape["wide"]
    owners = mesh.shape["narrow"] * mesh.shape["sub"]
    plan = line_plan if wide == owners == 4 else gather_plan

    def local(slab, noise, volts, labels, profile):
        return plan(slab, noise, volts, labels, profile, (wide, owners))

    return jax.shard_map(
        local,
        mesh=mesh,
        in_specs=(
            P(None, "wide", ("narrow", "sub")),
            P(("grp", "wide"), ("narrow", "sub")),
            P(("grp", "wide"), None),
            P(("narrow", "sub")),
            P(None, ("narrow", "sub")),
        ),
        out_specs=P(None, ("narrow", "sub"), ("grp", "wide")),
        check_vma=False,
    )
```

```python
import jax
import jax.numpy as jnp
from jax import lax
from jax.sharding import PartitionSpec as P

SITES = ("narrow", "sub")
ALL = ("wide", "narrow", "sub")


def dot_t(a, b):
    return lax.dot_general(a, b, (((1,), (1,)), ((), ())), preferred_element_type=jnp.float32)


def potential_of(noise, volts, labels):
    value = volts[:, 0:1]
    for kind in range(1, volts.shape[1]):
        value = jnp.where(labels[None, :] == kind, volts[:, kind:kind + 1], value)
    return (value + noise.astype(jnp.float32)).astype(jnp.bfloat16)


def finish(charges, total, weight_sum, profile):
    return charges - profile[:, :, None] * (total / weight_sum)[None, None, :]


def gather_plan(slab, noise, volts, labels, profile, sizes):
    wide, owners = sizes
    panels, rows, _ = slab.shape
    frames = noise.shape[0]
    pot = lax.all_gather(potential_of(noise, volts, labels), "wide", axis=0, tiled=True)
    part = dot_t(slab.reshape(panels * rows, -1), pot).reshape(panels, rows, wide, frames)
    mine = lax.all_to_all(part, "wide", 2, 1, tiled=True).reshape(panels, wide * rows, frames)
    charges = lax.psum_scatter(mine, SITES, scatter_dimension=1, tiled=True)
    total, weight_sum = lax.psum((jnp.sum(charges, axis=(0, 1)), jnp.sum(profile)), SITES)
    return finish(charges, total, weight_sum, profile)


def line_plan(slab, noise, volts, labels, profile, sizes):
    wide, owners = sizes
    panels, rows, sites = slab.shape
    frames = noise.shape[0]
    nrows = panels * rows
    part_rows = nrows // 3
    third = sites // 3 // 128 * 128
    cuts = (0, third, 2 * third, sites)
    z = lax.axis_index("wide")
    k = lax.axis_index(SITES)
    slab = slab.reshape(nrows, sites)
    cut = [slab[:, cuts[s]:cuts[s + 1]] for s in range(3)]

    def after(x, *others):
        return lax.optimization_barrier((x,) + others)[0]

    def potential_at(s, source):
        return potential_of(source[:, cuts[s]:cuts[s + 1]], volts, labels[cuts[s]:cuts[s + 1]])

    def send(x, pairs):
        return lax.ppermute(x, "wide", pairs)

    own0 = potential_at(0, noise)
    own1 = potential_at(1, after(noise, own0))
    own2 = potential_at(2, after(noise, own1))
    spare = [slab[part_rows * i:part_rows * (i + 1), cuts[2]:] for i in range(3)]
    ends_in = [(0, 1), (3, 2)]
    across = [(1, 2), (2, 1)]
    right = [(0, 1), (1, 2), (2, 3)]
    left = [(3, 2), (2, 1), (1, 0)]
    f1a_r, f1a_l = send(own0, right), send(own0, left)
    f1b_r, f1b_l = send(own1, right), send(own1, left)
    f2a_r, f2a_l = send(f1a_r, right[1:]), send(f1a_l, left[1:])
    g0 = send(after(own2, f1a_r, f1a_l), ends_in)
    f2b_r, f2b_l = send(f1b_r, right[1:]), send(f1b_l, left[1:])
    h1 = send(after(spare[0], f1b_r, f1b_l), ends_in)
    f3a_r, f3a_l = send(f2a_r, right[2:]), send(f2a_l, left[2:])
    g1 = send(after(own2, f2a_r, f2a_l), across)
    h2 = send(after(spare[1], f2a_r, f2a_l), ends_in)
    f3b_r, f3b_l = send(f2b_r, right[2:]), send(f2b_l, left[2:])
    g2 = send(after(g0, f2b_r, f2b_l), across)
    h3 = send(after(spare[2], f2b_r, f2b_l), ends_in)
    weight_sum = lax.psum(jnp.sum(after(profile, f1a_r, f1a_l)), SITES)

    own_part = dot_t(cut[0], own0) + dot_t(cut[1], own1) + dot_t(cut[2], own2)
    terms = [
        (z, own_part),
        (z - 1, dot_t(cut[0], f1a_r) + dot_t(cut[1], f1b_r)),
        (z + 1, dot_t(cut[0], f1a_l) + dot_t(cut[1], f1b_l)),
        (z - 2, dot_t(cut[0], f2a_r) + dot_t(cut[1], f2b_r)),
        (z + 2, dot_t(cut[0], f2a_l) + dot_t(cut[1], f2b_l)),
        (jnp.where(z == 0, 3, 0), dot_t(cut[0], f3a_r + f3a_l) + dot_t(cut[1], f3b_r + f3b_l)),
        (jnp.where(z == 1, 0, 3), dot_t(cut[2], g0)),
        (3 - z, dot_t(cut[2], g1)),
        (jnp.where(z == 1, 3, 0), dot_t(cut[2], g2)),
    ]
    brought = jnp.concatenate([h1, h2, h3], axis=0)
    extra_terms = [
        (z, dot_t(brought, own2)),
        (3 - z, dot_t(brought, g1)),
        (jnp.where(z == 1, 3, 0), dot_t(brought, g2)),
    ]

    def block_of(b):
        mine = sum(jnp.where(b == at, x, 0.0) for at, x in terms)
        extra = sum(jnp.where(b == at, x, 0.0) for at, x in extra_terms)
        return jnp.concatenate([mine, extra], axis=0)

    summed = block_of(k)
    for turn in range(1, owners):
        summed += lax.ppermute(block_of(k ^ turn), SITES, [(i, i ^ turn) for i in range(owners)])
    frame_sum = jnp.sum(summed, axis=0)
    flip = [(a * owners + b, b * owners + a) for a in range(wide) for b in range(owners)]
    flip_end = [(a * owners + b, b * owners + e) for a, e in ((1, 0), (2, 3)) for b in range(owners)]
    charges = lax.ppermute(summed[:nrows], ALL, flip) + lax.ppermute(summed[nrows:], ALL, flip_end)
    total = 0.0
    for turn in range(owners):
        pairs = [(a * owners + b, b * owners + (a ^ turn)) for a in range(wide) for b in range(owners)]
        total += lax.ppermute(frame_sum, ALL, pairs)
    return finish(charges.reshape(panels, rows, frames), total, weight_sum, profile)


def solution(mesh):
    wide = mesh.shape["wide"]
    owners = mesh.shape["narrow"] * mesh.shape["sub"]
    plan = line_plan if wide == owners == 4 else gather_plan

    def local(slab, noise, volts, labels, profile):
        return plan(slab, noise, volts, labels, profile, (wide, owners))

    return jax.shard_map(
        local,
        mesh=mesh,
        in_specs=(
            P(None, "wide", ("narrow", "sub")),
            P(("grp", "wide"), ("narrow", "sub")),
            P(("grp", "wide"), None),
            P(("narrow", "sub")),
            P(None, ("narrow", "sub")),
        ),
        out_specs=P(None, ("narrow", "sub"), ("grp", "wide")),
        check_vma=False,
    )
```

```python
import jax
import jax.numpy as jnp
from jax import lax
from jax.sharding import PartitionSpec as P

SITES = ("narrow", "sub")
ALL = ("wide", "narrow", "sub")


def dot_t(a, b):
    return lax.dot_general(a, b, (((1,), (1,)), ((), ())), preferred_element_type=jnp.float32)


def potential_of(noise, volts, labels):
    value = volts[:, 0:1]
    for kind in range(1, volts.shape[1]):
        value = jnp.where(labels[None, :] == kind, volts[:, kind:kind + 1], value)
    return (value + noise.astype(jnp.float32)).astype(jnp.bfloat16)


def finish(charges, total, weight_sum, profile):
    return charges - profile[:, :, None] * (total / weight_sum)[None, None, :]


def gather_plan(slab, noise, volts, labels, profile, sizes):
    wide, owners = sizes
    panels, rows, _ = slab.shape
    frames = noise.shape[0]
    pot = lax.all_gather(potential_of(noise, volts, labels), "wide", axis=0, tiled=True)
    part = dot_t(slab.reshape(panels * rows, -1), pot).reshape(panels, rows, wide, frames)
    mine = lax.all_to_all(part, "wide", 2, 1, tiled=True).reshape(panels, wide * rows, frames)
    charges = lax.psum_scatter(mine, SITES, scatter_dimension=1, tiled=True)
    total, weight_sum = lax.psum((jnp.sum(charges, axis=(0, 1)), jnp.sum(profile)), SITES)
    return finish(charges, total, weight_sum, profile)


def line_plan(slab, noise, volts, labels, profile, sizes):
    wide, owners = sizes
    panels, rows, sites = slab.shape
    frames = noise.shape[0]
    nrows = panels * rows
    part_rows = nrows // 3
    third = sites // 3 // 128 * 128
    cuts = (0, third, 2 * third, sites)
    z = lax.axis_index("wide")
    k = lax.axis_index(SITES)
    slab = slab.reshape(nrows, sites)
    cut = [slab[:, cuts[s]:cuts[s + 1]] for s in range(3)]

    def after(x, *others):
        return lax.optimization_barrier((x,) + others)[0]

    def send(x, pairs):
        return lax.ppermute(x, "wide", pairs)

    own01 = potential_of(noise[:, :cuts[2]], volts, labels[:cuts[2]])
    own2 = potential_of(after(noise, own01)[:, cuts[2]:], volts, labels[cuts[2]:])
    is_end = (z == 0) | (z == wide - 1)
    spare1, spare23 = (jnp.where(is_end, x[:, cuts[2]:], 0) for x in (slab[:part_rows], slab[part_rows:]))
    ends_in = [(0, 1), (3, 2)]
    across = [(1, 2), (2, 1)]
    right = [(0, 1), (1, 2), (2, 3)]
    left = [(3, 2), (2, 1), (1, 0)]
    f1_r, f1_l = send(own01, right), send(own01, left)
    f1_r, f1_l, own2, spare1 = lax.optimization_barrier((f1_r, f1_l, own2, spare1))
    f2_r, f2_l = send(f1_r, right[1:]), send(f1_l, left[1:])
    g0, h1 = send(own2, ends_in), send(spare1, ends_in)
    f2_r, f2_l, g0, h1, own2, spare23 = lax.optimization_barrier((f2_r, f2_l, g0, h1, own2, spare23))
    f3_r, f3_l = send(f2_r, right[2:]), send(f2_l, left[2:])
    g1, g2 = send(own2, across), send(g0, across)
    h23 = send(spare23, ends_in)
    f3_r, f3_l, g1, g2, h23 = lax.optimization_barrier((f3_r, f3_l, g1, g2, h23))

    both = slab[:, :cuts[2]]
    own_part = dot_t(both, own01) + dot_t(cut[2], own2)
    weight_sum = lax.psum(jnp.sum(profile), SITES)
    terms = [
        (z, own_part),
        (z - 1, dot_t(both, f1_r)),
        (z + 1, dot_t(both, f1_l)),
        (z - 2, dot_t(both, f2_r)),
        (z + 2, dot_t(both, f2_l)),
        (jnp.where(z == 0, 3, 0), dot_t(both, f3_r + f3_l)),
        (jnp.where(z == 1, 0, 3), dot_t(cut[2], g0)),
        (3 - z, dot_t(cut[2], g1)),
        (jnp.where(z == 1, 3, 0), dot_t(cut[2], g2)),
    ]
    brought = jnp.concatenate([h1, h23], axis=0)
    extra_terms = [
        (z, dot_t(brought, own2)),
        (3 - z, dot_t(brought, g1)),
        (jnp.where(z == 1, 3, 0), dot_t(brought, g2)),
    ]

    def block_of(b):
        mine = sum(jnp.where(b == at, x, 0.0) for at, x in terms)
        extra = sum(jnp.where(b == at, x, 0.0) for at, x in extra_terms)
        return jnp.concatenate([mine, extra], axis=0)

    summed = block_of(k)
    for turn in range(1, owners):
        summed += lax.ppermute(block_of(k ^ turn), SITES, [(i, i ^ turn) for i in range(owners)])
    frame_sum = jnp.sum(summed, axis=0)
    flip = [(a * owners + b, b * owners + a) for a in range(wide) for b in range(owners)]
    flip_end = [(a * owners + b, b * owners + e) for a, e in ((1, 0), (2, 3)) for b in range(owners)]
    charges = lax.ppermute(summed[:nrows], ALL, flip) + lax.ppermute(summed[nrows:], ALL, flip_end)
    total = 0.0
    for turn in range(owners):
        pairs = [(a * owners + b, b * owners + (a ^ turn)) for a in range(wide) for b in range(owners)]
        total += lax.ppermute(frame_sum, ALL, pairs)
    return finish(charges.reshape(panels, rows, frames), total, weight_sum, profile)


def solution(mesh):
    wide = mesh.shape["wide"]
    owners = mesh.shape["narrow"] * mesh.shape["sub"]
    plan = line_plan if wide == owners == 4 else gather_plan

    def local(slab, noise, volts, labels, profile):
        return plan(slab, noise, volts, labels, profile, (wide, owners))

    return jax.shard_map(
        local,
        mesh=mesh,
        in_specs=(
            P(None, "wide", ("narrow", "sub")),
            P(("grp", "wide"), ("narrow", "sub")),
            P(("grp", "wide"), None),
            P(("narrow", "sub")),
            P(None, ("narrow", "sub")),
        ),
        out_specs=P(None, ("narrow", "sub"), ("grp", "wide")),
        check_vma=False,
    )
```

```python
import jax
import jax.numpy as jnp
from jax import lax
from jax.experimental import pallas as pl
from jax.experimental.pallas import tpu as pltpu
from jax.sharding import PartitionSpec as P

SITES = ("narrow", "sub")
ALL = ("wide", "narrow", "sub")


def dot_t(a, b):
    return lax.dot_general(a, b, (((1,), (1,)), ((), ())), preferred_element_type=jnp.float32)


def potential_of(noise, volts, labels):
    value = volts[:, 0:1]
    for kind in range(1, volts.shape[1]):
        value = jnp.where(labels[None, :] == kind, volts[:, kind:kind + 1], value)
    return (value + noise.astype(jnp.float32)).astype(jnp.bfloat16)


def finish(charges, total, weight_sum, profile):
    return charges - profile[:, :, None] * (total / weight_sum)[None, None, :]


def gather_plan(slab, noise, volts, labels, profile, sizes):
    wide, owners = sizes
    panels, rows, _ = slab.shape
    frames = noise.shape[0]
    pot = lax.all_gather(potential_of(noise, volts, labels), "wide", axis=0, tiled=True)
    part = dot_t(slab.reshape(panels * rows, -1), pot).reshape(panels, rows, wide, frames)
    mine = lax.all_to_all(part, "wide", 2, 1, tiled=True).reshape(panels, wide * rows, frames)
    charges = lax.psum_scatter(mine, SITES, scatter_dimension=1, tiled=True)
    total, weight_sum = lax.psum((jnp.sum(charges, axis=(0, 1)), jnp.sum(profile)), SITES)
    return finish(charges, total, weight_sum, profile)


LANES = 128
STEPS = 4
WIDTH = 4 * LANES


def is_end(z):
    return (z == 0) | (z == 3)


def is_mid(z):
    return (z == 1) | (z == 2)


def far_block(z):
    return jnp.where(z < 2, 3, 0)


def across_block(z):
    return 3 - z


def absorb(place, slab, third_of, units, brought, sums, last=None):
    nrows, sites = slab.shape
    tile = sites // 3 // LANES * LANES // STEPS
    frames = units[0][0].shape[0]
    arrays = [x for x, _, _ in units]
    valid = [v for _, v, _ in units]
    row_sets, extra = [], []
    for number, rows, lane, block in brought:
        at = []
        for x in rows:
            known = [n for n, y in enumerate(row_sets) if y is x]
            at.append(known[0] if known else len(row_sets))
            if not known:
                row_sets.append(x)
        extra.append((number, at, lane, block))
    count, nsets = len(units), len(row_sets)
    blocks = 4
    whole = tile * STEPS
    rest = sites - 3 * whole
    rest_width = rest + -rest % LANES
    long = [n for n in range(count) if arrays[n].shape[1] > whole]

    def dot(a, b):
        return lax.dot_general(a, b, (((1,), (1,)), ((), ())), preferred_element_type=jnp.float32)

    def kernel(place_ref, slab_ref, *refs):
        xs, rows = refs[:count], refs[count:count + nsets]
        refs = refs[count + nsets:]
        if sums is not None:
            sums_ref, refs = refs[0], refs[1:]
        if long:
            slab_rest, rests, refs = refs[0], refs[1:1 + len(long)], refs[1 + len(long):]
        if last is None:
            acc, = refs
        else:
            profile_ref, outs, acc = refs[0], refs[1:-1], refs[-1]
        z, k = place_ref[0], place_ref[1]
        step = pl.program_id(0)

        @pl.when(step == 0)
        def _():
            acc[...] = jnp.zeros(acc.shape, acc.dtype) if sums is None else sums_ref[...]
            if long:
                column = lax.broadcasted_iota(jnp.int32, (nrows, rest_width), 1)
                piece = jnp.where(column < rest, slab_rest[...].astype(jnp.float32), 0.0).astype(jnp.bfloat16)
            for n, x in zip(long, rests if long else ()):
                @pl.when(valid[n](z))
                def _(n=n, x=x):
                    acc[units[n][2](z), :, 0:nrows] += dot(x[...], piece)

        for n in range(count):
            if units[n][2] is None:
                continue

            @pl.when(valid[n](z))
            def _(n=n):
                acc[units[n][2](z), :, 0:nrows] += dot(xs[n][...], slab_ref[...])

        if extra:
            @pl.when(is_mid(z))
            def _():
                for number, at, lane, block in extra:
                    piece = [rows[i][...] for i in at]
                    piece = piece[0] if len(piece) == 1 else jnp.concatenate(piece, axis=0)
                    acc[block(z), :, lane:lane + piece.shape[0]] += dot(xs[number][...], piece)

        if last is not None:
            @pl.when(step == STEPS - 1)
            def _():
                weight = jnp.sum(profile_ref[...])
                lane = lax.broadcasted_iota(jnp.int32, (frames, LANES), 1)
                for turn, out in enumerate(outs):
                    at = k ^ turn
                    out[:, :WIDTH - LANES] = acc[at, :, :WIDTH - LANES]
                    end = acc[at, :, WIDTH - LANES:]
                    out[:, WIDTH - LANES:] = jnp.where(lane >= nrows - LANES, weight, end)

    def unit_spec(ok):
        return pl.BlockSpec((frames, tile), lambda i, s: (0, jnp.where(ok(s[0]), i, 0)))

    in_specs = [pl.BlockSpec((nrows, tile), lambda i, s: (0, third_of(s[0]) * STEPS + i))]
    in_specs += [unit_spec(v) for v in valid]
    in_specs += [pl.BlockSpec((x.shape[0], tile), lambda i, s: (0, jnp.where(is_mid(s[0]), i, 0))) for x in row_sets]
    operands = [slab] + arrays + row_sets
    sums_shape = (blocks, frames, WIDTH)
    if sums is not None:
        in_specs.append(pl.BlockSpec(sums_shape, lambda i, s: (0, 0, 0)))
        operands.append(sums)
    if long:
        in_specs.append(pl.BlockSpec((nrows, rest_width), lambda i, s: (0, 3 * whole // rest_width)))
        in_specs += [pl.BlockSpec((frames, rest_width), lambda i, s: (0, whole // rest_width))] * len(long)
        operands += [slab] + [arrays[n] for n in long]
    if last is None:
        out_shape = jax.ShapeDtypeStruct(sums_shape, jnp.float32)
        out_specs = pl.BlockSpec(sums_shape, lambda i, s: (0, 0, 0))
        scratch = []
    else:
        in_specs.append(pl.BlockSpec(last.shape, lambda i, s: (0, 0)))
        operands.append(last)
        out_shape = [jax.ShapeDtypeStruct(sums_shape[1:], jnp.float32)] * blocks
        out_specs = [pl.BlockSpec(sums_shape[1:], lambda i, s: (0, 0))] * blocks
        scratch = [pltpu.VMEM(sums_shape, jnp.float32)]
    return pl.pallas_call(
        kernel,
        grid_spec=pltpu.PrefetchScalarGridSpec(
            num_scalar_prefetch=1, grid=(STEPS,), in_specs=in_specs, out_specs=out_specs, scratch_shapes=scratch),
        out_shape=out_shape,
        compiler_params=pltpu.CompilerParams(vmem_limit_bytes=32 * 1024 * 1024),
        cost_estimate=pl.CostEstimate(flops=1000, bytes_accessed=1000, transcendentals=0),
    )(place, *operands)


def line_plan(slab, noise, volts, labels, profile, sizes):
    wide, owners = sizes
    panels, rows, sites = slab.shape
    frames = noise.shape[0]
    nrows = panels * rows
    part_rows = nrows // 3
    third = sites // 3 // LANES * LANES
    z = lax.axis_index("wide")
    k = lax.axis_index(SITES)
    place = jnp.stack([z, k]).astype(jnp.int32)
    slab = slab.reshape(nrows, sites)

    def after(x, *others):
        return lax.optimization_barrier((x,) + others)[0]

    def potential_at(first, end, small):
        return potential_of(noise[:, first:end], small, labels[first:end])

    def send(x, pairs):
        return lax.ppermute(x, "wide", pairs)

    def spare(i, *others):
        return after(slab[part_rows * i:part_rows * (i + 1), 2 * third:3 * third], *others)

    ends_in = [(0, 1), (3, 2)]
    across = [(1, 2), (2, 1)]
    right = [(0, 1), (1, 2), (2, 3)]
    left = [(3, 2), (2, 1), (1, 0)]
    rest = sites - 3 * third
    own0 = jnp.concatenate([
        potential_at(0, third, volts), potential_at(3 * third, sites, volts),
        jnp.zeros((frames, -rest % LANES), jnp.bfloat16)], axis=1)
    own1 = potential_at(third, 2 * third, after(volts, own0))
    f1a_r, f1a_l = send(own0, right), send(own0, left)
    f1b_r, f1b_l = send(own1, right), send(own1, left)
    own2 = potential_at(2 * third, 3 * third, after(volts, own1))
    f2a_r, f2a_l = send(f1a_r, right[1:]), send(f1a_l, left[1:])
    g0 = send(after(own2, f1a_r, f1a_l), ends_in)
    f2b_r, f2b_l = send(f1b_r, right[1:]), send(f1b_l, left[1:])
    h1 = send(spare(0, f1b_r, f1b_l), ends_in)
    f3a_r, f3a_l = send(f2a_r, right[2:]), send(f2a_l, left[2:])
    g1 = send(after(own2, f2a_r, f2a_l), across)
    h2 = send(spare(1, f2a_r, f2a_l), ends_in)
    f3b_r, f3b_l = send(f2b_r, right[2:]), send(f2b_l, left[2:])
    g2 = send(after(g0, f2b_r, f2b_l), across)
    h3 = send(spare(2, f2b_r, f2b_l), ends_in)

    def always(z):
        return z >= 0

    def here(z):
        return z

    def pick(end_third, mid_third):
        return lambda z: jnp.where(is_mid(z), mid_third, end_third)

    def chain(x_r, x_l, hop):
        return [(x_r, lambda z: z >= hop, lambda z: z - hop), (x_l, lambda z: z < 4 - hop, lambda z: z + hop)]

    sums = absorb(place, slab, pick(0, 0), [(own0, always, here)] + chain(f1a_r, f1a_l, 1), [], None)
    sums = absorb(place, slab, pick(1, 1), [(own1, always, here)] + chain(f1b_r, f1b_l, 1), [], sums)
    sums = absorb(place, slab, pick(2, 2), [(own2, always, here), (g0, is_mid, lambda z: jnp.where(z == 1, 0, 3))], [], sums)
    sums = absorb(place, slab, pick(0, 0), chain(f2a_r, f2a_l, 2), [], sums)
    sums = absorb(place, slab, pick(1, 1), chain(f2b_r, f2b_l, 2), [], sums)
    sums = absorb(
        place, slab, pick(0, 2),
        chain(f3a_r, f3a_l, 3) + [(g1, is_mid, across_block), (own2, is_mid, None)],
        [(2, (h1, h2), 2 * LANES, across_block), (3, (h1, h2), 2 * LANES, here)], sums)
    messages = absorb(
        place, slab, pick(1, 2),
        chain(f3b_r, f3b_l, 3) + [(g2, is_mid, far_block), (g1, is_mid, None), (own2, is_mid, None)],
        [(2, (h1, h2, h3), 2 * LANES, far_block), (3, (h3,), 3 * LANES, across_block), (4, (h3,), 3 * LANES, here)], sums, profile)

    summed = messages[0]
    for turn in range(1, owners):
        summed += lax.ppermute(messages[turn], SITES, [(i, i ^ turn) for i in range(owners)])
    weight_sum = summed[0, WIDTH - 1]
    mine, extra = summed[:, :nrows], summed[:, 2 * LANES:2 * LANES + nrows]
    frame_sum = jnp.sum(mine, axis=1) + jnp.sum(extra, axis=1)
    flip = [(a * owners + b, b * owners + a) for a in range(wide) for b in range(owners)]
    flip_end = [(a * owners + b, b * owners + e) for a, e in ((1, 0), (2, 3)) for b in range(owners)]
    charges = lax.ppermute(mine, ALL, flip) + lax.ppermute(extra, ALL, flip_end)
    total = 0.0
    for turn in range(owners):
        pairs = [(a * owners + b, b * owners + (a ^ turn)) for a in range(wide) for b in range(owners)]
        total += lax.ppermute(frame_sum, ALL, pairs)
    charges = charges.reshape(frames, panels, rows).transpose(1, 2, 0)
    return finish(charges, total, weight_sum, profile)


def solution(mesh):
    wide = mesh.shape["wide"]
    owners = mesh.shape["narrow"] * mesh.shape["sub"]
    plan = line_plan if wide == owners == 4 else gather_plan

    def local(slab, noise, volts, labels, profile):
        return plan(slab, noise, volts, labels, profile, (wide, owners))

    return jax.shard_map(
        local,
        mesh=mesh,
        in_specs=(
            P(None, "wide", ("narrow", "sub")),
            P(("grp", "wide"), ("narrow", "sub")),
            P(("grp", "wide"), None),
            P(("narrow", "sub")),
            P(None, ("narrow", "sub")),
        ),
        out_specs=P(None, ("narrow", "sub"), ("grp", "wide")),
        check_vma=False,
    )
```

```python
import jax
import jax.numpy as jnp
from jax import lax
from jax.experimental import pallas as pl
from jax.experimental.pallas import tpu as pltpu
from jax.sharding import PartitionSpec as P

SITES = ("narrow", "sub")
ALL = ("wide", "narrow", "sub")


def dot_t(a, b):
    return lax.dot_general(a, b, (((1,), (1,)), ((), ())), preferred_element_type=jnp.float32)


def potential_of(noise, volts, labels):
    value = volts[:, 0:1]
    for kind in range(1, volts.shape[1]):
        value = jnp.where(labels[None, :] == kind, volts[:, kind:kind + 1], value)
    return (value + noise.astype(jnp.float32)).astype(jnp.bfloat16)


def finish(charges, total, weight_sum, profile):
    return charges - profile[:, :, None] * (total / weight_sum)[None, None, :]


def gather_plan(slab, noise, volts, labels, profile, sizes):
    wide, owners = sizes
    panels, rows, _ = slab.shape
    frames = noise.shape[0]
    pot = lax.all_gather(potential_of(noise, volts, labels), "wide", axis=0, tiled=True)
    part = dot_t(slab.reshape(panels * rows, -1), pot).reshape(panels, rows, wide, frames)
    mine = lax.all_to_all(part, "wide", 2, 1, tiled=True).reshape(panels, wide * rows, frames)
    charges = lax.psum_scatter(mine, SITES, scatter_dimension=1, tiled=True)
    total, weight_sum = lax.psum((jnp.sum(charges, axis=(0, 1)), jnp.sum(profile)), SITES)
    return finish(charges, total, weight_sum, profile)


LANES = 128
STEPS = 4
WIDTH = 4 * LANES
FREE = LANES * 2 - 1
PARAMS = pltpu.CompilerParams(vmem_limit_bytes=56 * 1024 * 1024)
SMALL = pl.CostEstimate(flops=1000, bytes_accessed=1000, transcendentals=0)


def always(z):
    return z >= 0


def is_mid(z):
    return (z == 1) | (z == 2)


def is_end(z):
    return (z == 0) | (z == 3)


def dot(a, b):
    return lax.dot_general(a, b, (((1,), (1,)), ((), ())), preferred_element_type=jnp.float32)


def first_potential(noise, volts, labels, third):
    frames, sites = noise.shape
    tile = third // STEPS
    rest = sites - 3 * third
    rest_width = rest + -rest % LANES
    labels = labels.reshape(1, sites)

    def kernel(noise_ref, labels_ref, volts_ref, noise_rest, labels_rest, out):
        def potential(noise, labels):
            value = jnp.broadcast_to(volts_ref[:, 0:1], noise.shape)
            for kind in range(1, volts_ref.shape[1]):
                value = jnp.where(labels == kind, volts_ref[:, kind:kind + 1], value)
            return value + noise.astype(jnp.float32)

        step = pl.program_id(0)
        at = pl.multiple_of(step * tile, LANES)
        out[:, pl.ds(at, tile)] = potential(noise_ref[...], labels_ref[...]).astype(jnp.bfloat16)

        @pl.when(step == 0)
        def _():
            column = lax.broadcasted_iota(jnp.int32, (frames, rest_width), 1)
            value = jnp.where(column < rest, potential(noise_rest[...], labels_rest[...]), 0.0)
            out[:, third:] = value.astype(jnp.bfloat16)

    last = 3 * third // rest_width
    return pl.pallas_call(
        kernel,
        grid=(STEPS,),
        in_specs=[
            pl.BlockSpec((frames, tile), lambda i: (0, i)),
            pl.BlockSpec((1, tile), lambda i: (0, i)),
            pl.BlockSpec(volts.shape, lambda i: (0, 0)),
            pl.BlockSpec((frames, rest_width), lambda i: (0, last)),
            pl.BlockSpec((1, rest_width), lambda i: (0, last)),
        ],
        out_specs=pl.BlockSpec((frames, third + rest_width), lambda i: (0, 0)),
        out_shape=jax.ShapeDtypeStruct((frames, third + rest_width), jnp.bfloat16),
        compiler_params=PARAMS,
        cost_estimate=SMALL,
    )(noise, labels, volts, noise, labels)


def route(place, sources, to_right, to_left, shape, tokens):
    arrays = [s[0] for s in sources]
    count = len(arrays)

    def kernel(place_ref, *refs):
        outs, sems = refs[count + len(tokens):-1], refs[-1]
        z = place_ref[0]
        for here in range(4):
            @pl.when(z == here)
            def _(here=here):
                copies = []
                for side, choice in enumerate((to_right[here], to_left[here])):
                    if choice is None:
                        continue
                    number, columns = choice
                    _, row, rows, column = sources[number]
                    copies.append(pltpu.make_async_copy(
                        refs[number].at[pl.ds(row, rows), pl.ds(column, columns)],
                        outs[side].at[pl.ds(0, rows), pl.ds(0, columns)], sems.at[side]))
                for copy in copies:
                    copy.start()
                for copy in copies:
                    copy.wait()

    anywhere = pl.BlockSpec(memory_space=pl.ANY)
    return pl.pallas_call(
        kernel,
        in_specs=[pl.BlockSpec(memory_space=pltpu.SMEM)] + [anywhere] * (count + len(tokens)),
        out_specs=[anywhere] * 2,
        out_shape=[jax.ShapeDtypeStruct(shape, jnp.bfloat16)] * 2,
        scratch_shapes=[pltpu.SemaphoreType.DMA((2,))],
        compiler_params=PARAMS,
        cost_estimate=SMALL,
    )(place, *arrays, *tokens)


def absorb(place, whole, streams, work, sums_shape, sums, first=None, profile=None):
    tile = whole // STEPS
    names = list(streams)
    slab = streams["slab"][0]
    nrows, sites = slab.shape
    rest = sites - 3 * whole
    rest_width = rest + -rest % LANES
    long = [n for n in names if streams[n][0].shape[1] == whole + rest_width] if first else []
    blocks, frames, width = sums_shape

    def kernel(place_ref, *refs):
        tiles = dict(zip(names, refs))
        refs = refs[len(names):]
        if sums is not None:
            sums_ref, refs = refs[0], refs[1:]
        if first:
            slab_rest, refs = refs[0], refs[1:]
            rests = dict(zip(long, refs))
            refs = refs[len(long):]
        if profile is None:
            acc, = refs
        else:
            profile_ref, outs, acc = refs[0], refs[1:-1], refs[-1]
        z, k = place_ref[0], place_ref[1]
        step = pl.program_id(0)

        def add(block, lane, value):
            acc[block, :, lane:lane + value.shape[1]] += value

        @pl.when(step == 0)
        def _():
            acc[...] = jnp.zeros(acc.shape, acc.dtype) if sums is None else sums_ref[...]
            if first:
                column = lax.broadcasted_iota(jnp.int32, (nrows, rest_width), 1)
                piece = jnp.where(column < rest, slab_rest[...].astype(jnp.float32), 0.0).astype(jnp.bfloat16)
                first(z, dict(rests, slab=piece), add)

        work(z, tiles, add)

        if profile is not None:
            @pl.when(step == STEPS - 1)
            def _():
                weight = jnp.sum(profile_ref[...])
                lane = lax.broadcasted_iota(jnp.int32, (frames, LANES), 1)
                for turn, out in enumerate(outs):
                    out[:, :width - LANES] = acc[k ^ turn, :, :width - LANES]
                    end = acc[k ^ turn, :, width - LANES:]
                    out[:, width - LANES:] = jnp.where(lane == LANES - 2, weight, end)

    def spec(array, needed, third):
        return pl.BlockSpec(
            (array.shape[0], tile), lambda i, s: (0, third(s[0]) * STEPS + jnp.where(needed(s[0]), i, 0)))

    in_specs = [spec(*streams[n]) for n in names]
    operands = [streams[n][0] for n in names]
    if sums is not None:
        in_specs.append(pl.BlockSpec(sums_shape, lambda i, s: (0, 0, 0)))
        operands.append(sums)
    if first:
        in_specs.append(pl.BlockSpec((nrows, rest_width), lambda i, s: (0, 3 * whole // rest_width)))
        in_specs += [pl.BlockSpec((frames, rest_width), lambda i, s: (0, whole // rest_width))] * len(long)
        operands += [slab] + [streams[n][0] for n in long]
    if profile is None:
        out_shape = jax.ShapeDtypeStruct(sums_shape, jnp.float32)
        out_specs = pl.BlockSpec(sums_shape, lambda i, s: (0, 0, 0))
        scratch = []
    else:
        in_specs.append(pl.BlockSpec(profile.shape, lambda i, s: (0, 0)))
        operands.append(profile)
        out_shape = [jax.ShapeDtypeStruct(sums_shape[1:], jnp.float32)] * blocks
        out_specs = [pl.BlockSpec(sums_shape[1:], lambda i, s: (0, 0))] * blocks
        scratch = [pltpu.VMEM(sums_shape, jnp.float32)]
    return pl.pallas_call(
        kernel,
        grid_spec=pltpu.PrefetchScalarGridSpec(
            num_scalar_prefetch=1, grid=(STEPS,), in_specs=in_specs, out_specs=out_specs, scratch_shapes=scratch),
        out_shape=out_shape,
        compiler_params=PARAMS,
        cost_estimate=SMALL,
    )(place, *operands)


def line_plan(slab, noise, volts, labels, profile, sizes):
    wide, owners = sizes
    panels, rows, sites = slab.shape
    frames = noise.shape[0]
    nrows = panels * rows
    part = nrows // 3
    third = sites // 3 // LANES * LANES
    z = lax.axis_index("wide")
    k = lax.axis_index(SITES)
    place = jnp.stack([z, k]).astype(jnp.int32)
    slab = slab.reshape(nrows, sites)
    right = [(0, 1), (1, 2), (2, 3)]
    left = [(3, 2), (2, 1), (1, 0)]

    def send(pair):
        return lax.ppermute(pair[0], "wide", right), lax.ppermute(pair[1], "wide", left)

    def potential_at(first, end, before):
        small = lax.optimization_barrier((volts, before))[0]
        return potential_of(noise[:, first:end], small, labels[first:end])

    def mirror(choice):
        swap = {0: 0, 1: 2, 2: 1, 3: 4, 4: 3}
        return [None if c is None else (swap[c[0]], c[1]) for c in reversed(choice)]

    def routed(sources, choice, width, tokens):
        sources = [s if isinstance(s, tuple) else (s, 0, frames, 0) for s in sources]
        return send(route(place, sources, choice, mirror(choice), (frames, width), tokens))

    def spare(i):
        return (slab, part * i, part, 2 * third)

    own_a = first_potential(noise, volts, labels, third)
    long = own_a.shape[1]
    r1 = send((own_a, own_a))
    own_b = potential_at(third, 2 * third, own_a)
    r2 = send((own_b, own_b))
    own_c = potential_at(2 * third, 3 * third, own_b)

    sums_shape = (wide, frames, WIDTH)

    def at(number):
        return lambda z: number

    def thirds(end, mid):
        return lambda z: jnp.where(is_mid(z), mid, end)

    def from_left(z):
        return z >= 1

    def from_right(z):
        return z <= 2

    def far(z, refs, name):
        return jnp.where(z < 2, refs[name + "l"][...], refs[name + "r"][...])

    def near(z, refs, name):
        return jnp.where(z < 2, refs[name + "r"][...], refs[name + "l"][...])

    def both(name, pair, right_needed=from_left, left_needed=from_right):
        return {name + "r": (pair[0], right_needed, at(0)), name + "l": (pair[1], left_needed, at(0))}

    def work1(z, refs, add):
        add(z, 0, dot(refs["own"][...], refs["slab"][...]))

        @pl.when(z >= 1)
        def _():
            add(z - 1, 0, dot(refs["r"][...], refs["slab"][...]))

        @pl.when(z <= 2)
        def _():
            add(z + 1, 0, dot(refs["l"][...], refs["slab"][...]))

    def work3(z, refs, add):
        add(z, 0, dot(refs["own"][...], refs["slab2"][...]))
        add((z + 2) % 4, 0, dot(far(z, refs, ""), refs["slab"][...]))

        @pl.when(is_mid(z))
        def _():
            add(jnp.where(z < 2, 0, 3), 0, dot(near(z, refs, ""), refs["slab2"][...]))

    def work4(z, refs, add):
        add((z + 2) % 4, 0, dot(far(z, refs, ""), refs["slab"][...]))

    def work5(z, refs, add):
        came = far(z, refs, "")
        add(3 - z, 0, dot(came, refs["slab"][...]))

        @pl.when(is_mid(z))
        def _():
            brought = jnp.concatenate([near(z, refs, "4"), near(z, refs, "")], axis=0)
            add(z, 2 * LANES, dot(refs["own"][...], brought))
            add(3 - z, 2 * LANES, dot(came, brought))

    def first5(z, refs, add):
        @pl.when(is_end(z))
        def _():
            add(3 - z, 0, dot(far(z, refs, ""), refs["slab"]))

    def work6(z, refs, add):
        came = far(z, refs, "")
        block = jnp.where(z < 2, 3, 0)
        add(block, 0, dot(came, refs["slab"][...]))

        @pl.when(is_mid(z))
        def _():
            newest = near(z, refs, "")
            brought = jnp.concatenate([near(z, refs, "4"), near(z, refs, "5"), newest], axis=0)
            add(block, 2 * LANES, dot(came, brought))
            add(z, 3 * LANES, dot(refs["own"][...], newest))
            add(3 - z, 3 * LANES, dot(far(z, refs, "5"), newest))

    def near_right(z):
        return z == 1

    def near_left(z):
        return z == 2

    r3 = routed([own_c, r1[0], r1[1]], [(0, third), (1, long), (1, long), None], long, [])
    r4 = routed([spare(0), r2[0], r2[1]], [(0, third), (1, third), (1, third), None], third, [])
    sums = absorb(
        place, third, dict(both("", r1), slab=(slab, always, at(0)), own=(own_a, always, at(0))), work1, sums_shape, None,
        first=lambda z, refs, add: work1(z, refs, add))
    sums = absorb(
        place, third, dict(both("", r2), slab=(slab, always, at(1)), own=(own_b, always, at(0))), work1, sums_shape, sums)
    r5 = routed([spare(1), r3[0], r3[1], own_c, own_c], [(0, third), (3, third), (1, long), None], long, [sums])
    sums = absorb(
        place, third,
        dict(both("", r3), slab=(slab, always, at(0)), slab2=(slab, always, at(2)), own=(own_c, always, at(0))),
        work3, sums_shape, sums, first=lambda z, refs, add: add((z + 2) % 4, 0, dot(far(z, refs, ""), refs["slab"])))
    r6 = routed([spare(2), r3[0], r3[1], r4[0], r4[1]], [(0, third), (1, third), (3, third), None], third, [sums])
    sums = absorb(place, third, dict(both("", r4), slab=(slab, always, at(1))), work4, sums_shape, sums)
    middle = dict(both("4", r4, near_right, near_left), own=(own_c, is_mid, at(0)))
    sums = absorb(
        place, third, dict(both("", r5), slab=(slab, always, thirds(0, 2)), **middle), work5, sums_shape, sums, first=first5)
    messages = absorb(
        place, third, dict(both("", r6), slab=(slab, always, thirds(1, 2)), **both("5", r5, is_mid, is_mid), **middle),
        work6, sums_shape, sums, profile=profile)

    summed = messages[0]
    for turn in range(1, owners):
        summed += lax.ppermute(messages[turn], SITES, [(i, i ^ turn) for i in range(owners)])
    weight_sum = summed[0, WIDTH - 2]
    half = WIDTH // 2
    frame_sum = jnp.sum(summed[:, :nrows], axis=1) + jnp.sum(summed[:, half:half + nrows], axis=1)
    lane = jnp.arange(half)
    mine, extra = (jnp.where(lane[None, :] == FREE, frame_sum[:, None], x) for x in (summed[:, :half], summed[:, half:]))
    def flip(turn):
        return [(a * owners + b, b * owners + (a ^ turn)) for a in range(wide) for b in range(owners)]

    mine, extra = lax.ppermute(mine, ALL, flip(0)), lax.ppermute(extra, ALL, flip(1))
    total = mine[:, FREE] + extra[:, FREE] + lax.ppermute(frame_sum, ALL, flip(2)) + lax.ppermute(frame_sum, ALL, flip(3))
    charges = (mine + extra)[:, :nrows].reshape(frames, panels, rows).transpose(1, 2, 0)
    return finish(charges, total, weight_sum, profile)


def solution(mesh):
    wide = mesh.shape["wide"]
    owners = mesh.shape["narrow"] * mesh.shape["sub"]
    plan = line_plan if wide == owners == 4 else gather_plan

    def local(slab, noise, volts, labels, profile):
        return plan(slab, noise, volts, labels, profile, (wide, owners))

    return jax.shard_map(
        local,
        mesh=mesh,
        in_specs=(
            P(None, "wide", ("narrow", "sub")),
            P(("grp", "wide"), ("narrow", "sub")),
            P(("grp", "wide"), None),
            P(("narrow", "sub")),
            P(None, ("narrow", "sub")),
        ),
        out_specs=P(None, ("narrow", "sub"), ("grp", "wide")),
        check_vma=False,
    )
```

```python
import jax
import jax.numpy as jnp
from jax import lax
from jax.experimental import pallas as pl
from jax.experimental.pallas import tpu as pltpu
from jax.sharding import PartitionSpec as P

SITES = ("narrow", "sub")
ALL = ("wide", "narrow", "sub")


def dot_t(a, b):
    return lax.dot_general(a, b, (((1,), (1,)), ((), ())), preferred_element_type=jnp.float32)


def potential_of(noise, volts, labels):
    value = volts[:, 0:1]
    for kind in range(1, volts.shape[1]):
        value = jnp.where(labels[None, :] == kind, volts[:, kind:kind + 1], value)
    return (value + noise.astype(jnp.float32)).astype(jnp.bfloat16)


def finish(charges, total, weight_sum, profile):
    return charges - profile[:, :, None] * (total / weight_sum)[None, None, :]


def gather_plan(slab, noise, volts, labels, profile, sizes):
    wide, owners = sizes
    panels, rows, _ = slab.shape
    frames = noise.shape[0]
    pot = lax.all_gather(potential_of(noise, volts, labels), "wide", axis=0, tiled=True)
    part = dot_t(slab.reshape(panels * rows, -1), pot).reshape(panels, rows, wide, frames)
    mine = lax.all_to_all(part, "wide", 2, 1, tiled=True).reshape(panels, wide * rows, frames)
    charges = lax.psum_scatter(mine, SITES, scatter_dimension=1, tiled=True)
    total, weight_sum = lax.psum((jnp.sum(charges, axis=(0, 1)), jnp.sum(profile)), SITES)
    return finish(charges, total, weight_sum, profile)


LANES = 128
STEPS = 4
ROWS = 64
WIDTH = 4 * LANES
FREE = LANES * 2 - 1
PARAMS = pltpu.CompilerParams(vmem_limit_bytes=56 * 1024 * 1024)
SMALL = pl.CostEstimate(flops=1000, bytes_accessed=1000, transcendentals=0)


def always(z):
    return z >= 0


def is_mid(z):
    return (z == 1) | (z == 2)


def is_end(z):
    return (z == 0) | (z == 3)


def dot(a, b):
    return lax.dot_general(a, b, (((1,), (1,)), ((), ())), preferred_element_type=jnp.float32)


def first_potential(noise, volts, labels, third):
    frames, sites = noise.shape
    tile = third // STEPS
    rest = sites - 3 * third
    rest_width = rest + -rest % LANES
    labels = labels.reshape(1, sites)
    volts = volts.T

    def kernel(noise_ref, labels_ref, volts_ref, noise_rest, labels_rest, out):
        def column_of(kind):
            shape = (frames, frames)
            diagonal = lax.broadcasted_iota(jnp.int32, shape, 0) == lax.broadcasted_iota(jnp.int32, shape, 1)
            return jnp.sum(jnp.where(diagonal, volts_ref[kind:kind + 1, :], 0.0), axis=1, keepdims=True)

        def potential(noise, labels):
            value = jnp.broadcast_to(column_of(0), noise.shape)
            for kind in range(1, volts_ref.shape[0]):
                value = jnp.where(labels == kind, column_of(kind), value)
            return value + noise.astype(jnp.float32)

        step = pl.program_id(0)
        at = pl.multiple_of(step * tile, LANES)
        out[:, pl.ds(at, tile)] = potential(noise_ref[...], labels_ref[...]).astype(jnp.bfloat16)

        @pl.when(step == 0)
        def _():
            column = lax.broadcasted_iota(jnp.int32, (frames, rest_width), 1)
            value = jnp.where(column < rest, potential(noise_rest[...], labels_rest[...]), 0.0)
            out[:, third:] = value.astype(jnp.bfloat16)

    last = 3 * third // rest_width
    return pl.pallas_call(
        kernel,
        grid=(STEPS,),
        in_specs=[
            pl.BlockSpec((frames, tile), lambda i: (0, i)),
            pl.BlockSpec((1, tile), lambda i: (0, i)),
            pl.BlockSpec(volts.shape, lambda i: (0, 0)),
            pl.BlockSpec((frames, rest_width), lambda i: (0, last)),
            pl.BlockSpec((1, rest_width), lambda i: (0, last)),
        ],
        out_specs=pl.BlockSpec((frames, third + rest_width), lambda i: (0, 0)),
        out_shape=jax.ShapeDtypeStruct((frames, third + rest_width), jnp.bfloat16),
        compiler_params=PARAMS,
        cost_estimate=SMALL,
    )(noise, labels, volts, noise, labels)


def route(place, whole, sources, to_right, to_left, width, tokens):
    tile = whole // STEPS
    count = len(sources)
    frames = ROWS

    def kernel(place_ref, *refs):
        outs = refs[count + len(tokens):]
        z = place_ref[0]
        for here in range(4):
            @pl.when(z == here)
            def _(here=here):
                for out, number in zip(outs, (to_right[here], to_left[here])):
                    if number is not None:
                        out[...] = refs[number][...]

    def spec(number):
        array, row, column = sources[number]
        last = (array.shape[1] - 1) // tile if column == 0 else column + STEPS - 1
        users = [here for here in range(4) if number in (to_right[here], to_left[here])]

        def index(i, s):
            used = sum((s[0] == here).astype(jnp.int32) for here in users)
            return row, jnp.minimum(column + i * used, last)

        return pl.BlockSpec((frames, tile), index)

    out_spec = pl.BlockSpec((frames, tile), lambda i, s: (0, i))
    return pl.pallas_call(
        kernel,
        grid_spec=pltpu.PrefetchScalarGridSpec(
            num_scalar_prefetch=1, grid=(pl.cdiv(width, tile),),
            in_specs=[spec(n) for n in range(count)] + [pl.BlockSpec(memory_space=pl.ANY)] * len(tokens),
            out_specs=[out_spec] * 2),
        out_shape=[jax.ShapeDtypeStruct((frames, width), jnp.bfloat16)] * 2,
        compiler_params=PARAMS,
        cost_estimate=SMALL,
    )(place, *[s[0] for s in sources], *tokens)


def absorb(place, whole, streams, work, sums_shape, sums, first=None, profile=None):
    tile = whole // STEPS
    names = list(streams)
    slab = streams["slab"][0]
    nrows, sites = slab.shape
    rest = sites - 3 * whole
    rest_width = rest + -rest % LANES
    long = [n for n in names if n in ("r", "l", "own") and streams[n][0].shape[1] == whole + rest_width] if first else []
    blocks, frames, width = sums_shape

    def kernel(place_ref, *refs):
        tiles = dict(zip(names, refs))
        refs = refs[len(names):]
        if sums is not None:
            sums_ref, refs = refs[0], refs[1:]
        if first:
            slab_rest, refs = refs[0], refs[1:]
            rests = dict(zip(long, refs))
            refs = refs[len(long):]
        if profile is None:
            acc, = refs
            turned = None
        else:
            profile_ref, outs, acc, turned = refs[0], refs[1:-2], refs[-2], refs[-1]
        z, k = place_ref[0], place_ref[1]
        step = pl.program_id(0)

        def add(block, lane, value):
            acc[block, :, lane:lane + value.shape[1]] += value

        @pl.when(step == 0)
        def _():
            acc[...] = jnp.zeros(acc.shape, acc.dtype) if sums is None else sums_ref[...]
            if first:
                column = lax.broadcasted_iota(jnp.int32, (nrows, rest_width), 1)
                piece = jnp.where(column < rest, slab_rest[...].astype(jnp.float32), 0.0).astype(jnp.bfloat16)
                first(z, dict(rests, slab=piece), add)

            if turned is not None:
                turned[...] = jnp.zeros(turned.shape, turned.dtype)

        work(z, tiles, add, *([] if turned is None else [turned]))

        if profile is not None:
            @pl.when(step == STEPS - 1)
            def _():
                block = jnp.where(z < 2, 3, 0)
                add(block, 0, turned[:nrows].T[:frames])
                add(block, width // 2, turned[nrows:].T[:frames])
                weight = jnp.sum(profile_ref[...])
                lane = lax.broadcasted_iota(jnp.int32, (frames, LANES), 1)
                for turn, out in enumerate(outs):
                    out[:, :width - LANES] = acc[k ^ turn, :, :width - LANES]
                    end = acc[k ^ turn, :, width - LANES:]
                    out[:, width - LANES:] = jnp.where(lane == LANES - 2, weight, end)

    def spec(array, needed, third):
        return pl.BlockSpec(
            (array.shape[0], tile), lambda i, s: (0, third(s[0]) * STEPS + jnp.where(needed(s[0]), i, 0)))

    in_specs = [spec(*streams[n]) for n in names]
    operands = [streams[n][0] for n in names]
    if sums is not None:
        in_specs.append(pl.BlockSpec(sums_shape, lambda i, s: (0, 0, 0)))
        operands.append(sums)
    if first:
        in_specs.append(pl.BlockSpec((nrows, rest_width), lambda i, s: (0, 3 * whole // rest_width)))
        in_specs += [pl.BlockSpec((frames, rest_width), lambda i, s: (0, whole // rest_width))] * len(long)
        operands += [slab] + [streams[n][0] for n in long]
    if profile is None:
        out_shape = jax.ShapeDtypeStruct(sums_shape, jnp.float32)
        out_specs = pl.BlockSpec(sums_shape, lambda i, s: (0, 0, 0))
        scratch = []
    else:
        in_specs.append(pl.BlockSpec(profile.shape, lambda i, s: (0, 0)))
        operands.append(profile)
        out_shape = [jax.ShapeDtypeStruct(sums_shape[1:], jnp.float32)] * blocks
        out_specs = [pl.BlockSpec(sums_shape[1:], lambda i, s: (0, 0))] * blocks
        scratch = [pltpu.VMEM(sums_shape, jnp.float32), pltpu.VMEM((2 * nrows, LANES), jnp.float32)]
    return pl.pallas_call(
        kernel,
        grid_spec=pltpu.PrefetchScalarGridSpec(
            num_scalar_prefetch=1, grid=(STEPS,), in_specs=in_specs, out_specs=out_specs, scratch_shapes=scratch),
        out_shape=out_shape,
        compiler_params=PARAMS,
        cost_estimate=SMALL,
    )(place, *operands)


def line_plan(slab, noise, volts, labels, profile, sizes):
    wide, owners = sizes
    panels, rows, sites = slab.shape
    frames = noise.shape[0]
    nrows = panels * rows
    third = sites // 3 // LANES * LANES
    z = lax.axis_index("wide")
    k = lax.axis_index(SITES)
    place = jnp.stack([z, k]).astype(jnp.int32)
    slab = slab.reshape(nrows, sites)
    right = [(0, 1), (1, 2), (2, 3)]
    left = [(3, 2), (2, 1), (1, 0)]

    def send(pair):
        return lax.ppermute(pair[0], "wide", right), lax.ppermute(pair[1], "wide", left)

    def potential_at(first, end, before):
        small = lax.optimization_barrier((volts, before))[0]
        return potential_of(noise[:, first:end], small, labels[first:end])

    def mirror(choice):
        swap = {0: 0, 1: 2, 2: 1, 3: 4, 4: 3}
        return [swap.get(c) for c in reversed(choice)]

    def routed(sources, choice, width, tokens):
        sources = [s if isinstance(s, tuple) else (s, 0, 0) for s in sources]
        pair = route(place, third, sources, choice, mirror(choice), width, tokens)
        return send(pair), pair[0]

    def spare(i):
        return (slab, i, 2 * STEPS)

    own_a = first_potential(noise, volts, labels, third)
    long = own_a.shape[1]
    r1 = send((own_a, own_a))
    own_b = potential_at(third, 2 * third, own_a)
    r2 = send((own_b, own_b))
    own_c = potential_at(2 * third, 3 * third, own_b)

    sums_shape = (wide, frames, WIDTH)

    def at(number):
        return lambda z: number

    def thirds(end, mid):
        return lambda z: jnp.where(is_mid(z), mid, end)

    def from_left(z):
        return z >= 1

    def from_right(z):
        return z <= 2

    def far(z, refs, name):
        return jnp.where(z < 2, refs[name + "l"][...], refs[name + "r"][...])

    def near(z, refs, name):
        return jnp.where(z < 2, refs[name + "r"][...], refs[name + "l"][...])

    def both(name, pair, right_needed=from_left, left_needed=from_right):
        return {name + "r": (pair[0], right_needed, at(0)), name + "l": (pair[1], left_needed, at(0))}

    def work1(z, refs, add):
        add(z, 0, dot(refs["own"][...], refs["slab"][...]))

        @pl.when(z >= 1)
        def _():
            add(z - 1, 0, dot(refs["r"][...], refs["slab"][...]))

        @pl.when(z <= 2)
        def _():
            add(z + 1, 0, dot(refs["l"][...], refs["slab"][...]))

    def work3(z, refs, add):
        add(z, 0, dot(refs["own"][...], refs["slab2"][...]))
        add((z + 2) % 4, 0, dot(far(z, refs, ""), refs["slab"][...]))

        @pl.when(is_mid(z))
        def _():
            add(jnp.where(z < 2, 0, 3), 0, dot(near(z, refs, ""), refs["slab2"][...]))

    def work4(z, refs, add):
        add((z + 2) % 4, 0, dot(far(z, refs, ""), refs["slab"][...]))

    def work5(z, refs, add):
        came = far(z, refs, "")
        add(3 - z, 0, dot(came, refs["slab"][...]))

        @pl.when(is_mid(z))
        def _():
            brought = jnp.concatenate([near(z, refs, "4"), near(z, refs, "")], axis=0)
            add(z, 2 * LANES, dot(refs["own"][...], brought))
            add(3 - z, 2 * LANES, dot(came, brought))

    def first3(z, refs, add):
        add((z + 2) % 4, 0, dot(far(z, refs, ""), refs["slab"]))

    def first5(z, refs, add):
        @pl.when(is_end(z))
        def _():
            add(3 - z, 0, dot(far(z, refs, ""), refs["slab"]))

    def work6(z, refs, add, turned):
        came = far(z, refs, "")
        turned[:nrows, :frames] += dot(refs["slab"][...], came)

        @pl.when(is_mid(z))
        def _():
            newest = near(z, refs, "")
            brought = jnp.concatenate([near(z, refs, "4"), near(z, refs, "5"), newest], axis=0)
            turned[nrows:, :frames] += dot(brought, came)
            both = dot(jnp.concatenate([refs["own"][...], far(z, refs, "5")], axis=0), newest)
            add(z, 3 * LANES, both[:frames])
            add(3 - z, 3 * LANES, both[frames:])

    def near_right(z):
        return z == 1

    def near_left(z):
        return z == 2

    r3, sent = routed([own_c, r1[0], r1[1]], [0, 1, 1, None], long, [])
    r4, sent = routed([spare(0), r2[0], r2[1]], [0, 1, 1, None], third, [sent])
    sums = absorb(
        place, third, dict(both("", r1), slab=(slab, always, at(0)), own=(own_a, always, at(0))), work1, sums_shape, None,
        first=work1)
    sums = absorb(
        place, third, dict(both("", r2), slab=(slab, always, at(1)), own=(own_b, always, at(0))), work1, sums_shape, sums)
    r5, sent = routed([spare(1), r3[0], r3[1], own_c, own_c], [0, 3, 1, None], long, [sent, sums])
    sums = absorb(
        place, third,
        dict(both("", r3), slab=(slab, always, at(0)), slab2=(slab, always, at(2)), own=(own_c, always, at(0))),
        work3, sums_shape, sums, first=first3)
    r6, sent = routed([spare(2), r3[0], r3[1], r4[0], r4[1]], [0, 1, 3, None], third, [sent, sums])
    sums = absorb(
        place, third, dict(both("", r4), slab=(slab, always, at(1))), work4, sums_shape, sums)
    middle = dict(both("4", r4, near_right, near_left), own=(own_c, is_mid, at(0)))
    sums = absorb(place, third, dict(both("", r5), slab=(slab, always, thirds(0, 2)), **middle), work5, sums_shape, sums,
        first=first5)
    messages = absorb(
        place, third, dict(both("", r6), slab=(slab, always, thirds(1, 2)), **both("5", r5, is_mid, is_mid), **middle),
        work6, sums_shape, sums, profile=profile)

    summed = messages[0]
    for turn in range(1, owners):
        summed += lax.ppermute(messages[turn], SITES, [(i, i ^ turn) for i in range(owners)])
    weight_sum = summed[0, WIDTH - 2]
    half = WIDTH // 2
    frame_sum = jnp.sum(summed[:, :nrows], axis=1) + jnp.sum(summed[:, half:half + nrows], axis=1)
    lane = jnp.arange(half)
    mine, extra = (jnp.where(lane[None, :] == FREE, frame_sum[:, None], x) for x in (summed[:, :half], summed[:, half:]))
    def flip(turn):
        return [(a * owners + b, b * owners + (a ^ turn)) for a in range(wide) for b in range(owners)]

    mine, extra = lax.ppermute(mine, ALL, flip(0)), lax.ppermute(extra, ALL, flip(1))
    total = mine[:, FREE] + extra[:, FREE] + lax.ppermute(frame_sum, ALL, flip(2)) + lax.ppermute(frame_sum, ALL, flip(3))
    charges = (mine + extra)[:, :nrows].reshape(frames, panels, rows).transpose(1, 2, 0)
    return finish(charges, total, weight_sum, profile)


def solution(mesh):
    wide = mesh.shape["wide"]
    owners = mesh.shape["narrow"] * mesh.shape["sub"]
    plan = line_plan if wide == owners == 4 else gather_plan

    def local(slab, noise, volts, labels, profile):
        return plan(slab, noise, volts, labels, profile, (wide, owners))

    return jax.shard_map(
        local,
        mesh=mesh,
        in_specs=(
            P(None, "wide", ("narrow", "sub")),
            P(("grp", "wide"), ("narrow", "sub")),
            P(("grp", "wide"), None),
            P(("narrow", "sub")),
            P(None, ("narrow", "sub")),
        ),
        out_specs=P(None, ("narrow", "sub"), ("grp", "wide")),
        check_vma=False,
    )
```

```python
import jax
import jax.numpy as jnp
from jax import lax
from jax.experimental import pallas as pl
from jax.experimental.pallas import tpu as pltpu
from jax.sharding import PartitionSpec as P

SITES = ("narrow", "sub")
ALL = ("wide", "narrow", "sub")


def dot_t(a, b):
    return lax.dot_general(a, b, (((1,), (1,)), ((), ())), preferred_element_type=jnp.float32)


def potential_of(noise, volts, labels):
    value = volts[:, 0:1]
    for kind in range(1, volts.shape[1]):
        value = jnp.where(labels[None, :] == kind, volts[:, kind:kind + 1], value)
    return (value + noise.astype(jnp.float32)).astype(jnp.bfloat16)


def finish(charges, total, weight_sum, profile):
    return charges - profile[:, :, None] * (total / weight_sum)[None, None, :]


def gather_plan(slab, noise, volts, labels, profile, sizes):
    wide, owners = sizes
    panels, rows, _ = slab.shape
    frames = noise.shape[0]
    pot = lax.all_gather(potential_of(noise, volts, labels), "wide", axis=0, tiled=True)
    part = dot_t(slab.reshape(panels * rows, -1), pot).reshape(panels, rows, wide, frames)
    mine = lax.all_to_all(part, "wide", 2, 1, tiled=True).reshape(panels, wide * rows, frames)
    charges = lax.psum_scatter(mine, SITES, scatter_dimension=1, tiled=True)
    total, weight_sum = lax.psum((jnp.sum(charges, axis=(0, 1)), jnp.sum(profile)), SITES)
    return finish(charges, total, weight_sum, profile)


LANES = 128
STEPS = 4
ROWS = 64
WIDTH = 4 * LANES
FREE = LANES * 2 - 1
PARAMS = pltpu.CompilerParams(vmem_limit_bytes=16 * 1024 * 1024)
SMALL = pl.CostEstimate(flops=1000, bytes_accessed=1000, transcendentals=0)


def always(z):
    return z >= 0


def is_mid(z):
    return (z == 1) | (z == 2)


def is_end(z):
    return (z == 0) | (z == 3)


def dot(a, b):
    return lax.dot_general(a, b, (((1,), (1,)), ((), ())), preferred_element_type=jnp.float32)


def later_potentials(noise, volts, labels, third, token):
    frames, sites = noise.shape
    tile = third // STEPS
    rest = sites - 3 * third
    rest_width = rest + -rest % LANES
    labels = labels.reshape(1, sites)
    volts = volts.T

    def kernel(noise_b, labels_b, noise_c, labels_c, noise_rest, labels_rest, volts_ref, token_ref, out_b, out_c):
        diagonal = (lax.broadcasted_iota(jnp.int32, (frames, frames), 0)
                    == lax.broadcasted_iota(jnp.int32, (frames, frames), 1))
        columns = [jnp.sum(jnp.where(diagonal, volts_ref[kind:kind + 1, :], 0.0), axis=1, keepdims=True)
                   for kind in range(volts_ref.shape[0])]

        def potential(noise, labels):
            value = jnp.broadcast_to(columns[0], noise.shape)
            for kind in range(1, len(columns)):
                value = jnp.where(labels == kind, columns[kind], value)
            return value + noise.astype(jnp.float32)

        step = pl.program_id(0)
        at = pl.multiple_of(step * tile, LANES)
        out_b[:, pl.ds(at, tile)] = potential(noise_b[...], labels_b[...]).astype(jnp.bfloat16)
        out_c[...] = potential(noise_c[...], labels_c[...]).astype(jnp.bfloat16)

        @pl.when(step == 0)
        def _():
            column = lax.broadcasted_iota(jnp.int32, (frames, rest_width), 1)
            value = jnp.where(column < rest, potential(noise_rest[...], labels_rest[...]), 0.0)
            out_b[:, third:] = value.astype(jnp.bfloat16)

    last = 3 * third // rest_width
    return pl.pallas_call(
        kernel,
        grid=(STEPS,),
        in_specs=[
            pl.BlockSpec((frames, tile), lambda i: (0, STEPS + i)),
            pl.BlockSpec((1, tile), lambda i: (0, STEPS + i)),
            pl.BlockSpec((frames, tile), lambda i: (0, 2 * STEPS + i)),
            pl.BlockSpec((1, tile), lambda i: (0, 2 * STEPS + i)),
            pl.BlockSpec((frames, rest_width), lambda i: (0, last)),
            pl.BlockSpec((1, rest_width), lambda i: (0, last)),
            pl.BlockSpec(volts.shape, lambda i: (0, 0)),
            pl.BlockSpec(memory_space=pl.ANY),
        ],
        out_specs=[pl.BlockSpec((frames, third + rest_width), lambda i: (0, 0)),
                   pl.BlockSpec((frames, tile), lambda i: (0, i))],
        out_shape=[jax.ShapeDtypeStruct((frames, third + rest_width), jnp.bfloat16),
                   jax.ShapeDtypeStruct((frames, third), jnp.bfloat16)],
        compiler_params=PARAMS,
        cost_estimate=SMALL,
    )(noise, labels, noise, labels, noise, labels, volts, token)


def route(place, whole, sources, to_right, to_left, width, tokens):
    tile = whole // STEPS
    count = len(sources)
    frames = ROWS

    def kernel(place_ref, *refs):
        outs = refs[count + len(tokens):]
        z = place_ref[0]
        for here in range(4):
            @pl.when(z == here)
            def _(here=here):
                for out, number in zip(outs, (to_right[here], to_left[here])):
                    if number is not None:
                        out[...] = refs[number][...]

    def spec(number):
        array, row, column = sources[number]
        last = (array.shape[1] - 1) // tile if column == 0 else column + STEPS - 1
        users = [here for here in range(4) if number in (to_right[here], to_left[here])]

        def index(i, s):
            used = sum((s[0] == here).astype(jnp.int32) for here in users)
            return row, jnp.minimum(column + i * used, last)

        return pl.BlockSpec((frames, tile), index)

    out_spec = pl.BlockSpec((frames, tile), lambda i, s: (0, i))
    return pl.pallas_call(
        kernel,
        grid_spec=pltpu.PrefetchScalarGridSpec(
            num_scalar_prefetch=1, grid=(pl.cdiv(width, tile),),
            in_specs=[spec(n) for n in range(count)] + [pl.BlockSpec(memory_space=pl.ANY)] * len(tokens),
            out_specs=[out_spec] * 2),
        out_shape=[jax.ShapeDtypeStruct((frames, width), jnp.bfloat16)] * 2,
        compiler_params=PARAMS,
        cost_estimate=SMALL,
    )(place, *[s[0] for s in sources], *tokens)


def absorb(place, whole, streams, work, sums_shape, sums, first=None, profile=None):
    tile = whole // STEPS
    names = list(streams)
    slab = streams["slab"][0]
    nrows, sites = slab.shape
    rest = sites - 3 * whole
    rest_width = rest + -rest % LANES
    long = [n for n in names if n in ("r", "l", "own") and streams[n][0].shape[1] == whole + rest_width] if first else []
    blocks, frames, width = sums_shape

    def kernel(place_ref, *refs):
        tiles = dict(zip(names, refs))
        refs = refs[len(names):]
        if sums is not None:
            sums_ref, refs = refs[0], refs[1:]
        if first:
            slab_rest, refs = refs[0], refs[1:]
            rests = dict(zip(long, refs))
            refs = refs[len(long):]
        if profile is None:
            acc, = refs
            turned = None
        else:
            profile_ref, outs, acc, turned = refs[0], refs[1:-2], refs[-2], refs[-1]
        z, k = place_ref[0], place_ref[1]
        step = pl.program_id(0)

        def add(block, lane, value):
            acc[block, :, lane:lane + value.shape[1]] += value

        @pl.when(step == 0)
        def _():
            acc[...] = jnp.zeros(acc.shape, acc.dtype) if sums is None else sums_ref[...]
            if turned is not None:
                turned[...] = jnp.zeros(turned.shape, turned.dtype)
            if first:
                column = lax.broadcasted_iota(jnp.int32, (nrows, rest_width), 1)
                piece = jnp.where(column < rest, slab_rest[...].astype(jnp.float32), 0.0).astype(jnp.bfloat16)
                first(z, dict(rests, slab=piece), add, turned)


        work(z, tiles, add, turned)

        if profile is not None:
            @pl.when(step == STEPS - 1)
            def _():
                block = jnp.where(z < 2, 3, 0)
                add(block, 0, turned[:nrows].T[:frames])
                add(block, width // 2, turned[nrows:].T[:frames])
                weight = jnp.sum(profile_ref[...])
                lane = lax.broadcasted_iota(jnp.int32, (frames, LANES), 1)
                for turn, out in enumerate(outs):
                    out[:, :width - LANES] = acc[k ^ turn, :, :width - LANES]
                    end = acc[k ^ turn, :, width - LANES:]
                    out[:, width - LANES:] = jnp.where(lane == LANES - 2, weight, end)

    def spec(array, needed, third):
        return pl.BlockSpec(
            (array.shape[0], tile), lambda i, s: (0, third(s[0]) * STEPS + jnp.where(needed(s[0]), i, 0)))

    in_specs = [spec(*streams[n]) for n in names]
    operands = [streams[n][0] for n in names]
    if sums is not None:
        in_specs.append(pl.BlockSpec(sums_shape, lambda i, s: (0, 0, 0)))
        operands.append(sums)
    if first:
        in_specs.append(pl.BlockSpec((nrows, rest_width), lambda i, s: (0, 3 * whole // rest_width)))
        in_specs += [pl.BlockSpec((frames, rest_width), lambda i, s: (0, whole // rest_width))] * len(long)
        operands += [slab] + [streams[n][0] for n in long]
    if profile is None:
        out_shape = jax.ShapeDtypeStruct(sums_shape, jnp.float32)
        out_specs = pl.BlockSpec(sums_shape, lambda i, s: (0, 0, 0))
        scratch = []
    else:
        in_specs.append(pl.BlockSpec(profile.shape, lambda i, s: (0, 0)))
        operands.append(profile)
        out_shape = [jax.ShapeDtypeStruct(sums_shape[1:], jnp.float32)] * blocks
        out_specs = [pl.BlockSpec(sums_shape[1:], lambda i, s: (0, 0))] * blocks
        scratch = [pltpu.VMEM(sums_shape, jnp.float32), pltpu.VMEM((2 * nrows, LANES), jnp.float32)]
    return pl.pallas_call(
        kernel,
        grid_spec=pltpu.PrefetchScalarGridSpec(
            num_scalar_prefetch=1, grid=(STEPS,), in_specs=in_specs, out_specs=out_specs, scratch_shapes=scratch),
        out_shape=out_shape,
        compiler_params=PARAMS,
        cost_estimate=SMALL,
    )(place, *operands)


def line_plan(slab, noise, volts, labels, profile, sizes):
    wide, owners = sizes
    panels, rows, sites = slab.shape
    frames = noise.shape[0]
    nrows = panels * rows
    third = sites // 3 // LANES * LANES
    z = lax.axis_index("wide")
    k = lax.axis_index(SITES)
    place = jnp.stack([z, k]).astype(jnp.int32)
    slab = slab.reshape(nrows, sites)
    right = [(0, 1), (1, 2), (2, 3)]
    left = [(3, 2), (2, 1), (1, 0)]

    def send(pair):
        return lax.ppermute(pair[0], "wide", right), lax.ppermute(pair[1], "wide", left)

    def mirror(choice):
        swap = {0: 0, 1: 2, 2: 1, 3: 4, 4: 3}
        return [swap.get(c) for c in reversed(choice)]

    def routed(sources, choice, width, tokens):
        sources = [s if isinstance(s, tuple) else (s, 0, 0) for s in sources]
        pair = route(place, third, sources, choice, mirror(choice), width, tokens)
        return send(pair), pair[0]

    def spare(i):
        return (slab, i, 2 * STEPS)

    rest = sites - 3 * third
    long = third + rest + -rest % LANES
    own_a = potential_of(noise[:, :long], volts, labels[:long])
    r1 = send((own_a, own_a))
    own_b, own_c = later_potentials(noise, volts, labels, third, own_a)
    r2 = send((own_b, own_b))

    sums_shape = (wide, frames, WIDTH)

    def at(number):
        return lambda z: number

    def thirds(end, mid):
        return lambda z: jnp.where(is_mid(z), mid, end)

    def from_left(z):
        return z >= 1

    def from_right(z):
        return z <= 2

    def far(z, refs, name):
        return jnp.where(z < 2, refs[name + "l"][...], refs[name + "r"][...])

    def near(z, refs, name):
        return jnp.where(z < 2, refs[name + "r"][...], refs[name + "l"][...])

    def both(name, pair, right_needed=from_left, left_needed=from_right):
        return {name + "r": (pair[0], right_needed, at(0)), name + "l": (pair[1], left_needed, at(0))}

    def work1(z, refs, add, turned):
        add(z, 0, dot(refs["own"][...], refs["slab"][...]))

        @pl.when(z >= 1)
        def _():
            add(z - 1, 0, dot(refs["r"][...], refs["slab"][...]))

        @pl.when(z <= 2)
        def _():
            add(z + 1, 0, dot(refs["l"][...], refs["slab"][...]))

    def work3(z, refs, add, turned):
        add(z, 0, dot(refs["own"][...], refs["slab2"][...]))
        add((z + 2) % 4, 0, dot(far(z, refs, ""), refs["slab"][...]))

        @pl.when(is_mid(z))
        def _():
            add(jnp.where(z < 2, 0, 3), 0, dot(near(z, refs, ""), refs["slab2"][...]))

    def work4(z, refs, add, turned):
        add((z + 2) % 4, 0, dot(far(z, refs, ""), refs["slab"][...]))

    def work5(z, refs, add, turned):
        came = far(z, refs, "")
        add(3 - z, 0, dot(came, refs["slab"][...]))

        @pl.when(is_mid(z))
        def _():
            brought = jnp.concatenate([near(z, refs, "4"), near(z, refs, "")], axis=0)
            add(z, 2 * LANES, dot(refs["own"][...], brought))
            add(3 - z, 2 * LANES, dot(came, brought))

    def first4(z, refs, add, turned):
        add((z + 2) % 4, 0, dot(far(z, refs, ""), refs["slab"]))

    def first6(z, refs, add, turned):
        @pl.when(is_end(z))
        def _():
            turned[:nrows, :frames] += dot(refs["slab"], far(z, refs, ""))

    def work6(z, refs, add, turned):
        came = far(z, refs, "")
        turned[:nrows, :frames] += dot(refs["slab"][...], came)

        @pl.when(is_mid(z))
        def _():
            newest = near(z, refs, "")
            brought = jnp.concatenate([near(z, refs, "4"), near(z, refs, "5"), newest], axis=0)
            turned[nrows:, :frames] += dot(brought, came)
            both = dot(jnp.concatenate([refs["own"][...], far(z, refs, "5")], axis=0), newest)
            add(z, 3 * LANES, both[:frames])
            add(3 - z, 3 * LANES, both[frames:])

    def near_right(z):
        return z == 1

    def near_left(z):
        return z == 2

    r3, sent = routed([own_c, r1[0], r1[1]], [0, 1, 1, None], long, [])
    r4, sent = routed([spare(0), r2[0], r2[1]], [0, 1, 1, None], long, [sent])
    sums = absorb(
        place, third, dict(both("", r1), slab=(slab, always, at(0)), own=(own_a, always, at(0))), work1, sums_shape, None)
    sums = absorb(
        place, third, dict(both("", r2), slab=(slab, always, at(1)), own=(own_b, always, at(0))), work1, sums_shape, sums,
        first=work1)
    r5, sent = routed([spare(1), r3[0], r3[1], own_c, own_c], [0, 3, 1, None], long, [sent, sums])
    sums = absorb(
        place, third,
        dict(both("", r3), slab=(slab, always, at(0)), slab2=(slab, always, at(2)), own=(own_c, always, at(0))),
        work3, sums_shape, sums)
    r6, sent = routed([spare(2), r3[0], r3[1], r4[0], r4[1]], [0, 1, 3, None], long, [sent, sums])
    sums = absorb(
        place, third, dict(both("", r4), slab=(slab, always, at(1))), work4, sums_shape, sums, first=first4)
    middle = dict(both("4", r4, near_right, near_left), own=(own_c, is_mid, at(0)))
    sums = absorb(place, third, dict(both("", r5), slab=(slab, always, thirds(0, 2)), **middle), work5, sums_shape, sums)
    messages = absorb(
        place, third, dict(both("", r6), slab=(slab, always, thirds(1, 2)), **both("5", r5, is_mid, is_mid), **middle),
        work6, sums_shape, sums, first=first6, profile=profile)

    summed = messages[0]
    for turn in range(1, owners):
        summed += lax.ppermute(messages[turn], SITES, [(i, i ^ turn) for i in range(owners)])
    weight_sum = summed[0, WIDTH - 2]
    half = WIDTH // 2
    frame_sum = jnp.sum(summed[:, :nrows], axis=1) + jnp.sum(summed[:, half:half + nrows], axis=1)
    lane = jnp.arange(half)
    mine, extra = (jnp.where(lane[None, :] == FREE, frame_sum[:, None], x) for x in (summed[:, :half], summed[:, half:]))
    def flip(turn):
        return [(a * owners + b, b * owners + (a ^ turn)) for a in range(wide) for b in range(owners)]

    mine, extra = lax.ppermute(mine, ALL, flip(0)), lax.ppermute(extra, ALL, flip(1))
    total = mine[:, FREE] + extra[:, FREE] + lax.ppermute(frame_sum, ALL, flip(2)) + lax.ppermute(frame_sum, ALL, flip(3))
    charges = (mine + extra)[:, :nrows].reshape(frames, panels, rows).transpose(1, 2, 0)
    return finish(charges, total, weight_sum, profile)


def solution(mesh):
    wide = mesh.shape["wide"]
    owners = mesh.shape["narrow"] * mesh.shape["sub"]
    plan = line_plan if wide == owners == 4 else gather_plan

    def local(slab, noise, volts, labels, profile):
        return plan(slab, noise, volts, labels, profile, (wide, owners))

    return jax.shard_map(
        local,
        mesh=mesh,
        in_specs=(
            P(None, "wide", ("narrow", "sub")),
            P(("grp", "wide"), ("narrow", "sub")),
            P(("grp", "wide"), None),
            P(("narrow", "sub")),
            P(None, ("narrow", "sub")),
        ),
        out_specs=P(None, ("narrow", "sub"), ("grp", "wide")),
        check_vma=False,
    )
```

```python
import jax
import jax.numpy as jnp
from jax import lax
from jax.experimental import pallas as pl
from jax.experimental.pallas import tpu as pltpu
from jax.sharding import PartitionSpec as P

SITES = ("narrow", "sub")
ALL = ("wide", "narrow", "sub")


def dot_t(a, b):
    return lax.dot_general(a, b, (((1,), (1,)), ((), ())), preferred_element_type=jnp.float32)


def potential_of(noise, volts, labels):
    value = volts[:, 0:1]
    for kind in range(1, volts.shape[1]):
        value = jnp.where(labels[None, :] == kind, volts[:, kind:kind + 1], value)
    return (value + noise.astype(jnp.float32)).astype(jnp.bfloat16)


def finish(charges, total, weight_sum, profile):
    return charges - profile[:, :, None] * (total / weight_sum)[None, None, :]


def gather_plan(slab, noise, volts, labels, profile, sizes):
    wide, owners = sizes
    panels, rows, _ = slab.shape
    frames = noise.shape[0]
    pot = lax.all_gather(potential_of(noise, volts, labels), "wide", axis=0, tiled=True)
    part = dot_t(slab.reshape(panels * rows, -1), pot).reshape(panels, rows, wide, frames)
    mine = lax.all_to_all(part, "wide", 2, 1, tiled=True).reshape(panels, wide * rows, frames)
    charges = lax.psum_scatter(mine, SITES, scatter_dimension=1, tiled=True)
    total, weight_sum = lax.psum((jnp.sum(charges, axis=(0, 1)), jnp.sum(profile)), SITES)
    return finish(charges, total, weight_sum, profile)


LANES = 128
STEPS = 4
ROWS = 64
WIDTH = 4 * LANES
FREE = LANES * 2 - 1
PARAMS = pltpu.CompilerParams(vmem_limit_bytes=16 * 1024 * 1024)
SMALL = pl.CostEstimate(flops=1000, bytes_accessed=1000, transcendentals=0)


def always(z):
    return z >= 0


def is_mid(z):
    return (z == 1) | (z == 2)


def is_end(z):
    return (z == 0) | (z == 3)


def dot(a, b):
    return lax.dot_general(a, b, (((1,), (1,)), ((), ())), preferred_element_type=jnp.float32)


def later_potentials(noise, volts, labels, third, token):
    frames, sites = noise.shape
    tile = third // STEPS
    rest = sites - 3 * third
    rest_width = rest + -rest % LANES
    labels = labels.reshape(1, sites)
    volts = volts.T

    def kernel(noise_b, labels_b, noise_c, labels_c, noise_rest, labels_rest, volts_ref, token_ref, out_b, out_c):
        diagonal = (lax.broadcasted_iota(jnp.int32, (frames, frames), 0)
                    == lax.broadcasted_iota(jnp.int32, (frames, frames), 1))
        columns = [jnp.sum(jnp.where(diagonal, volts_ref[kind:kind + 1, :], 0.0), axis=1, keepdims=True)
                   for kind in range(volts_ref.shape[0])]

        def potential(noise, labels):
            value = jnp.broadcast_to(columns[0], noise.shape)
            for kind in range(1, len(columns)):
                value = jnp.where(labels == kind, columns[kind], value)
            return value + noise.astype(jnp.float32)

        step = pl.program_id(0)
        at = pl.multiple_of(step * tile, LANES)
        out_b[:, pl.ds(at, tile)] = potential(noise_b[...], labels_b[...]).astype(jnp.bfloat16)
        out_c[...] = potential(noise_c[...], labels_c[...]).astype(jnp.bfloat16)

        @pl.when(step == 0)
        def _():
            column = lax.broadcasted_iota(jnp.int32, (frames, rest_width), 1)
            value = jnp.where(column < rest, potential(noise_rest[...], labels_rest[...]), 0.0)
            out_b[:, third:] = value.astype(jnp.bfloat16)

    last = 3 * third // rest_width
    return pl.pallas_call(
        kernel,
        grid=(STEPS,),
        in_specs=[
            pl.BlockSpec((frames, tile), lambda i: (0, STEPS + i)),
            pl.BlockSpec((1, tile), lambda i: (0, STEPS + i)),
            pl.BlockSpec((frames, tile), lambda i: (0, 2 * STEPS + i)),
            pl.BlockSpec((1, tile), lambda i: (0, 2 * STEPS + i)),
            pl.BlockSpec((frames, rest_width), lambda i: (0, last)),
            pl.BlockSpec((1, rest_width), lambda i: (0, last)),
            pl.BlockSpec(volts.shape, lambda i: (0, 0)),
            pl.BlockSpec(memory_space=pl.ANY),
        ],
        out_specs=[pl.BlockSpec((frames, third + rest_width), lambda i: (0, 0)),
                   pl.BlockSpec((frames, tile), lambda i: (0, i))],
        out_shape=[jax.ShapeDtypeStruct((frames, third + rest_width), jnp.bfloat16),
                   jax.ShapeDtypeStruct((frames, third), jnp.bfloat16)],
        compiler_params=PARAMS,
        cost_estimate=SMALL,
    )(noise, labels, noise, labels, noise, labels, volts, token)


def route(place, whole, sources, to_right, to_left, start, width, tokens):
    tile = whole // STEPS
    count = len(sources)
    frames = ROWS

    def kernel(place_ref, *refs):
        outs = refs[count + len(tokens):]
        z = place_ref[0]
        for here in range(4):
            @pl.when(z == here)
            def _(here=here):
                for out, number in zip(outs, (to_right[here], to_left[here])):
                    if number is not None:
                        out[...] = refs[number][...]

    def spec(number):
        array, row, column = sources[number]
        last = (array.shape[1] - 1) // tile if column == 0 else column + STEPS - 1
        users = [here for here in range(4) if number in (to_right[here], to_left[here])]

        def index(i, s):
            used = sum((s[0] == here).astype(jnp.int32) for here in users)
            return row, jnp.minimum(column + start + i * used, last)

        return pl.BlockSpec((frames, tile), index)

    out_spec = pl.BlockSpec((frames, tile), lambda i, s: (0, i))
    return pl.pallas_call(
        kernel,
        grid_spec=pltpu.PrefetchScalarGridSpec(
            num_scalar_prefetch=1, grid=(pl.cdiv(width, tile),),
            in_specs=[spec(n) for n in range(count)] + [pl.BlockSpec(memory_space=pl.ANY)] * len(tokens),
            out_specs=[out_spec] * 2),
        out_shape=[jax.ShapeDtypeStruct((frames, width), jnp.bfloat16)] * 2,
        compiler_params=PARAMS,
        cost_estimate=SMALL,
    )(place, *[s[0] for s in sources], *tokens)


def absorb(place, whole, streams, work, sums_shape, sums, first=None, profile=None, tiles=(0, STEPS)):
    start, count = tiles
    tile = whole // STEPS
    names = list(streams)
    slab = streams["slab"][0]
    nrows, sites = slab.shape
    rest = sites - 3 * whole
    rest_width = rest + -rest % LANES
    long = [n for n in ("own", "r", "l") if n in names and streams[n][0].shape[1] % tile == rest_width] if first else []
    blocks, frames, width = sums_shape

    def kernel(place_ref, *refs):
        now = dict(zip(names, refs))
        refs = refs[len(names):]
        if sums is not None:
            sums_ref, refs = refs[0], refs[1:]
        if first:
            slab_rest, refs = refs[0], refs[1:]
            rests = dict(zip(long, refs))
            refs = refs[len(long):]
        if profile is None:
            acc, = refs
        else:
            profile_ref, outs, acc = refs[0], refs[1:-1], refs[-1]
        z, k = place_ref[0], place_ref[1]
        step = pl.program_id(0)

        def add(block, lane, value):
            acc[block, :, lane:lane + value.shape[1]] += value

        @pl.when(step == 0)
        def _():
            acc[...] = jnp.zeros(acc.shape, acc.dtype) if sums is None else sums_ref[...]
            if first:
                column = lax.broadcasted_iota(jnp.int32, (nrows, rest_width), 1)
                piece = jnp.where(column < rest, slab_rest[...].astype(jnp.float32), 0.0).astype(jnp.bfloat16)
                first(z, dict(rests, slab=piece), add)


        work(z, now, add)

        if profile is not None:
            @pl.when(step == count - 1)
            def _():
                weight = jnp.sum(profile_ref[...])
                lane = lax.broadcasted_iota(jnp.int32, (frames, LANES), 1)
                for turn, out in enumerate(outs):
                    out[...] = acc[k ^ turn]
                    middle = slice(LANES, 2 * LANES)
                    out[:, middle] = jnp.where(lane == FREE - 1 - LANES, weight, acc[k ^ turn, :, middle])

    def base(array):
        return 0 if array.shape[1] <= count * tile + rest_width else start

    def spec(array, needed, third):
        return pl.BlockSpec(
            (array.shape[0], tile),
            lambda i, s: (0, third(s[0]) * STEPS + jnp.where(needed(s[0]), base(array) + i, 0)))

    in_specs = [spec(*streams[n]) for n in names]
    operands = [streams[n][0] for n in names]
    if sums is not None:
        in_specs.append(pl.BlockSpec(sums_shape, lambda i, s: (0, 0, 0)))
        operands.append(sums)
    if first:
        in_specs.append(pl.BlockSpec((nrows, rest_width), lambda i, s: (0, 3 * whole // rest_width)))
        in_specs += [pl.BlockSpec((frames, rest_width), lambda i, s, n=streams[n][0].shape[1]: (0, n // rest_width - 1)) for n in long]
        operands += [slab] + [streams[n][0] for n in long]
    if profile is None:
        out_shape = jax.ShapeDtypeStruct(sums_shape, jnp.float32)
        out_specs = pl.BlockSpec(sums_shape, lambda i, s: (0, 0, 0))
        scratch = []
    else:
        in_specs.append(pl.BlockSpec(profile.shape, lambda i, s: (0, 0)))
        operands.append(profile)
        out_shape = [jax.ShapeDtypeStruct(sums_shape[1:], jnp.float32)] * blocks
        out_specs = [pl.BlockSpec(sums_shape[1:], lambda i, s: (0, 0))] * blocks
        scratch = [pltpu.VMEM(sums_shape, jnp.float32)]
    return pl.pallas_call(
        kernel,
        grid_spec=pltpu.PrefetchScalarGridSpec(
            num_scalar_prefetch=1, grid=(count,), in_specs=in_specs, out_specs=out_specs, scratch_shapes=scratch),
        out_shape=out_shape,
        compiler_params=PARAMS,
        cost_estimate=SMALL,
    )(place, *operands)


def line_plan(slab, noise, volts, labels, profile, sizes):
    wide, owners = sizes
    panels, rows, sites = slab.shape
    frames = noise.shape[0]
    nrows = panels * rows
    third = sites // 3 // LANES * LANES
    z = lax.axis_index("wide")
    k = lax.axis_index(SITES)
    place = jnp.stack([z, k]).astype(jnp.int32)
    slab = slab.reshape(nrows, sites)
    right = [(0, 1), (1, 2), (2, 3)]
    left = [(3, 2), (2, 1), (1, 0)]

    def send(pair):
        return lax.ppermute(pair[0], "wide", right), lax.ppermute(pair[1], "wide", left)

    def mirror(choice):
        swap = {0: 0, 1: 2, 2: 1, 3: 4, 4: 3}
        return [swap.get(c) for c in reversed(choice)]

    def routed(sources, choice, width, tokens, start=0):
        sources = [s if isinstance(s, tuple) else (s, 0, 0) for s in sources]
        pair = route(place, third, sources, choice, mirror(choice), start, width, tokens)
        return send(pair), pair[0]

    def spare(i):
        return (slab, i, 2 * STEPS)

    rest = sites - 3 * third
    long = third + rest + -rest % LANES
    own_a = potential_of(noise[:, :long], volts, labels[:long])
    r1 = send((own_a, own_a))
    own_b, own_c = later_potentials(noise, volts, labels, third, own_a)
    r2 = send((own_b, own_b))

    sums_shape = (wide, frames, WIDTH)

    def at(number):
        return lambda z: number

    def thirds(end, mid):
        return lambda z: jnp.where(is_mid(z), mid, end)

    def from_left(z):
        return z >= 1

    def from_right(z):
        return z <= 2

    def far(z, refs, name):
        return jnp.where(z < 2, refs[name + "l"][...], refs[name + "r"][...])

    def near(z, refs, name):
        return jnp.where(z < 2, refs[name + "r"][...], refs[name + "l"][...])

    def both(name, pair, right_needed=from_left, left_needed=from_right):
        return {name + "r": (pair[0], right_needed, at(0)), name + "l": (pair[1], left_needed, at(0))}

    def work1(z, refs, add):
        add(z, 0, dot(refs["own"][...], refs["slab"][...]))

        @pl.when(z >= 1)
        def _():
            add(z - 1, 0, dot(refs["r"][...], refs["slab"][...]))

        @pl.when(z <= 2)
        def _():
            add(z + 1, 0, dot(refs["l"][...], refs["slab"][...]))

    def work3(z, refs, add):
        add(z, 0, dot(refs["own"][...], refs["slab2"][...]))
        add((z + 2) % 4, 0, dot(far(z, refs, ""), refs["slab"][...]))

        @pl.when(is_mid(z))
        def _():
            add(jnp.where(z < 2, 0, 3), 0, dot(near(z, refs, ""), refs["slab2"][...]))

    def work4(z, refs, add):
        add((z + 2) % 4, 0, dot(far(z, refs, ""), refs["slab"][...]))

    def work5(z, refs, add):
        came = far(z, refs, "")
        add(3 - z, 0, dot(came, refs["slab"][...]))

        @pl.when(is_mid(z))
        def _():
            brought = jnp.concatenate([near(z, refs, "4"), near(z, refs, "")], axis=0)
            add(z, 2 * LANES, dot(refs["own"][...], brought))
            add(3 - z, 2 * LANES, dot(came, brought))

    def first4(z, refs, add):
        add((z + 2) % 4, 0, dot(far(z, refs, ""), refs["slab"]))

    def first6(z, refs, add):
        @pl.when(is_end(z))
        def _():
            add(3 - z, 0, dot(far(z, refs, ""), refs["slab"]))

    def work6(z, refs, add):
        came = far(z, refs, "")
        block = jnp.where(z < 2, 3, 0)
        add(block, 0, dot(came, refs["slab"][...]))

        @pl.when(is_mid(z))
        def _():
            newest = near(z, refs, "")
            brought = jnp.concatenate([near(z, refs, "4"), near(z, refs, "5"), newest], axis=0)
            add(block, 2 * LANES, dot(came, brought))
            both = dot(jnp.concatenate([refs["own"][...], far(z, refs, "5")], axis=0), newest)
            add(z, 3 * LANES, both[:frames])
            add(3 - z, 3 * LANES, both[frames:])

    def near_right(z):
        return z == 1

    def near_left(z):
        return z == 2

    r3, sent = routed([own_c, r1[0], r1[1]], [0, 1, 1, None], long, [])
    r4, sent = routed([spare(0), r2[0], r2[1]], [0, 1, 1, None], long, [sent])
    sums = absorb(
        place, third, dict(both("", r1), slab=(slab, always, at(0)), own=(own_a, always, at(0))), work1, sums_shape, None)
    sums = absorb(
        place, third, dict(both("", r2), slab=(slab, always, at(1)), own=(own_b, always, at(0))), work1, sums_shape, sums,
        first=work1)
    r5, sent = routed([spare(1), r3[0], r3[1], own_c, own_c], [0, 3, 1, None], long, [sent, sums])
    sums = absorb(
        place, third,
        dict(both("", r3), slab=(slab, always, at(0)), slab2=(slab, always, at(2)), own=(own_c, always, at(0))),
        work3, sums_shape, sums)
    tile = third // STEPS
    r6_sources, r6_choice = [spare(2), r3[0], r3[1], r4[0], r4[1]], [0, 1, 3, None]
    r6, sent = routed(r6_sources, r6_choice, third - tile, [sent, sums])
    r7, sent = routed(r6_sources, r6_choice, long - third + tile, [sent], STEPS - 1)
    sums = absorb(
        place, third, dict(both("", r4), slab=(slab, always, at(1))), work4, sums_shape, sums, first=first4)
    middle = dict(both("4", r4, near_right, near_left), own=(own_c, is_mid, at(0)))
    sums = absorb(place, third, dict(both("", r5), slab=(slab, always, thirds(0, 2)), **middle), work5, sums_shape, sums)
    middle.update(both("5", r5, is_mid, is_mid))
    sums = absorb(
        place, third, dict(both("", r6), slab=(slab, always, thirds(1, 2)), **middle), work6, sums_shape, sums,
        tiles=(0, STEPS - 1))
    messages = absorb(
        place, third, dict(both("", r7), slab=(slab, always, thirds(1, 2)), **middle), work6, sums_shape, sums,
        first=first6, profile=profile, tiles=(STEPS - 1, 1))

    summed = messages[0]
    for turn in range(1, owners):
        summed += lax.ppermute(messages[turn], SITES, [(i, i ^ turn) for i in range(owners)])
    half = WIDTH // 2
    frame_sum = jnp.sum(summed[:, :nrows], axis=1) + jnp.sum(summed[:, half:half + nrows], axis=1)
    lane = jnp.arange(half)
    mine, extra = (jnp.where(lane[None, :] == FREE, frame_sum[:, None], x) for x in (summed[:, :half], summed[:, half:]))
    def flip(turn):
        return [(a * owners + b, b * owners + (a ^ turn)) for a in range(wide) for b in range(owners)]

    mine, extra = lax.ppermute(mine, ALL, flip(0)), lax.ppermute(extra, ALL, flip(1))
    total = mine[:, FREE] + extra[:, FREE] + lax.ppermute(frame_sum, ALL, flip(2)) + lax.ppermute(frame_sum, ALL, flip(3))
    weight_sum = mine[:, FREE - 1]
    charges = (mine + extra)[:, :nrows].reshape(frames, panels, rows).transpose(1, 2, 0)
    return finish(charges, total, weight_sum, profile)


def solution(mesh):
    wide = mesh.shape["wide"]
    owners = mesh.shape["narrow"] * mesh.shape["sub"]
    plan = line_plan if wide == owners == 4 else gather_plan

    def local(slab, noise, volts, labels, profile):
        return plan(slab, noise, volts, labels, profile, (wide, owners))

    return jax.shard_map(
        local,
        mesh=mesh,
        in_specs=(
            P(None, "wide", ("narrow", "sub")),
            P(("grp", "wide"), ("narrow", "sub")),
            P(("grp", "wide"), None),
            P(("narrow", "sub")),
            P(None, ("narrow", "sub")),
        ),
        out_specs=P(None, ("narrow", "sub"), ("grp", "wide")),
        check_vma=False,
    )
```

```python
import jax
import jax.numpy as jnp
from jax import lax
from jax.experimental import pallas as pl
from jax.experimental.pallas import tpu as pltpu
from jax.sharding import PartitionSpec as P

SITES = ("narrow", "sub")
ALL = ("wide", "narrow", "sub")


def dot_t(a, b):
    return lax.dot_general(a, b, (((1,), (1,)), ((), ())), preferred_element_type=jnp.float32)


def potential_of(noise, volts, labels):
    value = volts[:, 0:1]
    for kind in range(1, volts.shape[1]):
        value = jnp.where(labels[None, :] == kind, volts[:, kind:kind + 1], value)
    return (value + noise.astype(jnp.float32)).astype(jnp.bfloat16)


def finish(charges, total, weight_sum, profile):
    return charges - profile[:, :, None] * (total / weight_sum)[None, None, :]


def gather_plan(slab, noise, volts, labels, profile, sizes):
    wide, owners = sizes
    panels, rows, _ = slab.shape
    frames = noise.shape[0]
    pot = lax.all_gather(potential_of(noise, volts, labels), "wide", axis=0, tiled=True)
    part = dot_t(slab.reshape(panels * rows, -1), pot).reshape(panels, rows, wide, frames)
    mine = lax.all_to_all(part, "wide", 2, 1, tiled=True).reshape(panels, wide * rows, frames)
    charges = lax.psum_scatter(mine, SITES, scatter_dimension=1, tiled=True)
    total, weight_sum = lax.psum((jnp.sum(charges, axis=(0, 1)), jnp.sum(profile)), SITES)
    return finish(charges, total, weight_sum, profile)


LANES = 128
STEPS = 4
ROWS = 64
WIDTH = 4 * LANES
FREE = LANES * 2 - 1
PARAMS = pltpu.CompilerParams(vmem_limit_bytes=16 * 1024 * 1024)
SMALL = pl.CostEstimate(flops=1000, bytes_accessed=1000, transcendentals=0)


def always(z):
    return z >= 0


def is_mid(z):
    return (z == 1) | (z == 2)


def is_end(z):
    return (z == 0) | (z == 3)


def dot(a, b):
    return lax.dot_general(a, b, (((1,), (1,)), ((), ())), preferred_element_type=jnp.float32)


def later_potentials(noise, volts, labels, third, token):
    frames, sites = noise.shape
    tile = third // STEPS
    rest = sites - 3 * third
    rest_width = rest + -rest % LANES
    labels = labels.reshape(1, sites)
    volts = volts.T

    def kernel(noise_b, labels_b, noise_c, labels_c, noise_rest, labels_rest, volts_ref, token_ref, out_b, out_c):
        diagonal = (lax.broadcasted_iota(jnp.int32, (frames, frames), 0)
                    == lax.broadcasted_iota(jnp.int32, (frames, frames), 1))
        columns = [jnp.sum(jnp.where(diagonal, volts_ref[kind:kind + 1, :], 0.0), axis=1, keepdims=True)
                   for kind in range(volts_ref.shape[0])]

        def potential(noise, labels):
            value = jnp.broadcast_to(columns[0], noise.shape)
            for kind in range(1, len(columns)):
                value = jnp.where(labels == kind, columns[kind], value)
            return value + noise.astype(jnp.float32)

        step = pl.program_id(0)
        at = pl.multiple_of(step * tile, LANES)
        out_b[:, pl.ds(at, tile)] = potential(noise_b[...], labels_b[...]).astype(jnp.bfloat16)
        out_c[...] = potential(noise_c[...], labels_c[...]).astype(jnp.bfloat16)

        @pl.when(step == 0)
        def _():
            column = lax.broadcasted_iota(jnp.int32, (frames, rest_width), 1)
            value = jnp.where(column < rest, potential(noise_rest[...], labels_rest[...]), 0.0)
            out_b[:, third:] = value.astype(jnp.bfloat16)

    last = 3 * third // rest_width
    return pl.pallas_call(
        kernel,
        grid=(STEPS,),
        in_specs=[
            pl.BlockSpec((frames, tile), lambda i: (0, STEPS + i)),
            pl.BlockSpec((1, tile), lambda i: (0, STEPS + i)),
            pl.BlockSpec((frames, tile), lambda i: (0, 2 * STEPS + i)),
            pl.BlockSpec((1, tile), lambda i: (0, 2 * STEPS + i)),
            pl.BlockSpec((frames, rest_width), lambda i: (0, last)),
            pl.BlockSpec((1, rest_width), lambda i: (0, last)),
            pl.BlockSpec(volts.shape, lambda i: (0, 0)),
            pl.BlockSpec(memory_space=pl.ANY),
        ],
        out_specs=[pl.BlockSpec((frames, third + rest_width), lambda i: (0, 0)),
                   pl.BlockSpec((frames, tile), lambda i: (0, i))],
        out_shape=[jax.ShapeDtypeStruct((frames, third + rest_width), jnp.bfloat16),
                   jax.ShapeDtypeStruct((frames, third), jnp.bfloat16)],
        compiler_params=PARAMS,
        cost_estimate=SMALL,
    )(noise, labels, noise, labels, noise, labels, volts, token)


def route(place, whole, sources, outer, inner, start, width, tokens):
    tile = whole // STEPS
    count = len(sources)

    def kernel(place_ref, *refs):
        out_x, out_y = refs[count + len(tokens):]
        z = place_ref[0]

        @pl.when(is_end(z))
        def _():
            out_x[...] = refs[outer[0]][...]

        @pl.when(is_mid(z))
        def _():
            out_x[...] = refs[outer[1]][...]
            out_y[...] = refs[inner][...]

    def spec(number):
        array, row, column = sources[number]
        last = (array.shape[1] - 1) // tile if column == 0 else column + STEPS - 1

        def index(i, s):
            used = is_end(s[0]) if number == outer[0] else is_mid(s[0])
            return row, jnp.where(used, jnp.minimum(column + start + i, last), column)

        return pl.BlockSpec((ROWS, tile), index)

    return pl.pallas_call(
        kernel,
        grid_spec=pltpu.PrefetchScalarGridSpec(
            num_scalar_prefetch=1, grid=(pl.cdiv(width, tile),),
            in_specs=[spec(n) for n in range(count)] + [pl.BlockSpec(memory_space=pl.ANY)] * len(tokens),
            out_specs=[pl.BlockSpec((ROWS, tile), lambda i, s: (0, i)),
                       pl.BlockSpec((ROWS, tile), lambda i, s: (0, jnp.where(is_mid(s[0]), i, 0)))]),
        out_shape=[jax.ShapeDtypeStruct((ROWS, width), jnp.bfloat16)] * 2,
        compiler_params=PARAMS,
        cost_estimate=SMALL,
    )(place, *[s[0] for s in sources], *tokens)


def absorb(place, whole, streams, work, sums_shape, sums, first=None, profile=None, tiles=(0, STEPS)):
    start, count = tiles
    tile = whole // STEPS
    names = list(streams)
    slab = streams["slab"][0]
    nrows, sites = slab.shape
    rest = sites - 3 * whole
    rest_width = rest + -rest % LANES
    long = [n for n in ("own", "x", "y") if n in names and streams[n][0].shape[1] % tile == rest_width] if first else []
    blocks, frames, width = sums_shape

    def kernel(place_ref, *refs):
        now = dict(zip(names, refs))
        refs = refs[len(names):]
        if sums is not None:
            sums_ref, refs = refs[0], refs[1:]
        if first:
            slab_rest, refs = refs[0], refs[1:]
            rests = dict(zip(long, refs))
            refs = refs[len(long):]
        if profile is None:
            acc, = refs
        else:
            profile_ref, outs, acc = refs[0], refs[1:-1], refs[-1]
        z, k = place_ref[0], place_ref[1]
        step = pl.program_id(0)

        def add(block, lane, value):
            acc[block, :, lane:lane + value.shape[1]] += value

        @pl.when(step == 0)
        def _():
            acc[...] = jnp.zeros(acc.shape, acc.dtype) if sums is None else sums_ref[...]
            if first:
                column = lax.broadcasted_iota(jnp.int32, (nrows, rest_width), 1)
                piece = jnp.where(column < rest, slab_rest[...].astype(jnp.float32), 0.0).astype(jnp.bfloat16)
                first(z, dict(rests, slab=piece), add)


        work(z, now, add)

        if profile is not None:
            @pl.when(step == count - 1)
            def _():
                weight = jnp.sum(profile_ref[...])
                lane = lax.broadcasted_iota(jnp.int32, (frames, LANES), 1)
                for turn, out in enumerate(outs):
                    out[...] = acc[k ^ turn]
                    middle = slice(LANES, 2 * LANES)
                    out[:, middle] = jnp.where(lane == FREE - 1 - LANES, weight, acc[k ^ turn, :, middle])

    def base(array):
        return 0 if array.shape[1] <= count * tile + rest_width else start

    def spec(array, needed, third):
        return pl.BlockSpec(
            (array.shape[0], tile),
            lambda i, s: (0, third(s[0]) * STEPS + jnp.where(needed(s[0]), base(array) + i, 0)))

    in_specs = [spec(*streams[n]) for n in names]
    operands = [streams[n][0] for n in names]
    if sums is not None:
        in_specs.append(pl.BlockSpec(sums_shape, lambda i, s: (0, 0, 0)))
        operands.append(sums)
    if first:
        in_specs.append(pl.BlockSpec((nrows, rest_width), lambda i, s: (0, 3 * whole // rest_width)))
        in_specs += [pl.BlockSpec((frames, rest_width), lambda i, s, n=streams[n][0].shape[1]: (0, n // rest_width - 1)) for n in long]
        operands += [slab] + [streams[n][0] for n in long]
    if profile is None:
        out_shape = jax.ShapeDtypeStruct(sums_shape, jnp.float32)
        out_specs = pl.BlockSpec(sums_shape, lambda i, s: (0, 0, 0))
        scratch = []
    else:
        in_specs.append(pl.BlockSpec(profile.shape, lambda i, s: (0, 0)))
        operands.append(profile)
        out_shape = [jax.ShapeDtypeStruct(sums_shape[1:], jnp.float32)] * blocks
        out_specs = [pl.BlockSpec(sums_shape[1:], lambda i, s: (0, 0))] * blocks
        scratch = [pltpu.VMEM(sums_shape, jnp.float32)]
    return pl.pallas_call(
        kernel,
        grid_spec=pltpu.PrefetchScalarGridSpec(
            num_scalar_prefetch=1, grid=(count,), in_specs=in_specs, out_specs=out_specs, scratch_shapes=scratch),
        out_shape=out_shape,
        compiler_params=PARAMS,
        cost_estimate=SMALL,
    )(place, *operands)


def line_plan(slab, noise, volts, labels, profile, sizes):
    wide, owners = sizes
    panels, rows, sites = slab.shape
    frames = noise.shape[0]
    nrows = panels * rows
    third = sites // 3 // LANES * LANES
    z = lax.axis_index("wide")
    k = lax.axis_index(SITES)
    place = jnp.stack([z, k]).astype(jnp.int32)
    slab = slab.reshape(nrows, sites)
    outer = [(0, 1), (1, 0), (2, 3), (3, 2)]
    inner = [(1, 2), (2, 1)]

    def send(pair):
        return lax.ppermute(pair[0], "wide", outer), lax.ppermute(pair[1], "wide", inner)

    def routed(sources, to_outer, to_inner, width, tokens, start=0):
        sources = [s if isinstance(s, tuple) else (s, 0, 0) for s in sources]
        pair = route(place, third, sources, to_outer, to_inner, start, width, tokens)
        return send(pair), pair[0]

    def spare(i):
        return (slab, i, 2 * STEPS)

    rest = sites - 3 * third
    long = third + rest + -rest % LANES
    own_a = potential_of(noise[:, :long], volts, labels[:long])
    r1 = send((own_a, own_a))
    own_b, own_c = later_potentials(noise, volts, labels, third, own_a)
    r2 = send((own_b, own_b))

    sums_shape = (wide, frames, WIDTH)

    def at(number):
        return lambda z: number

    def thirds(end, mid):
        return lambda z: jnp.where(is_mid(z), mid, end)

    def far(z, refs, name):
        return jnp.where(is_end(z), refs[name + "x"][...], refs[name + "y"][...])

    def both(name, pair, x_needed=always):
        return {name + "x": (pair[0], x_needed, at(0)), name + "y": (pair[1], is_mid, at(0))}

    def work1(z, refs, add):
        add(z, 0, dot(refs["own"][...], refs["slab"][...]))
        add(z ^ 1, 0, dot(refs["x"][...], refs["slab"][...]))

        @pl.when(is_mid(z))
        def _():
            add(3 - z, 0, dot(refs["y"][...], refs["slab"][...]))

    def work3(z, refs, add):
        add(z, 0, dot(refs["own"][...], refs["slab2"][...]))
        add((z + 2) % 4, 0, dot(far(z, refs, ""), refs["slab"][...]))

        @pl.when(is_mid(z))
        def _():
            add(z ^ 1, 0, dot(refs["x"][...], refs["slab2"][...]))

    def work4(z, refs, add):
        add((z + 2) % 4, 0, dot(far(z, refs, ""), refs["slab"][...]))

    def work5(z, refs, add):
        came = far(z, refs, "")
        add(3 - z, 0, dot(came, refs["slab"][...]))

        @pl.when(is_mid(z))
        def _():
            brought = jnp.concatenate([refs["4"][...], refs["x"][...]], axis=0)
            add(z, 2 * LANES, dot(refs["own"][...], brought))
            add(3 - z, 2 * LANES, dot(came, brought))

    def first4(z, refs, add):
        add((z + 2) % 4, 0, dot(far(z, refs, ""), refs["slab"]))

    def first6(z, refs, add):
        @pl.when(is_end(z))
        def _():
            add(3 - z, 0, dot(far(z, refs, ""), refs["slab"]))

    def work6(z, refs, add):
        came = far(z, refs, "")
        block = jnp.where(z < 2, 3, 0)
        add(block, 0, dot(came, refs["slab"][...]))

        @pl.when(is_mid(z))
        def _():
            newest = refs["x"][...]
            brought = jnp.concatenate([refs["4"][...], refs["5x"][...], newest], axis=0)
            add(block, 2 * LANES, dot(came, brought))
            both = dot(jnp.concatenate([refs["own"][...], refs["5y"][...]], axis=0), newest)
            add(z, 3 * LANES, both[:frames])
            add(3 - z, 3 * LANES, both[frames:])

    r3, sent = routed([own_c, r1[1], r1[0]], (0, 1), 2, long, [])
    r4, sent = routed([spare(0), r2[1], r2[0]], (0, 1), 2, long, [sent])
    sums = absorb(
        place, third, dict(both("", r1), slab=(slab, always, at(0)), own=(own_a, always, at(0))), work1, sums_shape, None)
    sums = absorb(
        place, third, dict(both("", r2), slab=(slab, always, at(1)), own=(own_b, always, at(0))), work1, sums_shape, sums,
        first=work1)
    r5, sent = routed([spare(1), r3[1], own_c], (0, 1), 2, long, [sent, sums])
    sums = absorb(
        place, third,
        dict(both("", r3), slab=(slab, always, at(0)), slab2=(slab, always, at(2)), own=(own_c, always, at(0))),
        work3, sums_shape, sums)
    tile = third // STEPS
    r6_sources = [spare(2), r4[1], r3[0]]
    r6, sent = routed(r6_sources, (0, 1), 2, third - tile, [sent, sums])
    r7, sent = routed(r6_sources, (0, 1), 2, long - third + tile, [sent], STEPS - 1)
    sums = absorb(
        place, third, dict(both("", r4), slab=(slab, always, at(1))), work4, sums_shape, sums, first=first4)
    middle = {"4": (r4[0], is_mid, at(0)), "own": (own_c, is_mid, at(0))}
    sums = absorb(place, third, dict(both("", r5), slab=(slab, always, thirds(0, 2)), **middle), work5, sums_shape, sums)
    middle.update(both("5", r5, is_mid))
    sums = absorb(
        place, third, dict(both("", r6), slab=(slab, always, thirds(1, 2)), **middle), work6, sums_shape, sums,
        tiles=(0, STEPS - 1))
    messages = absorb(
        place, third, dict(both("", r7), slab=(slab, always, thirds(1, 2)), **middle), work6, sums_shape, sums,
        first=first6, profile=profile, tiles=(STEPS - 1, 1))

    summed = messages[0]
    for turn in range(1, owners):
        summed += lax.ppermute(messages[turn], SITES, [(i, i ^ turn) for i in range(owners)])
    half = WIDTH // 2
    frame_sum = jnp.sum(summed[:, :nrows], axis=1) + jnp.sum(summed[:, half:half + nrows], axis=1)
    lane = jnp.arange(half)
    mine, extra = (jnp.where(lane[None, :] == FREE, frame_sum[:, None], x) for x in (summed[:, :half], summed[:, half:]))
    def flip(turn):
        return [(a * owners + b, b * owners + (a ^ turn)) for a in range(wide) for b in range(owners)]

    mine, extra = lax.ppermute(mine, ALL, flip(0)), lax.ppermute(extra, ALL, flip(1))
    total = mine[:, FREE] + extra[:, FREE] + lax.ppermute(frame_sum, ALL, flip(2)) + lax.ppermute(frame_sum, ALL, flip(3))
    weight_sum = mine[:, FREE - 1]
    charges = (mine + extra)[:, :nrows].reshape(frames, panels, rows).transpose(1, 2, 0)
    return finish(charges, total, weight_sum, profile)


def solution(mesh):
    wide = mesh.shape["wide"]
    owners = mesh.shape["narrow"] * mesh.shape["sub"]
    plan = line_plan if wide == owners == 4 else gather_plan

    def local(slab, noise, volts, labels, profile):
        return plan(slab, noise, volts, labels, profile, (wide, owners))

    return jax.shard_map(
        local,
        mesh=mesh,
        in_specs=(
            P(None, "wide", ("narrow", "sub")),
            P(("grp", "wide"), ("narrow", "sub")),
            P(("grp", "wide"), None),
            P(("narrow", "sub")),
            P(None, ("narrow", "sub")),
        ),
        out_specs=P(None, ("narrow", "sub"), ("grp", "wide")),
        check_vma=False,
    )
```

```python
import jax
import jax.numpy as jnp
from jax import lax
from jax.experimental import pallas as pl
from jax.experimental.pallas import tpu as pltpu
from jax.sharding import PartitionSpec as P

SITES = ("narrow", "sub")
ALL = ("wide", "narrow", "sub")


def dot_t(a, b):
    return lax.dot_general(a, b, (((1,), (1,)), ((), ())), preferred_element_type=jnp.float32)


def potential_of(noise, volts, labels):
    value = volts[:, 0:1]
    for kind in range(1, volts.shape[1]):
        value = jnp.where(labels[None, :] == kind, volts[:, kind:kind + 1], value)
    return (value + noise.astype(jnp.float32)).astype(jnp.bfloat16)


def finish(charges, total, weight_sum, profile):
    return charges - profile[:, :, None] * (total / weight_sum)[None, None, :]


def gather_plan(slab, noise, volts, labels, profile, sizes):
    wide, owners = sizes
    panels, rows, _ = slab.shape
    frames = noise.shape[0]
    pot = lax.all_gather(potential_of(noise, volts, labels), "wide", axis=0, tiled=True)
    part = dot_t(slab.reshape(panels * rows, -1), pot).reshape(panels, rows, wide, frames)
    mine = lax.all_to_all(part, "wide", 2, 1, tiled=True).reshape(panels, wide * rows, frames)
    charges = lax.psum_scatter(mine, SITES, scatter_dimension=1, tiled=True)
    total, weight_sum = lax.psum((jnp.sum(charges, axis=(0, 1)), jnp.sum(profile)), SITES)
    return finish(charges, total, weight_sum, profile)


LANES = 128
STEPS = 4
ROWS = 64
WIDTH = 4 * LANES
FREE = LANES * 2 - 1
PARAMS = pltpu.CompilerParams(vmem_limit_bytes=16 * 1024 * 1024)
SMALL = pl.CostEstimate(flops=1000, bytes_accessed=1000, transcendentals=0)


def always(z):
    return z >= 0


def is_mid(z):
    return (z == 1) | (z == 2)


def is_end(z):
    return (z == 0) | (z == 3)


def dot(a, b):
    return lax.dot_general(a, b, (((1,), (1,)), ((), ())), preferred_element_type=jnp.float32)


def later_potentials(noise, volts, labels, third, token):
    frames, sites = noise.shape
    tile = third // STEPS
    rest = sites - 3 * third
    rest_width = rest + -rest % LANES
    labels = labels.reshape(1, sites)
    volts = volts.T

    def kernel(noise_b, labels_b, noise_c, labels_c, noise_rest, labels_rest, volts_ref, token_ref, out_b, out_c):
        diagonal = (lax.broadcasted_iota(jnp.int32, (frames, frames), 0)
                    == lax.broadcasted_iota(jnp.int32, (frames, frames), 1))
        columns = [jnp.sum(jnp.where(diagonal, volts_ref[kind:kind + 1, :], 0.0), axis=1, keepdims=True)
                   for kind in range(volts_ref.shape[0])]

        def potential(noise, labels):
            value = jnp.broadcast_to(columns[0], noise.shape)
            for kind in range(1, len(columns)):
                value = jnp.where(labels == kind, columns[kind], value)
            return value + noise.astype(jnp.float32)

        step = pl.program_id(0)
        at = pl.multiple_of(step * tile, LANES)
        out_b[:, pl.ds(at, tile)] = potential(noise_b[...], labels_b[...]).astype(jnp.bfloat16)
        out_c[...] = potential(noise_c[...], labels_c[...]).astype(jnp.bfloat16)

        @pl.when(step == 0)
        def _():
            column = lax.broadcasted_iota(jnp.int32, (frames, rest_width), 1)
            value = jnp.where(column < rest, potential(noise_rest[...], labels_rest[...]), 0.0)
            out_b[:, third:] = value.astype(jnp.bfloat16)

    last = 3 * third // rest_width
    return pl.pallas_call(
        kernel,
        grid=(STEPS,),
        in_specs=[
            pl.BlockSpec((frames, tile), lambda i: (0, STEPS + i)),
            pl.BlockSpec((1, tile), lambda i: (0, STEPS + i)),
            pl.BlockSpec((frames, tile), lambda i: (0, 2 * STEPS + i)),
            pl.BlockSpec((1, tile), lambda i: (0, 2 * STEPS + i)),
            pl.BlockSpec((frames, rest_width), lambda i: (0, last)),
            pl.BlockSpec((1, rest_width), lambda i: (0, last)),
            pl.BlockSpec(volts.shape, lambda i: (0, 0)),
            pl.BlockSpec(memory_space=pl.ANY),
        ],
        out_specs=[pl.BlockSpec((frames, third + rest_width), lambda i: (0, 0)),
                   pl.BlockSpec((frames, tile), lambda i: (0, i))],
        out_shape=[jax.ShapeDtypeStruct((frames, third + rest_width), jnp.bfloat16),
                   jax.ShapeDtypeStruct((frames, third), jnp.bfloat16)],
        compiler_params=PARAMS,
        cost_estimate=SMALL,
    )(noise, labels, noise, labels, noise, labels, volts, token)


def route(place, whole, sources, outer, inner, start, width, tokens):
    tile = whole // STEPS
    count = len(sources)

    def kernel(place_ref, *refs):
        out_x, out_y = refs[count + len(tokens):]
        z = place_ref[0]

        @pl.when(is_end(z))
        def _():
            out_x[...] = refs[outer[0]][...]

        @pl.when(is_mid(z))
        def _():
            out_x[...] = refs[outer[1]][...]
            out_y[...] = refs[inner][...]

    def spec(number):
        array, row, column = sources[number]
        last = (array.shape[1] - 1) // tile if column == 0 else column + STEPS - 1

        def index(i, s):
            used = is_end(s[0]) if number == outer[0] else is_mid(s[0])
            return row, jnp.where(used, jnp.minimum(column + start + i, last), column)

        return pl.BlockSpec((ROWS, tile), index)

    return pl.pallas_call(
        kernel,
        grid_spec=pltpu.PrefetchScalarGridSpec(
            num_scalar_prefetch=1, grid=(pl.cdiv(width, tile),),
            in_specs=[spec(n) for n in range(count)] + [pl.BlockSpec(memory_space=pl.ANY)] * len(tokens),
            out_specs=[pl.BlockSpec((ROWS, tile), lambda i, s: (0, i)),
                       pl.BlockSpec((ROWS, tile), lambda i, s: (0, jnp.where(is_mid(s[0]), i, 0)))]),
        out_shape=[jax.ShapeDtypeStruct((ROWS, width), jnp.bfloat16)] * 2,
        compiler_params=PARAMS,
        cost_estimate=SMALL,
    )(place, *[s[0] for s in sources], *tokens)


def absorb(place, whole, streams, work, sums_shape, sums, first=None, profile=None, tiles=(0, STEPS)):
    start, count = tiles
    tile = whole // STEPS
    names = list(streams)
    slab = streams["slab"][0]
    nrows, sites = slab.shape
    rest = sites - 3 * whole
    rest_width = rest + -rest % LANES
    long = [n for n in ("own", "x", "y") if n in names and streams[n][0].shape[1] % tile == rest_width] if first else []
    blocks, frames, width = sums_shape

    def kernel(place_ref, *refs):
        now = dict(zip(names, refs))
        refs = refs[len(names):]
        if sums is not None:
            sums_ref, refs = refs[0], refs[1:]
        if first:
            slab_rest, refs = refs[0], refs[1:]
            rests = dict(zip(long, refs))
            refs = refs[len(long):]
        if profile is None:
            acc, = refs
        else:
            profile_ref, outs, acc = refs[0], refs[1:-1], refs[-1]
        z, k = place_ref[0], place_ref[1]
        step = pl.program_id(0)

        def add(block, lane, value):
            acc[block, :, lane:lane + value.shape[1]] += value

        @pl.when(step == 0)
        def _():
            acc[...] = jnp.zeros(acc.shape, acc.dtype) if sums is None else sums_ref[...]
            if first:
                column = lax.broadcasted_iota(jnp.int32, (nrows, rest_width), 1)
                piece = jnp.where(column < rest, slab_rest[...].astype(jnp.float32), 0.0).astype(jnp.bfloat16)
                first(z, dict(rests, slab=piece), add)


        work(z, now, add)

        if profile is not None:
            @pl.when(step == count - 1)
            def _():
                weight = jnp.sum(profile_ref[...])
                lane = lax.broadcasted_iota(jnp.int32, (frames, LANES), 1)
                for turn, out in enumerate(outs):
                    out[...] = acc[k ^ turn]
                    middle = slice(LANES, 2 * LANES)
                    out[:, middle] = jnp.where(lane == FREE - 1 - LANES, weight, acc[k ^ turn, :, middle])

    def base(array):
        return 0 if array.shape[1] <= count * tile + rest_width else start

    def spec(array, needed, third):
        return pl.BlockSpec(
            (array.shape[0], tile),
            lambda i, s: (0, third(s[0]) * STEPS + jnp.where(needed(s[0]), base(array) + i, 0)))

    in_specs = [spec(*streams[n]) for n in names]
    operands = [streams[n][0] for n in names]
    if sums is not None:
        in_specs.append(pl.BlockSpec(sums_shape, lambda i, s: (0, 0, 0)))
        operands.append(sums)
    if first:
        in_specs.append(pl.BlockSpec((nrows, rest_width), lambda i, s: (0, 3 * whole // rest_width)))
        in_specs += [pl.BlockSpec((frames, rest_width), lambda i, s, n=streams[n][0].shape[1]: (0, n // rest_width - 1)) for n in long]
        operands += [slab] + [streams[n][0] for n in long]
    if profile is None:
        out_shape = jax.ShapeDtypeStruct(sums_shape, jnp.float32)
        out_specs = pl.BlockSpec(sums_shape, lambda i, s: (0, 0, 0))
        scratch = []
    else:
        in_specs.append(pl.BlockSpec(profile.shape, lambda i, s: (0, 0)))
        operands.append(profile)
        out_shape = [jax.ShapeDtypeStruct(sums_shape[1:], jnp.float32)] * blocks
        out_specs = [pl.BlockSpec(sums_shape[1:], lambda i, s: (0, 0))] * blocks
        scratch = [pltpu.VMEM(sums_shape, jnp.float32)]
    return pl.pallas_call(
        kernel,
        grid_spec=pltpu.PrefetchScalarGridSpec(
            num_scalar_prefetch=1, grid=(count,), in_specs=in_specs, out_specs=out_specs, scratch_shapes=scratch),
        out_shape=out_shape,
        compiler_params=PARAMS,
        cost_estimate=SMALL,
    )(place, *operands)


def line_plan(slab, noise, volts, labels, profile, sizes):
    wide, owners = sizes
    panels, rows, sites = slab.shape
    frames = noise.shape[0]
    nrows = panels * rows
    third = sites // 3 // LANES * LANES
    z = lax.axis_index("wide")
    k = lax.axis_index(SITES)
    place = jnp.stack([z, k]).astype(jnp.int32)
    slab = slab.reshape(nrows, sites)
    outer = [(0, 1), (1, 0), (2, 3), (3, 2)]
    inner = [(1, 2), (2, 1)]

    def send(pair):
        y = lax.ppermute(pair[1], "wide", inner)
        return lax.ppermute(pair[0], "wide", outer), y

    def routed(sources, to_outer, to_inner, width, tokens, start=0):
        sources = [s if isinstance(s, tuple) else (s, 0, 0) for s in sources]
        pair = route(place, third, sources, to_outer, to_inner, start, width, tokens)
        return send(pair), pair[0]

    def spare(i):
        return (slab, i, 2 * STEPS)

    rest = sites - 3 * third
    long = third + rest + -rest % LANES
    own_a = potential_of(noise[:, :long], volts, labels[:long])
    r1 = send((own_a, own_a))
    own_b, own_c = later_potentials(noise, volts, labels, third, own_a)
    r2 = send((own_b, own_b))

    sums_shape = (wide, frames, WIDTH)

    def at(number):
        return lambda z: number

    def thirds(end, mid):
        return lambda z: jnp.where(is_mid(z), mid, end)

    def far(z, refs, name):
        return jnp.where(is_end(z), refs[name + "x"][...], refs[name + "y"][...])

    def both(name, pair, x_needed=always):
        return {name + "x": (pair[0], x_needed, at(0)), name + "y": (pair[1], is_mid, at(0))}

    def work1(z, refs, add):
        add(z, 0, dot(refs["own"][...], refs["slab"][...]))
        add(z ^ 1, 0, dot(refs["x"][...], refs["slab"][...]))

        @pl.when(is_mid(z))
        def _():
            add(3 - z, 0, dot(refs["y"][...], refs["slab"][...]))

    def work3(z, refs, add):
        add(z, 0, dot(refs["own"][...], refs["slab2"][...]))
        add((z + 2) % 4, 0, dot(far(z, refs, ""), refs["slab"][...]))

        @pl.when(is_mid(z))
        def _():
            add(z ^ 1, 0, dot(refs["x"][...], refs["slab2"][...]))

    def work4(z, refs, add):
        add((z + 2) % 4, 0, dot(far(z, refs, ""), refs["slab"][...]))

    def work5(z, refs, add):
        came = far(z, refs, "")
        add(3 - z, 0, dot(came, refs["slab"][...]))

        @pl.when(is_mid(z))
        def _():
            brought = jnp.concatenate([refs["4"][...], refs["x"][...]], axis=0)
            add(z, 2 * LANES, dot(refs["own"][...], brought))
            add(3 - z, 2 * LANES, dot(came, brought))

    def first4(z, refs, add):
        add((z + 2) % 4, 0, dot(far(z, refs, ""), refs["slab"]))

    def first6(z, refs, add):
        @pl.when(is_end(z))
        def _():
            add(3 - z, 0, dot(far(z, refs, ""), refs["slab"]))

    def work6(z, refs, add):
        came = far(z, refs, "")
        block = jnp.where(z < 2, 3, 0)
        add(block, 0, dot(came, refs["slab"][...]))

        @pl.when(is_mid(z))
        def _():
            newest = refs["x"][...]
            brought = jnp.concatenate([refs["4"][...], refs["5x"][...], newest], axis=0)
            add(block, 2 * LANES, dot(came, brought))
            both = dot(jnp.concatenate([refs["own"][...], refs["5y"][...]], axis=0), newest)
            add(z, 3 * LANES, both[:frames])
            add(3 - z, 3 * LANES, both[frames:])

    r3, sent = routed([own_c, r1[0], r1[1]], (0, 2), 1, long, [])
    r4, sent = routed([spare(0), r2[0], r2[1]], (0, 2), 1, long, [sent])
    sums = absorb(
        place, third, dict(both("", r1), slab=(slab, always, at(0)), own=(own_a, always, at(0))), work1, sums_shape, None)
    sums = absorb(
        place, third, dict(both("", r2), slab=(slab, always, at(1)), own=(own_b, always, at(0))), work1, sums_shape, sums,
        first=work1)
    r5, sent = routed([spare(1), r3[1], own_c], (0, 1), 2, long, [sent, sums])
    sums = absorb(
        place, third,
        dict(both("", r3), slab=(slab, always, at(0)), slab2=(slab, always, at(2)), own=(own_c, always, at(0))),
        work3, sums_shape, sums)
    tile = third // STEPS
    r6_sources = [spare(2), r4[1], r3[0]]
    r6, sent = routed(r6_sources, (0, 1), 2, third - tile, [sent, sums])
    r7, sent = routed(r6_sources, (0, 1), 2, long - third + tile, [sent], STEPS - 1)
    sums = absorb(
        place, third, dict(both("", r4), slab=(slab, always, at(1))), work4, sums_shape, sums, first=first4)
    middle = {"4": (r4[0], is_mid, at(0)), "own": (own_c, is_mid, at(0))}
    sums = absorb(place, third, dict(both("", r5), slab=(slab, always, thirds(0, 2)), **middle), work5, sums_shape, sums)
    middle.update(both("5", r5, is_mid))
    sums = absorb(
        place, third, dict(both("", r6), slab=(slab, always, thirds(1, 2)), **middle), work6, sums_shape, sums,
        tiles=(0, STEPS - 1))
    messages = absorb(
        place, third, dict(both("", r7), slab=(slab, always, thirds(1, 2)), **middle), work6, sums_shape, sums,
        first=first6, profile=profile, tiles=(STEPS - 1, 1))

    summed = messages[0]
    for turn in range(1, owners):
        summed += lax.ppermute(messages[turn], SITES, [(i, i ^ turn) for i in range(owners)])
    half = WIDTH // 2
    frame_sum = jnp.sum(summed[:, :nrows], axis=1) + jnp.sum(summed[:, half:half + nrows], axis=1)
    lane = jnp.arange(half)
    mine, extra = (jnp.where(lane[None, :] == FREE, frame_sum[:, None], x) for x in (summed[:, :half], summed[:, half:]))
    def flip(turn):
        return [(a * owners + b, b * owners + (a ^ turn)) for a in range(wide) for b in range(owners)]

    mine, extra = lax.ppermute(mine, ALL, flip(0)), lax.ppermute(extra, ALL, flip(1))
    total = mine[:, FREE] + extra[:, FREE]
    total += lax.ppermute(total, SITES, [(i, i ^ 2) for i in range(owners)])
    weight_sum = mine[:, FREE - 1]
    charges = (mine + extra)[:, :nrows].reshape(frames, panels, rows).transpose(1, 2, 0)
    return finish(charges, total, weight_sum, profile)


def solution(mesh):
    wide = mesh.shape["wide"]
    owners = mesh.shape["narrow"] * mesh.shape["sub"]
    plan = line_plan if wide == owners == 4 else gather_plan

    def local(slab, noise, volts, labels, profile):
        return plan(slab, noise, volts, labels, profile, (wide, owners))

    return jax.shard_map(
        local,
        mesh=mesh,
        in_specs=(
            P(None, "wide", ("narrow", "sub")),
            P(("grp", "wide"), ("narrow", "sub")),
            P(("grp", "wide"), None),
            P(("narrow", "sub")),
            P(None, ("narrow", "sub")),
        ),
        out_specs=P(None, ("narrow", "sub"), ("grp", "wide")),
        check_vma=False,
    )
```

```python
import jax
import jax.numpy as jnp
from jax import lax
from jax.experimental import pallas as pl
from jax.experimental.pallas import tpu as pltpu
from jax.sharding import PartitionSpec as P

SITES = ("narrow", "sub")
ALL = ("wide", "narrow", "sub")


def dot_t(a, b):
    return lax.dot_general(a, b, (((1,), (1,)), ((), ())), preferred_element_type=jnp.float32)


def potential_of(noise, volts, labels):
    value = volts[:, 0:1]
    for kind in range(1, volts.shape[1]):
        value = jnp.where(labels[None, :] == kind, volts[:, kind:kind + 1], value)
    return (value + noise.astype(jnp.float32)).astype(jnp.bfloat16)


def finish(charges, total, weight_sum, profile):
    return charges - profile[:, :, None] * (total / weight_sum)[None, None, :]


def gather_plan(slab, noise, volts, labels, profile, sizes):
    wide, owners = sizes
    panels, rows, _ = slab.shape
    frames = noise.shape[0]
    pot = lax.all_gather(potential_of(noise, volts, labels), "wide", axis=0, tiled=True)
    part = dot_t(slab.reshape(panels * rows, -1), pot).reshape(panels, rows, wide, frames)
    mine = lax.all_to_all(part, "wide", 2, 1, tiled=True).reshape(panels, wide * rows, frames)
    charges = lax.psum_scatter(mine, SITES, scatter_dimension=1, tiled=True)
    total, weight_sum = lax.psum((jnp.sum(charges, axis=(0, 1)), jnp.sum(profile)), SITES)
    return finish(charges, total, weight_sum, profile)


LANES = 128
STEPS = 4
ROWS = 64
WIDTH = 4 * LANES
FREE = LANES * 2 - 1
PARAMS = pltpu.CompilerParams(vmem_limit_bytes=16 * 1024 * 1024)
SMALL = pl.CostEstimate(flops=1000, bytes_accessed=1000, transcendentals=0)


def always(z):
    return z >= 0


def is_mid(z):
    return (z == 1) | (z == 2)


def is_end(z):
    return (z == 0) | (z == 3)


def dot(a, b):
    return lax.dot_general(a, b, (((1,), (1,)), ((), ())), preferred_element_type=jnp.float32)


def later_potentials(noise, volts, labels, third, token):
    frames, sites = noise.shape
    tile = third // STEPS
    rest = sites - 3 * third
    rest_width = rest + -rest % LANES
    labels = labels.reshape(1, sites)
    volts = volts.T

    def kernel(noise_b, labels_b, noise_c, labels_c, noise_rest, labels_rest, volts_ref, token_ref, out_b, out_c):
        diagonal = (lax.broadcasted_iota(jnp.int32, (frames, frames), 0)
                    == lax.broadcasted_iota(jnp.int32, (frames, frames), 1))
        columns = [jnp.sum(jnp.where(diagonal, volts_ref[kind:kind + 1, :], 0.0), axis=1, keepdims=True)
                   for kind in range(volts_ref.shape[0])]

        def potential(noise, labels):
            value = jnp.broadcast_to(columns[0], noise.shape)
            for kind in range(1, len(columns)):
                value = jnp.where(labels == kind, columns[kind], value)
            return value + noise.astype(jnp.float32)

        step = pl.program_id(0)
        at = pl.multiple_of(step * tile, LANES)
        out_b[:, pl.ds(at, tile)] = potential(noise_b[...], labels_b[...]).astype(jnp.bfloat16)
        out_c[...] = potential(noise_c[...], labels_c[...]).astype(jnp.bfloat16)

        @pl.when(step == 0)
        def _():
            column = lax.broadcasted_iota(jnp.int32, (frames, rest_width), 1)
            value = jnp.where(column < rest, potential(noise_rest[...], labels_rest[...]), 0.0)
            out_b[:, third:] = value.astype(jnp.bfloat16)

    last = 3 * third // rest_width
    return pl.pallas_call(
        kernel,
        grid=(STEPS,),
        in_specs=[
            pl.BlockSpec((frames, tile), lambda i: (0, STEPS + i)),
            pl.BlockSpec((1, tile), lambda i: (0, STEPS + i)),
            pl.BlockSpec((frames, tile), lambda i: (0, 2 * STEPS + i)),
            pl.BlockSpec((1, tile), lambda i: (0, 2 * STEPS + i)),
            pl.BlockSpec((frames, rest_width), lambda i: (0, last)),
            pl.BlockSpec((1, rest_width), lambda i: (0, last)),
            pl.BlockSpec(volts.shape, lambda i: (0, 0)),
            pl.BlockSpec(memory_space=pl.ANY),
        ],
        out_specs=[pl.BlockSpec((frames, third + rest_width), lambda i: (0, 0)),
                   pl.BlockSpec((frames, tile), lambda i: (0, i))],
        out_shape=[jax.ShapeDtypeStruct((frames, third + rest_width), jnp.bfloat16),
                   jax.ShapeDtypeStruct((frames, third), jnp.bfloat16)],
        compiler_params=PARAMS,
        cost_estimate=SMALL,
    )(noise, labels, noise, labels, noise, labels, volts, token)


def route(place, whole, sources, outer, inner, start, width, tokens):
    tile = whole // STEPS
    count = len(sources)

    def kernel(place_ref, *refs):
        out_x, out_y = refs[count + len(tokens):]
        z = place_ref[0]

        @pl.when(is_end(z))
        def _():
            out_x[...] = refs[outer[0]][...]

        @pl.when(is_mid(z))
        def _():
            out_x[...] = refs[outer[1]][...]
            out_y[...] = refs[inner][...]

    def spec(number):
        array, row, column = sources[number]
        last = (array.shape[1] - 1) // tile if column == 0 else column + STEPS - 1

        def index(i, s):
            used = is_end(s[0]) if number == outer[0] else is_mid(s[0])
            return row, jnp.where(used, jnp.minimum(column + start + i, last), column)

        return pl.BlockSpec((ROWS, tile), index)

    return pl.pallas_call(
        kernel,
        grid_spec=pltpu.PrefetchScalarGridSpec(
            num_scalar_prefetch=1, grid=(pl.cdiv(width, tile),),
            in_specs=[spec(n) for n in range(count)] + [pl.BlockSpec(memory_space=pl.ANY)] * len(tokens),
            out_specs=[pl.BlockSpec((ROWS, tile), lambda i, s: (0, i)),
                       pl.BlockSpec((ROWS, tile), lambda i, s: (0, jnp.where(is_mid(s[0]), i, 0)))]),
        out_shape=[jax.ShapeDtypeStruct((ROWS, width), jnp.bfloat16)] * 2,
        compiler_params=PARAMS,
        cost_estimate=SMALL,
    )(place, *[s[0] for s in sources], *tokens)


def absorb(place, whole, streams, work, sums_shape, sums, first=None, profile=None, tiles=(0, STEPS)):
    start, count = tiles
    tile = whole // STEPS
    names = list(streams)
    slab = streams["slab"][0]
    nrows, sites = slab.shape
    rest = sites - 3 * whole
    rest_width = rest + -rest % LANES
    long = [n for n in ("own", "x", "y") if n in names and streams[n][0].shape[1] % tile == rest_width] if first else []
    blocks, frames, width = sums_shape

    def kernel(place_ref, *refs):
        now = dict(zip(names, refs))
        refs = refs[len(names):]
        if sums is not None:
            sums_ref, refs = refs[0], refs[1:]
        if first:
            slab_rest, refs = refs[0], refs[1:]
            rests = dict(zip(long, refs))
            refs = refs[len(long):]
        if profile is None:
            acc, = refs
        else:
            profile_ref, outs, acc = refs[0], refs[1:-1], refs[-1]
        z, k = place_ref[0], place_ref[1]
        step = pl.program_id(0)

        def add(block, lane, value):
            acc[block, :, lane:lane + value.shape[1]] += value

        @pl.when(step == 0)
        def _():
            acc[...] = jnp.zeros(acc.shape, acc.dtype) if sums is None else sums_ref[...]
            if first:
                column = lax.broadcasted_iota(jnp.int32, (nrows, rest_width), 1)
                piece = jnp.where(column < rest, slab_rest[...].astype(jnp.float32), 0.0).astype(jnp.bfloat16)
                first(z, dict(rests, slab=piece), add)


        work(z, now, add)

        if profile is not None:
            @pl.when(step == count - 1)
            def _():
                weight = jnp.sum(profile_ref[...])
                lane = lax.broadcasted_iota(jnp.int32, (frames, LANES), 1)
                for turn, out in enumerate(outs):
                    out[...] = acc[k ^ turn]
                    middle = slice(LANES, 2 * LANES)
                    out[:, middle] = jnp.where(lane == FREE - 1 - LANES, weight, acc[k ^ turn, :, middle])

    def base(array):
        return 0 if array.shape[1] <= count * tile + rest_width else start

    def spec(array, needed, third):
        return pl.BlockSpec(
            (array.shape[0], tile),
            lambda i, s: (0, third(s[0]) * STEPS + jnp.where(needed(s[0]), base(array) + i, 0)))

    in_specs = [spec(*streams[n]) for n in names]
    operands = [streams[n][0] for n in names]
    if sums is not None:
        in_specs.append(pl.BlockSpec(sums_shape, lambda i, s: (0, 0, 0)))
        operands.append(sums)
    if first:
        in_specs.append(pl.BlockSpec((nrows, rest_width), lambda i, s: (0, 3 * whole // rest_width)))
        in_specs += [pl.BlockSpec((frames, rest_width), lambda i, s, n=streams[n][0].shape[1]: (0, n // rest_width - 1)) for n in long]
        operands += [slab] + [streams[n][0] for n in long]
    if profile is None:
        out_shape = jax.ShapeDtypeStruct(sums_shape, jnp.float32)
        out_specs = pl.BlockSpec(sums_shape, lambda i, s: (0, 0, 0))
        scratch = []
    else:
        in_specs.append(pl.BlockSpec(profile.shape, lambda i, s: (0, 0)))
        operands.append(profile)
        out_shape = [jax.ShapeDtypeStruct(sums_shape[1:], jnp.float32)] * blocks
        out_specs = [pl.BlockSpec(sums_shape[1:], lambda i, s: (0, 0))] * blocks
        scratch = [pltpu.VMEM(sums_shape, jnp.float32)]
    return pl.pallas_call(
        kernel,
        grid_spec=pltpu.PrefetchScalarGridSpec(
            num_scalar_prefetch=1, grid=(count,), in_specs=in_specs, out_specs=out_specs, scratch_shapes=scratch),
        out_shape=out_shape,
        compiler_params=PARAMS,
        cost_estimate=SMALL,
    )(place, *operands)


def line_plan(slab, noise, volts, labels, profile, sizes):
    wide, owners = sizes
    panels, rows, sites = slab.shape
    frames = noise.shape[0]
    nrows = panels * rows
    third = sites // 3 // LANES * LANES
    z = lax.axis_index("wide")
    k = lax.axis_index(SITES)
    place = jnp.stack([z, k]).astype(jnp.int32)
    slab = slab.reshape(nrows, sites)
    outer = [(0, 1), (1, 0), (2, 3), (3, 2)]
    inner = [(1, 2), (2, 1)]

    def send(pair):
        y = lax.ppermute(pair[1], "wide", inner)
        return lax.ppermute(pair[0], "wide", outer), y

    def routed(sources, to_outer, to_inner, width, tokens, start=0):
        sources = [s if isinstance(s, tuple) else (s, 0, 0) for s in sources]
        pair = route(place, third, sources, to_outer, to_inner, start, width, tokens)
        return send(pair), pair[0]

    def spare(i):
        return (slab, i, 2 * STEPS)

    rest = sites - 3 * third
    long = third + rest + -rest % LANES
    own_a = potential_of(noise[:, :long], volts, labels[:long])
    r1 = send((own_a, own_a))
    own_b, own_c = later_potentials(noise, volts, labels, third, own_a)
    r2 = send((own_b, own_b))

    sums_shape = (wide, frames, WIDTH)

    def at(number):
        return lambda z: number

    def thirds(end, mid):
        return lambda z: jnp.where(is_mid(z), mid, end)

    def far(z, refs, name):
        return jnp.where(is_end(z), refs[name + "x"][...], refs[name + "y"][...])

    def both(name, pair, x_needed=always):
        return {name + "x": (pair[0], x_needed, at(0)), name + "y": (pair[1], is_mid, at(0))}

    def work1(z, refs, add):
        add(z, 0, dot(refs["own"][...], refs["slab"][...]))
        add(z ^ 1, 0, dot(refs["x"][...], refs["slab"][...]))

        @pl.when(is_mid(z))
        def _():
            add(3 - z, 0, dot(refs["y"][...], refs["slab"][...]))

    def work3(z, refs, add):
        add(z, 0, dot(refs["own"][...], refs["slab2"][...]))
        add((z + 2) % 4, 0, dot(far(z, refs, ""), refs["slab"][...]))

        @pl.when(is_mid(z))
        def _():
            add(z ^ 1, 0, dot(refs["x"][...], refs["slab2"][...]))

    def work4(z, refs, add):
        add((z + 2) % 4, 0, dot(far(z, refs, ""), refs["slab"][...]))

    def work5(z, refs, add):
        came = far(z, refs, "")
        add(3 - z, 0, dot(came, refs["slab"][...]))

        @pl.when(is_mid(z))
        def _():
            brought = jnp.concatenate([refs["4"][...], refs["x"][...]], axis=0)
            add(z, 2 * LANES, dot(refs["own"][...], brought))
            add(3 - z, 2 * LANES, dot(came, brought))

    def first4(z, refs, add):
        add((z + 2) % 4, 0, dot(far(z, refs, ""), refs["slab"]))

    def first6(z, refs, add):
        @pl.when(is_end(z))
        def _():
            add(3 - z, 0, dot(far(z, refs, ""), refs["slab"]))

    def work6(z, refs, add):
        came = far(z, refs, "")
        block = jnp.where(z < 2, 3, 0)
        add(block, 0, dot(came, refs["slab"][...]))

        @pl.when(is_mid(z))
        def _():
            newest = refs["x"][...]
            brought = jnp.concatenate([refs["4"][...], refs["5x"][...], newest], axis=0)
            add(block, 2 * LANES, dot(came, brought))
            both = dot(jnp.concatenate([refs["own"][...], refs["5y"][...]], axis=0), newest)
            add(z, 3 * LANES, both[:frames])
            add(3 - z, 3 * LANES, both[frames:])

    r3, sent = routed([own_c, r1[0], r1[1]], (0, 2), 1, long, [])
    r4, sent = routed([spare(0), r2[0], r2[1]], (0, 2), 1, long, [sent])
    sums = absorb(
        place, third, dict(both("", r1), slab=(slab, always, at(0)), own=(own_a, always, at(0))), work1, sums_shape, None)
    sums = absorb(
        place, third, dict(both("", r2), slab=(slab, always, at(1)), own=(own_b, always, at(0))), work1, sums_shape, sums,
        first=work1)
    r5, sent = routed([spare(1), r3[1], own_c], (0, 1), 2, long, [sent, sums])
    sums = absorb(
        place, third,
        dict(both("", r3), slab=(slab, always, at(0)), slab2=(slab, always, at(2)), own=(own_c, always, at(0))),
        work3, sums_shape, sums)
    tile = third // STEPS
    r6_sources = [spare(2), r4[1], r3[0]]
    r6, sent = routed(r6_sources, (0, 1), 2, third - tile, [sent, sums])
    r7, sent = routed(r6_sources, (0, 1), 2, long - third + tile, [sent], STEPS - 1)
    sums = absorb(
        place, third, dict(both("", r4), slab=(slab, always, at(1))), work4, sums_shape, sums, first=first4)
    middle = {"4": (r4[0], is_mid, at(0)), "own": (own_c, is_mid, at(0))}
    sums = absorb(place, third, dict(both("", r5), slab=(slab, always, thirds(0, 2)), **middle), work5, sums_shape, sums)
    middle.update(both("5", r5, is_mid))
    sums = absorb(
        place, third, dict(both("", r6), slab=(slab, always, thirds(1, 2)), **middle), work6, sums_shape, sums,
        tiles=(0, STEPS - 1))
    messages = absorb(
        place, third, dict(both("", r7), slab=(slab, always, thirds(1, 2)), **middle), work6, sums_shape, sums,
        first=first6, profile=profile, tiles=(STEPS - 1, 1))

    summed = messages[0]
    for turn in range(1, owners):
        summed += lax.ppermute(messages[turn], SITES, [(i, i ^ turn) for i in range(owners)])
    half = WIDTH // 2
    frame_sum = jnp.sum(summed[:, :nrows], axis=1) + jnp.sum(summed[:, half:half + nrows], axis=1)
    lane = jnp.arange(WIDTH) % half
    sent = jnp.where(lane[None, :] == FREE, frame_sum[:, None], summed)
    flip = [(a * owners + b, b * owners + a) for a in range(wide) for b in range(owners)]
    got = lax.ppermute(sent, ALL, flip)

    def beside(x, turn):
        return lax.ppermute(x, SITES, [(i, i ^ turn) for i in range(owners)])

    mine, frame_sum = got[:, :half], got[:, FREE]
    extra = beside(got[:, half:], 1)
    total = frame_sum + extra[:, FREE] + beside(frame_sum, 2) + beside(frame_sum, 3)
    weight_sum = mine[:, FREE - 1]
    charges = (mine + extra)[:, :nrows].reshape(frames, panels, rows).transpose(1, 2, 0)
    return finish(charges, total, weight_sum, profile)


def solution(mesh):
    wide = mesh.shape["wide"]
    owners = mesh.shape["narrow"] * mesh.shape["sub"]
    plan = line_plan if wide == owners == 4 else gather_plan

    def local(slab, noise, volts, labels, profile):
        return plan(slab, noise, volts, labels, profile, (wide, owners))

    return jax.shard_map(
        local,
        mesh=mesh,
        in_specs=(
            P(None, "wide", ("narrow", "sub")),
            P(("grp", "wide"), ("narrow", "sub")),
            P(("grp", "wide"), None),
            P(("narrow", "sub")),
            P(None, ("narrow", "sub")),
        ),
        out_specs=P(None, ("narrow", "sub"), ("grp", "wide")),
        check_vma=False,
    )
```

```python
import jax
import jax.numpy as jnp
from jax import lax
from jax.experimental import pallas as pl
from jax.experimental.pallas import tpu as pltpu
from jax.sharding import PartitionSpec as P

SITES = ("narrow", "sub")
ALL = ("wide", "narrow", "sub")


def dot_t(a, b):
    return lax.dot_general(a, b, (((1,), (1,)), ((), ())), preferred_element_type=jnp.float32)


def potential_of(noise, volts, labels):
    value = volts[:, 0:1]
    for kind in range(1, volts.shape[1]):
        value = jnp.where(labels[None, :] == kind, volts[:, kind:kind + 1], value)
    return (value + noise.astype(jnp.float32)).astype(jnp.bfloat16)


def finish(charges, total, weight_sum, profile):
    return charges - profile[:, :, None] * (total / weight_sum)[None, None, :]


def gather_plan(slab, noise, volts, labels, profile, sizes):
    wide, owners = sizes
    panels, rows, _ = slab.shape
    frames = noise.shape[0]
    pot = lax.all_gather(potential_of(noise, volts, labels), "wide", axis=0, tiled=True)
    part = dot_t(slab.reshape(panels * rows, -1), pot).reshape(panels, rows, wide, frames)
    mine = lax.all_to_all(part, "wide", 2, 1, tiled=True).reshape(panels, wide * rows, frames)
    charges = lax.psum_scatter(mine, SITES, scatter_dimension=1, tiled=True)
    total, weight_sum = lax.psum((jnp.sum(charges, axis=(0, 1)), jnp.sum(profile)), SITES)
    return finish(charges, total, weight_sum, profile)


LANES = 128
STEPS = 4
ROWS = 64
WIDTH = 4 * LANES
FREE = LANES * 2 - 1
PARAMS = pltpu.CompilerParams(vmem_limit_bytes=16 * 1024 * 1024)
SMALL = pl.CostEstimate(flops=1000, bytes_accessed=1000, transcendentals=0)


def always(z):
    return z >= 0


def is_mid(z):
    return (z == 1) | (z == 2)


def is_end(z):
    return (z == 0) | (z == 3)


def dot(a, b):
    return lax.dot_general(a, b, (((1,), (1,)), ((), ())), preferred_element_type=jnp.float32)


def later_potentials(noise, volts, labels, third, token):
    frames, sites = noise.shape
    tile = third // STEPS
    rest = sites - 3 * third
    rest_width = rest + -rest % LANES
    labels = labels.reshape(1, sites)
    volts = volts.T

    def kernel(noise_b, labels_b, noise_c, labels_c, noise_rest, labels_rest, volts_ref, token_ref, out_b, out_c):
        diagonal = (lax.broadcasted_iota(jnp.int32, (frames, frames), 0)
                    == lax.broadcasted_iota(jnp.int32, (frames, frames), 1))
        columns = [jnp.sum(jnp.where(diagonal, volts_ref[kind:kind + 1, :], 0.0), axis=1, keepdims=True)
                   for kind in range(volts_ref.shape[0])]

        def potential(noise, labels):
            value = jnp.broadcast_to(columns[0], noise.shape)
            for kind in range(1, len(columns)):
                value = jnp.where(labels == kind, columns[kind], value)
            return value + noise.astype(jnp.float32)

        step = pl.program_id(0)
        at = pl.multiple_of(step * tile, LANES)
        out_b[:, pl.ds(at, tile)] = potential(noise_b[...], labels_b[...]).astype(jnp.bfloat16)
        out_c[...] = potential(noise_c[...], labels_c[...]).astype(jnp.bfloat16)

        @pl.when(step == 0)
        def _():
            column = lax.broadcasted_iota(jnp.int32, (frames, rest_width), 1)
            value = jnp.where(column < rest, potential(noise_rest[...], labels_rest[...]), 0.0)
            out_b[:, third:] = value.astype(jnp.bfloat16)

    last = 3 * third // rest_width
    return pl.pallas_call(
        kernel,
        grid=(STEPS,),
        in_specs=[
            pl.BlockSpec((frames, tile), lambda i: (0, STEPS + i)),
            pl.BlockSpec((1, tile), lambda i: (0, STEPS + i)),
            pl.BlockSpec((frames, tile), lambda i: (0, 2 * STEPS + i)),
            pl.BlockSpec((1, tile), lambda i: (0, 2 * STEPS + i)),
            pl.BlockSpec((frames, rest_width), lambda i: (0, last)),
            pl.BlockSpec((1, rest_width), lambda i: (0, last)),
            pl.BlockSpec(volts.shape, lambda i: (0, 0)),
            pl.BlockSpec(memory_space=pl.ANY),
        ],
        out_specs=[pl.BlockSpec((frames, third + rest_width), lambda i: (0, 0)),
                   pl.BlockSpec((frames, tile), lambda i: (0, i))],
        out_shape=[jax.ShapeDtypeStruct((frames, third + rest_width), jnp.bfloat16),
                   jax.ShapeDtypeStruct((frames, third), jnp.bfloat16)],
        compiler_params=PARAMS,
        cost_estimate=SMALL,
    )(noise, labels, noise, labels, noise, labels, volts, token)


def route(place, whole, sources, outer, inner, start, width, tokens):
    tile = whole // STEPS
    count = len(sources)

    def kernel(place_ref, *refs):
        out_x, out_y = refs[count + len(tokens):]
        z = place_ref[0]

        @pl.when(is_end(z))
        def _():
            out_x[...] = refs[outer[0]][...]

        @pl.when(is_mid(z))
        def _():
            out_x[...] = refs[outer[1]][...]
            out_y[...] = refs[inner][...]

    def spec(number):
        array, row, column = sources[number]
        last = (array.shape[1] - 1) // tile if column == 0 else column + STEPS - 1

        def index(i, s):
            used = is_end(s[0]) if number == outer[0] else is_mid(s[0])
            return row, jnp.where(used, jnp.minimum(column + start + i, last), column)

        return pl.BlockSpec((ROWS, tile), index)

    return pl.pallas_call(
        kernel,
        grid_spec=pltpu.PrefetchScalarGridSpec(
            num_scalar_prefetch=1, grid=(pl.cdiv(width, tile),),
            in_specs=[spec(n) for n in range(count)] + [pl.BlockSpec(memory_space=pl.ANY)] * len(tokens),
            out_specs=[pl.BlockSpec((ROWS, tile), lambda i, s: (0, i)),
                       pl.BlockSpec((ROWS, tile), lambda i, s: (0, jnp.where(is_mid(s[0]), i, 0)))]),
        out_shape=[jax.ShapeDtypeStruct((ROWS, width), jnp.bfloat16)] * 2,
        compiler_params=PARAMS,
        cost_estimate=SMALL,
    )(place, *[s[0] for s in sources], *tokens)


def absorb(place, whole, streams, work, sums_shape, sums, first=None, profile=None, tiles=(0, STEPS)):
    start, count = tiles
    tile = whole // STEPS
    names = list(streams)
    slab = streams["slab"][0]
    nrows, sites = slab.shape
    rest = sites - 3 * whole
    rest_width = rest + -rest % LANES
    long = [n for n in ("own", "x", "y") if n in names and streams[n][0].shape[1] % tile == rest_width] if first else []
    blocks, frames, width = sums_shape

    def kernel(place_ref, *refs):
        now = dict(zip(names, refs))
        refs = refs[len(names):]
        if sums is not None:
            sums_ref, refs = refs[0], refs[1:]
        if first:
            slab_rest, refs = refs[0], refs[1:]
            rests = dict(zip(long, refs))
            refs = refs[len(long):]
        if profile is None:
            acc, = refs
        else:
            profile_ref, outs, acc = refs[0], refs[1:-1], refs[-1]
        z, k = place_ref[0], place_ref[1]
        step = pl.program_id(0)

        def add(block, lane, value):
            acc[block, :, lane:lane + value.shape[1]] += value

        @pl.when(step == 0)
        def _():
            acc[...] = jnp.zeros(acc.shape, acc.dtype) if sums is None else sums_ref[...]
            if first:
                column = lax.broadcasted_iota(jnp.int32, (nrows, rest_width), 1)
                piece = jnp.where(column < rest, slab_rest[...].astype(jnp.float32), 0.0).astype(jnp.bfloat16)
                first(z, dict(rests, slab=piece), add)


        work(z, now, add)

        if profile is not None:
            @pl.when(step == count - 1)
            def _():
                weight = jnp.sum(profile_ref[...])
                lane = lax.broadcasted_iota(jnp.int32, (frames, width), 1)
                for turn, out in enumerate(outs):
                    value = acc[k ^ turn]
                    moved = pltpu.roll(value, width // 2 + nrows, axis=1)
                    out[:frames, :] = jnp.where(lane < nrows, value, moved)[:, :2 * nrows]
                    out[frames:, :] = jnp.full((8, 2 * nrows), weight, jnp.float32)

    def base(array):
        return 0 if array.shape[1] <= count * tile + rest_width else start

    def spec(array, needed, third):
        return pl.BlockSpec(
            (array.shape[0], tile),
            lambda i, s: (0, third(s[0]) * STEPS + jnp.where(needed(s[0]), base(array) + i, 0)))

    in_specs = [spec(*streams[n]) for n in names]
    operands = [streams[n][0] for n in names]
    if sums is not None:
        in_specs.append(pl.BlockSpec(sums_shape, lambda i, s: (0, 0, 0)))
        operands.append(sums)
    if first:
        in_specs.append(pl.BlockSpec((nrows, rest_width), lambda i, s: (0, 3 * whole // rest_width)))
        in_specs += [pl.BlockSpec((frames, rest_width), lambda i, s, n=streams[n][0].shape[1]: (0, n // rest_width - 1)) for n in long]
        operands += [slab] + [streams[n][0] for n in long]
    if profile is None:
        out_shape = jax.ShapeDtypeStruct(sums_shape, jnp.float32)
        out_specs = pl.BlockSpec(sums_shape, lambda i, s: (0, 0, 0))
        scratch = []
    else:
        in_specs.append(pl.BlockSpec(profile.shape, lambda i, s: (0, 0)))
        operands.append(profile)
        message = (frames + 8, 2 * nrows)
        out_shape = [jax.ShapeDtypeStruct(message, jnp.float32)] * blocks
        out_specs = [pl.BlockSpec(message, lambda i, s: (0, 0))] * blocks
        scratch = [pltpu.VMEM(sums_shape, jnp.float32)]
    return pl.pallas_call(
        kernel,
        grid_spec=pltpu.PrefetchScalarGridSpec(
            num_scalar_prefetch=1, grid=(count,), in_specs=in_specs, out_specs=out_specs, scratch_shapes=scratch),
        out_shape=out_shape,
        compiler_params=PARAMS,
        cost_estimate=SMALL,
    )(place, *operands)


def line_plan(slab, noise, volts, labels, profile, sizes):
    wide, owners = sizes
    panels, rows, sites = slab.shape
    frames = noise.shape[0]
    nrows = panels * rows
    third = sites // 3 // LANES * LANES
    z = lax.axis_index("wide")
    k = lax.axis_index(SITES)
    place = jnp.stack([z, k]).astype(jnp.int32)
    slab = slab.reshape(nrows, sites)
    outer = [(0, 1), (1, 0), (2, 3), (3, 2)]
    inner = [(1, 2), (2, 1)]

    def send(pair):
        return lax.ppermute(pair[0], "wide", outer), lax.ppermute(pair[1], "wide", inner)

    def routed(sources, to_outer, to_inner, width, tokens, start=0):
        sources = [s if isinstance(s, tuple) else (s, 0, 0) for s in sources]
        pair = route(place, third, sources, to_outer, to_inner, start, width, tokens)
        return send(pair), pair[0]

    def spare(i):
        return (slab, i, 2 * STEPS)

    rest = sites - 3 * third
    long = third + rest + -rest % LANES
    own_a = potential_of(noise[:, :long], volts, labels[:long])
    r1 = send((own_a, own_a))
    own_b, own_c = later_potentials(noise, volts, labels, third, own_a)
    r2 = send((own_b, own_b))

    sums_shape = (wide, frames, WIDTH)

    def at(number):
        return lambda z: number

    def thirds(end, mid):
        return lambda z: jnp.where(is_mid(z), mid, end)

    def far(z, refs, name):
        return jnp.where(is_end(z), refs[name + "x"][...], refs[name + "y"][...])

    def both(name, pair, x_needed=always):
        return {name + "x": (pair[0], x_needed, at(0)), name + "y": (pair[1], is_mid, at(0))}

    def work1(z, refs, add):
        add(z, 0, dot(refs["own"][...], refs["slab"][...]))
        add(z ^ 1, 0, dot(refs["x"][...], refs["slab"][...]))

        @pl.when(is_mid(z))
        def _():
            add(3 - z, 0, dot(refs["y"][...], refs["slab"][...]))

    def work3(z, refs, add):
        add(z, 0, dot(refs["own"][...], refs["slab2"][...]))
        add((z + 2) % 4, 0, dot(far(z, refs, ""), refs["slab"][...]))

        @pl.when(is_mid(z))
        def _():
            add(z ^ 1, 0, dot(refs["x"][...], refs["slab2"][...]))

    def work4(z, refs, add):
        add((z + 2) % 4, 0, dot(far(z, refs, ""), refs["slab"][...]))

    def work5(z, refs, add):
        came = far(z, refs, "")
        add(3 - z, 0, dot(came, refs["slab"][...]))

        @pl.when(is_mid(z))
        def _():
            brought = jnp.concatenate([refs["4"][...], refs["x"][...]], axis=0)
            add(z, 2 * LANES, dot(refs["own"][...], brought))
            add(3 - z, 2 * LANES, dot(came, brought))

    def first4(z, refs, add):
        add((z + 2) % 4, 0, dot(far(z, refs, ""), refs["slab"]))

    def first6(z, refs, add):
        @pl.when(is_end(z))
        def _():
            add(3 - z, 0, dot(far(z, refs, ""), refs["slab"]))

    def work6(z, refs, add):
        came = far(z, refs, "")
        block = jnp.where(z < 2, 3, 0)
        add(block, 0, dot(came, refs["slab"][...]))

        @pl.when(is_mid(z))
        def _():
            newest = refs["x"][...]
            brought = jnp.concatenate([refs["4"][...], refs["5x"][...], newest], axis=0)
            add(block, 2 * LANES, dot(came, brought))
            both = dot(jnp.concatenate([refs["own"][...], refs["5y"][...]], axis=0), newest)
            add(z, 3 * LANES, both[:frames])
            add(3 - z, 3 * LANES, both[frames:])

    r3, sent = routed([own_c, r1[1], r1[0]], (0, 1), 2, long, [])
    r4, sent = routed([spare(0), r2[1], r2[0]], (0, 1), 2, long, [sent])
    sums = absorb(
        place, third, dict(both("", r1), slab=(slab, always, at(0)), own=(own_a, always, at(0))), work1, sums_shape, None)
    sums = absorb(
        place, third, dict(both("", r2), slab=(slab, always, at(1)), own=(own_b, always, at(0))), work1, sums_shape, sums,
        first=work1)
    r5, sent = routed([spare(1), r3[1], own_c], (0, 1), 2, long, [sent, sums])
    sums = absorb(
        place, third,
        dict(both("", r3), slab=(slab, always, at(0)), slab2=(slab, always, at(2)), own=(own_c, always, at(0))),
        work3, sums_shape, sums)
    tile = third // STEPS
    r6_sources = [spare(2), r4[1], r3[0]]
    r6, sent = routed(r6_sources, (0, 1), 2, third - tile, [sent, sums])
    r7, sent = routed(r6_sources, (0, 1), 2, long - third + tile, [sent], STEPS - 1)
    sums = absorb(
        place, third, dict(both("", r4), slab=(slab, always, at(1))), work4, sums_shape, sums, first=first4)
    middle = {"4": (r4[0], is_mid, at(0)), "own": (own_c, is_mid, at(0))}
    sums = absorb(place, third, dict(both("", r5), slab=(slab, always, thirds(0, 2)), **middle), work5, sums_shape, sums)
    middle.update(both("5", r5, is_mid))
    sums = absorb(
        place, third, dict(both("", r6), slab=(slab, always, thirds(1, 2)), **middle), work6, sums_shape, sums,
        tiles=(0, STEPS - 1))
    messages = absorb(
        place, third, dict(both("", r7), slab=(slab, always, thirds(1, 2)), **middle), work6, sums_shape, sums,
        first=first6, profile=profile, tiles=(STEPS - 1, 1))

    summed = messages[0]
    for turn in range(1, owners):
        summed += lax.ppermute(messages[turn], SITES, [(i, i ^ turn) for i in range(owners)])
    half = WIDTH // 2
    weights, summed = summed[frames:frames + 1], summed[:frames]
    frame_sum = jnp.sum(summed, axis=1)
    lane = jnp.arange(half)[None, :]
    skip = 2 * nrows - half
    mine = jnp.where(lane == FREE - 1, weights[:, :half], summed[:, :half])
    mine = jnp.where(lane == FREE, frame_sum[:, None], mine)
    extra = jnp.where(lane == 0, frame_sum[:, None], summed[:, skip:])
    def flip(turn):
        return [(a * owners + b, b * owners + (a ^ turn)) for a in range(wide) for b in range(owners)]

    mine, extra = lax.ppermute(mine, ALL, flip(0)), lax.ppermute(extra, ALL, flip(1))
    total = mine[:, FREE] + extra[:, 0] + lax.ppermute(frame_sum, ALL, flip(2)) + lax.ppermute(frame_sum, ALL, flip(3))
    weight_sum = mine[:, FREE - 1]
    charges = (mine[:, :nrows] + extra[:, nrows - skip:]).reshape(frames, panels, rows).transpose(1, 2, 0)
    return finish(charges, total, weight_sum, profile)


def solution(mesh):
    wide = mesh.shape["wide"]
    owners = mesh.shape["narrow"] * mesh.shape["sub"]
    plan = line_plan if wide == owners == 4 else gather_plan

    def local(slab, noise, volts, labels, profile):
        return plan(slab, noise, volts, labels, profile, (wide, owners))

    return jax.shard_map(
        local,
        mesh=mesh,
        in_specs=(
            P(None, "wide", ("narrow", "sub")),
            P(("grp", "wide"), ("narrow", "sub")),
            P(("grp", "wide"), None),
            P(("narrow", "sub")),
            P(None, ("narrow", "sub")),
        ),
        out_specs=P(None, ("narrow", "sub"), ("grp", "wide")),
        check_vma=False,
    )
```

```python
import jax
import jax.numpy as jnp
from jax import lax
from jax.experimental import pallas as pl
from jax.experimental.pallas import tpu as pltpu
from jax.sharding import PartitionSpec as P

SITES = ("narrow", "sub")
ALL = ("wide", "narrow", "sub")


def dot_t(a, b):
    return lax.dot_general(a, b, (((1,), (1,)), ((), ())), preferred_element_type=jnp.float32)


def potential_of(noise, volts, labels):
    value = volts[:, 0:1]
    for kind in range(1, volts.shape[1]):
        value = jnp.where(labels[None, :] == kind, volts[:, kind:kind + 1], value)
    return (value + noise.astype(jnp.float32)).astype(jnp.bfloat16)


def finish(charges, total, weight_sum, profile):
    return charges - profile[:, :, None] * (total / weight_sum)[None, None, :]


def gather_plan(slab, noise, volts, labels, profile, sizes):
    wide, owners = sizes
    panels, rows, _ = slab.shape
    frames = noise.shape[0]
    pot = lax.all_gather(potential_of(noise, volts, labels), "wide", axis=0, tiled=True)
    part = dot_t(slab.reshape(panels * rows, -1), pot).reshape(panels, rows, wide, frames)
    mine = lax.all_to_all(part, "wide", 2, 1, tiled=True).reshape(panels, wide * rows, frames)
    charges = lax.psum_scatter(mine, SITES, scatter_dimension=1, tiled=True)
    total, weight_sum = lax.psum((jnp.sum(charges, axis=(0, 1)), jnp.sum(profile)), SITES)
    return finish(charges, total, weight_sum, profile)


LANES = 128
STEPS = 4
ROWS = 64
WIDTH = 4 * LANES
FREE = LANES * 2 - 1
PARAMS = pltpu.CompilerParams(vmem_limit_bytes=16 * 1024 * 1024)
SMALL = pl.CostEstimate(flops=1000, bytes_accessed=1000, transcendentals=0)


def always(z):
    return z >= 0


def is_mid(z):
    return (z == 1) | (z == 2)


def is_end(z):
    return (z == 0) | (z == 3)


def dot(a, b):
    return lax.dot_general(a, b, (((1,), (1,)), ((), ())), preferred_element_type=jnp.float32)


def later_potentials(noise, volts, labels, third, token):
    frames, sites = noise.shape
    tile = third // STEPS
    rest = sites - 3 * third
    rest_width = rest + -rest % LANES
    labels = labels.reshape(1, sites)
    volts = volts.T

    def kernel(noise_b, labels_b, noise_c, labels_c, noise_rest, labels_rest, volts_ref, token_ref, out_b, out_c):
        diagonal = (lax.broadcasted_iota(jnp.int32, (frames, frames), 0)
                    == lax.broadcasted_iota(jnp.int32, (frames, frames), 1))
        columns = [jnp.sum(jnp.where(diagonal, volts_ref[kind:kind + 1, :], 0.0), axis=1, keepdims=True)
                   for kind in range(volts_ref.shape[0])]

        def potential(noise, labels):
            value = jnp.broadcast_to(columns[0], noise.shape)
            for kind in range(1, len(columns)):
                value = jnp.where(labels == kind, columns[kind], value)
            return value + noise.astype(jnp.float32)

        step = pl.program_id(0)
        at = pl.multiple_of(step * tile, LANES)
        out_b[:, pl.ds(at, tile)] = potential(noise_b[...], labels_b[...]).astype(jnp.bfloat16)
        out_c[...] = potential(noise_c[...], labels_c[...]).astype(jnp.bfloat16)

        @pl.when(step == 0)
        def _():
            column = lax.broadcasted_iota(jnp.int32, (frames, rest_width), 1)
            value = jnp.where(column < rest, potential(noise_rest[...], labels_rest[...]), 0.0)
            out_b[:, third:] = value.astype(jnp.bfloat16)

    last = 3 * third // rest_width
    return pl.pallas_call(
        kernel,
        grid=(STEPS,),
        in_specs=[
            pl.BlockSpec((frames, tile), lambda i: (0, STEPS + i)),
            pl.BlockSpec((1, tile), lambda i: (0, STEPS + i)),
            pl.BlockSpec((frames, tile), lambda i: (0, 2 * STEPS + i)),
            pl.BlockSpec((1, tile), lambda i: (0, 2 * STEPS + i)),
            pl.BlockSpec((frames, rest_width), lambda i: (0, last)),
            pl.BlockSpec((1, rest_width), lambda i: (0, last)),
            pl.BlockSpec(volts.shape, lambda i: (0, 0)),
            pl.BlockSpec(memory_space=pl.ANY),
        ],
        out_specs=[pl.BlockSpec((frames, third + rest_width), lambda i: (0, 0)),
                   pl.BlockSpec((frames, tile), lambda i: (0, i))],
        out_shape=[jax.ShapeDtypeStruct((frames, third + rest_width), jnp.bfloat16),
                   jax.ShapeDtypeStruct((frames, third), jnp.bfloat16)],
        compiler_params=PARAMS,
        cost_estimate=SMALL,
    )(noise, labels, noise, labels, noise, labels, volts, token)


def route(place, whole, sources, outer, inner, start, width, tokens):
    tile = whole // STEPS
    count = len(sources)

    def kernel(place_ref, *refs):
        out_x, out_y = refs[count + len(tokens):]
        z = place_ref[0]

        @pl.when(is_end(z))
        def _():
            out_x[...] = refs[outer[0]][...]

        @pl.when(is_mid(z))
        def _():
            out_x[...] = refs[outer[1]][...]
            out_y[...] = refs[inner][...]

    def spec(number):
        array, row, column = sources[number]
        last = (array.shape[1] - 1) // tile if column == 0 else column + STEPS - 1

        def index(i, s):
            used = is_end(s[0]) if number == outer[0] else is_mid(s[0])
            return row, jnp.where(used, jnp.minimum(column + start + i, last), column)

        return pl.BlockSpec((ROWS, tile), index)

    return pl.pallas_call(
        kernel,
        grid_spec=pltpu.PrefetchScalarGridSpec(
            num_scalar_prefetch=1, grid=(pl.cdiv(width, tile),),
            in_specs=[spec(n) for n in range(count)] + [pl.BlockSpec(memory_space=pl.ANY)] * len(tokens),
            out_specs=[pl.BlockSpec((ROWS, tile), lambda i, s: (0, i)),
                       pl.BlockSpec((ROWS, tile), lambda i, s: (0, jnp.where(is_mid(s[0]), i, 0)))]),
        out_shape=[jax.ShapeDtypeStruct((ROWS, width), jnp.bfloat16)] * 2,
        compiler_params=PARAMS,
        cost_estimate=SMALL,
    )(place, *[s[0] for s in sources], *tokens)


def absorb(place, whole, streams, work, sums_shape, sums, first=None, profile=None, tiles=(0, STEPS)):
    start, count = tiles
    tile = whole // STEPS
    names = list(streams)
    slab = streams["slab"][0]
    nrows, sites = slab.shape
    rest = sites - 3 * whole
    rest_width = rest + -rest % LANES
    long = [n for n in ("own", "x", "y") if n in names and streams[n][0].shape[1] % tile == rest_width] if first else []
    blocks, frames, width = sums_shape

    def kernel(place_ref, *refs):
        now = dict(zip(names, refs))
        refs = refs[len(names):]
        if sums is not None:
            sums_ref, refs = refs[0], refs[1:]
        if first:
            slab_rest, refs = refs[0], refs[1:]
            rests = dict(zip(long, refs))
            refs = refs[len(long):]
        if profile is None:
            acc, = refs
        else:
            profile_ref, outs, acc = refs[0], refs[1:-1], refs[-1]
        z, k = place_ref[0], place_ref[1]
        step = pl.program_id(0)

        def add(block, lane, value):
            acc[block, :, lane:lane + value.shape[1]] += value

        @pl.when(step == 0)
        def _():
            acc[...] = jnp.zeros(acc.shape, acc.dtype) if sums is None else sums_ref[...]
            if first:
                column = lax.broadcasted_iota(jnp.int32, (nrows, rest_width), 1)
                piece = jnp.where(column < rest, slab_rest[...].astype(jnp.float32), 0.0).astype(jnp.bfloat16)
                first(z, dict(rests, slab=piece), add)


        work(z, now, add)

        if profile is not None:
            @pl.when(step == count - 1)
            def _():
                weight = jnp.sum(profile_ref[...])
                lane = lax.broadcasted_iota(jnp.int32, (frames, width), 1)
                for turn, out in enumerate(outs):
                    value = acc[k ^ turn]
                    moved = pltpu.roll(value, width // 2 + nrows, axis=1)
                    out[:frames, :] = jnp.where(lane < nrows, value, moved)[:, :2 * nrows]
                    out[frames:, :] = jnp.full((8, 2 * nrows), weight, jnp.float32)

    def base(array):
        return 0 if array.shape[1] <= count * tile + rest_width else start

    def spec(array, needed, third):
        return pl.BlockSpec(
            (array.shape[0], tile),
            lambda i, s: (0, third(s[0]) * STEPS + jnp.where(needed(s[0]), base(array) + i, 0)))

    in_specs = [spec(*streams[n]) for n in names]
    operands = [streams[n][0] for n in names]
    if sums is not None:
        in_specs.append(pl.BlockSpec(sums_shape, lambda i, s: (0, 0, 0)))
        operands.append(sums)
    if first:
        in_specs.append(pl.BlockSpec((nrows, rest_width), lambda i, s: (0, 3 * whole // rest_width)))
        in_specs += [pl.BlockSpec((frames, rest_width), lambda i, s, n=streams[n][0].shape[1]: (0, n // rest_width - 1)) for n in long]
        operands += [slab] + [streams[n][0] for n in long]
    if profile is None:
        out_shape = jax.ShapeDtypeStruct(sums_shape, jnp.float32)
        out_specs = pl.BlockSpec(sums_shape, lambda i, s: (0, 0, 0))
        scratch = []
    else:
        in_specs.append(pl.BlockSpec(profile.shape, lambda i, s: (0, 0)))
        operands.append(profile)
        message = (frames + 8, 2 * nrows)
        out_shape = [jax.ShapeDtypeStruct(message, jnp.float32)] * blocks
        out_specs = [pl.BlockSpec(message, lambda i, s: (0, 0))] * blocks
        scratch = [pltpu.VMEM(sums_shape, jnp.float32)]
    return pl.pallas_call(
        kernel,
        grid_spec=pltpu.PrefetchScalarGridSpec(
            num_scalar_prefetch=1, grid=(count,), in_specs=in_specs, out_specs=out_specs, scratch_shapes=scratch),
        out_shape=out_shape,
        compiler_params=PARAMS,
        cost_estimate=SMALL,
    )(place, *operands)


def line_plan(slab, noise, volts, labels, profile, sizes):
    wide, owners = sizes
    panels, rows, sites = slab.shape
    frames = noise.shape[0]
    nrows = panels * rows
    third = sites // 3 // LANES * LANES
    z = lax.axis_index("wide")
    k = lax.axis_index(SITES)
    place = jnp.stack([z, k]).astype(jnp.int32)
    slab = slab.reshape(nrows, sites)
    outer = [(0, 1), (1, 0), (2, 3), (3, 2)]
    inner = [(1, 2), (2, 1)]

    def send(pair):
        y = lax.ppermute(pair[1], "wide", inner)
        return lax.ppermute(pair[0], "wide", outer), y

    def routed(sources, to_outer, to_inner, width, tokens, start=0):
        sources = [s if isinstance(s, tuple) else (s, 0, 0) for s in sources]
        pair = route(place, third, sources, to_outer, to_inner, start, width, tokens)
        return send(pair), pair[0]

    def spare(i):
        return (slab, i, 2 * STEPS)

    rest = sites - 3 * third
    long = third + rest + -rest % LANES
    own_a = potential_of(noise[:, :long], volts, labels[:long])
    r1 = send((own_a, own_a))
    own_b, own_c = later_potentials(noise, volts, labels, third, own_a)
    r2 = send((own_b, own_b))

    sums_shape = (wide, frames, WIDTH)

    def at(number):
        return lambda z: number

    def thirds(end, mid):
        return lambda z: jnp.where(is_mid(z), mid, end)

    def far(z, refs, name):
        return jnp.where(is_end(z), refs[name + "x"][...], refs[name + "y"][...])

    def both(name, pair, x_needed=always):
        return {name + "x": (pair[0], x_needed, at(0)), name + "y": (pair[1], is_mid, at(0))}

    def work1(z, refs, add):
        add(z, 0, dot(refs["own"][...], refs["slab"][...]))
        add(z ^ 1, 0, dot(refs["x"][...], refs["slab"][...]))

        @pl.when(is_mid(z))
        def _():
            add(3 - z, 0, dot(refs["y"][...], refs["slab"][...]))

    def work3(z, refs, add):
        add(z, 0, dot(refs["own"][...], refs["slab2"][...]))
        add((z + 2) % 4, 0, dot(far(z, refs, ""), refs["slab"][...]))

        @pl.when(is_mid(z))
        def _():
            add(z ^ 1, 0, dot(refs["x"][...], refs["slab2"][...]))

    def work4(z, refs, add):
        add((z + 2) % 4, 0, dot(far(z, refs, ""), refs["slab"][...]))

    def work5(z, refs, add):
        came = far(z, refs, "")
        add(3 - z, 0, dot(came, refs["slab"][...]))

        @pl.when(is_mid(z))
        def _():
            brought = jnp.concatenate([refs["4"][...], refs["x"][...]], axis=0)
            add(z, 2 * LANES, dot(refs["own"][...], brought))
            add(3 - z, 2 * LANES, dot(came, brought))

    def first4(z, refs, add):
        add((z + 2) % 4, 0, dot(far(z, refs, ""), refs["slab"]))

    def first6(z, refs, add):
        @pl.when(is_end(z))
        def _():
            add(3 - z, 0, dot(far(z, refs, ""), refs["slab"]))

    def work6(z, refs, add):
        came = far(z, refs, "")
        block = jnp.where(z < 2, 3, 0)
        add(block, 0, dot(came, refs["slab"][...]))

        @pl.when(is_mid(z))
        def _():
            newest = refs["x"][...]
            brought = jnp.concatenate([refs["4"][...], refs["5x"][...], newest], axis=0)
            add(block, 2 * LANES, dot(came, brought))
            both = dot(jnp.concatenate([refs["own"][...], refs["5y"][...]], axis=0), newest)
            add(z, 3 * LANES, both[:frames])
            add(3 - z, 3 * LANES, both[frames:])

    r3, sent = routed([own_c, r1[0], r1[1]], (0, 2), 1, long, [])
    r4, sent = routed([spare(0), r2[0], r2[1]], (0, 2), 1, long, [sent])
    sums = absorb(
        place, third, dict(both("", r1), slab=(slab, always, at(0)), own=(own_a, always, at(0))), work1, sums_shape, None)
    sums = absorb(
        place, third, dict(both("", r2), slab=(slab, always, at(1)), own=(own_b, always, at(0))), work1, sums_shape, sums,
        first=work1)
    r5, sent = routed([spare(1), r3[1], own_c], (0, 1), 2, long, [sent, sums])
    sums = absorb(
        place, third,
        dict(both("", r3), slab=(slab, always, at(0)), slab2=(slab, always, at(2)), own=(own_c, always, at(0))),
        work3, sums_shape, sums)
    tile = third // STEPS
    r6_sources = [spare(2), r4[1], r3[0]]
    r6, sent = routed(r6_sources, (0, 1), 2, third - tile, [sent, sums])
    r7, sent = routed(r6_sources, (0, 1), 2, long - third + tile, [sent], STEPS - 1)
    sums = absorb(
        place, third, dict(both("", r4), slab=(slab, always, at(1))), work4, sums_shape, sums, first=first4)
    middle = {"4": (r4[0], is_mid, at(0)), "own": (own_c, is_mid, at(0))}
    sums = absorb(place, third, dict(both("", r5), slab=(slab, always, thirds(0, 2)), **middle), work5, sums_shape, sums)
    middle.update(both("5", r5, is_mid))
    sums = absorb(
        place, third, dict(both("", r6), slab=(slab, always, thirds(1, 2)), **middle), work6, sums_shape, sums,
        tiles=(0, STEPS - 1))
    messages = absorb(
        place, third, dict(both("", r7), slab=(slab, always, thirds(1, 2)), **middle), work6, sums_shape, sums,
        first=first6, profile=profile, tiles=(STEPS - 1, 1))

    summed = messages[0]
    for turn in range(1, owners):
        summed += lax.ppermute(messages[turn], SITES, [(i, i ^ turn) for i in range(owners)])
    half = WIDTH // 2
    weights, summed = summed[frames:frames + 1], summed[:frames]
    frame_sum = jnp.sum(summed, axis=1)
    lane = jnp.arange(half)[None, :]
    skip = 2 * nrows - half
    mine = jnp.where(lane == FREE - 1, weights[:, :half], summed[:, :half])
    mine = jnp.where(lane == FREE, frame_sum[:, None], mine)
    extra = jnp.where(lane == 0, frame_sum[:, None], summed[:, skip:])
    def flip(turn):
        return [(a * owners + b, b * owners + (a ^ turn)) for a in range(wide) for b in range(owners)]

    mine, extra = lax.ppermute(mine, ALL, flip(0)), lax.ppermute(extra, ALL, flip(1))
    total = mine[:, FREE] + extra[:, 0] + lax.ppermute(frame_sum, ALL, flip(2)) + lax.ppermute(frame_sum, ALL, flip(3))
    weight_sum = mine[:, FREE - 1]
    charges = (mine[:, :nrows] + extra[:, nrows - skip:]).reshape(frames, panels, rows).transpose(1, 2, 0)
    return finish(charges, total, weight_sum, profile)


def solution(mesh):
    wide = mesh.shape["wide"]
    owners = mesh.shape["narrow"] * mesh.shape["sub"]
    plan = line_plan if wide == owners == 4 else gather_plan

    def local(slab, noise, volts, labels, profile):
        return plan(slab, noise, volts, labels, profile, (wide, owners))

    return jax.shard_map(
        local,
        mesh=mesh,
        in_specs=(
            P(None, "wide", ("narrow", "sub")),
            P(("grp", "wide"), ("narrow", "sub")),
            P(("grp", "wide"), None),
            P(("narrow", "sub")),
            P(None, ("narrow", "sub")),
        ),
        out_specs=P(None, ("narrow", "sub"), ("grp", "wide")),
        check_vma=False,
    )
```

```python
import jax
import jax.numpy as jnp
from jax import lax
from jax.experimental import pallas as pl
from jax.experimental.pallas import tpu as pltpu
from jax.sharding import PartitionSpec as P

SITES = ("narrow", "sub")
ALL = ("wide", "narrow", "sub")


def dot_t(a, b):
    return lax.dot_general(a, b, (((1,), (1,)), ((), ())), preferred_element_type=jnp.float32)


def potential_of(noise, volts, labels):
    value = volts[:, 0:1]
    for kind in range(1, volts.shape[1]):
        value = jnp.where(labels[None, :] == kind, volts[:, kind:kind + 1], value)
    return (value + noise.astype(jnp.float32)).astype(jnp.bfloat16)


def finish(charges, total, weight_sum, profile):
    return charges - profile[:, :, None] * (total / weight_sum)[None, None, :]


def gather_plan(slab, noise, volts, labels, profile, sizes):
    wide, owners = sizes
    panels, rows, _ = slab.shape
    frames = noise.shape[0]
    pot = lax.all_gather(potential_of(noise, volts, labels), "wide", axis=0, tiled=True)
    part = dot_t(slab.reshape(panels * rows, -1), pot).reshape(panels, rows, wide, frames)
    mine = lax.all_to_all(part, "wide", 2, 1, tiled=True).reshape(panels, wide * rows, frames)
    charges = lax.psum_scatter(mine, SITES, scatter_dimension=1, tiled=True)
    total, weight_sum = lax.psum((jnp.sum(charges, axis=(0, 1)), jnp.sum(profile)), SITES)
    return finish(charges, total, weight_sum, profile)


LANES = 128
STEPS = 8
ROWS = 64
WIDTH = 4 * LANES
FREE = LANES * 2 - 1
PARAMS = pltpu.CompilerParams(vmem_limit_bytes=16 * 1024 * 1024)
SMALL = pl.CostEstimate(flops=1000, bytes_accessed=1000, transcendentals=0)


def always(z):
    return z >= 0


def is_mid(z):
    return (z == 1) | (z == 2)


def is_end(z):
    return (z == 0) | (z == 3)


def dot(a, b):
    return lax.dot_general(a, b, (((1,), (1,)), ((), ())), preferred_element_type=jnp.float32)


def later_potentials(noise, volts, labels, third, token):
    frames, sites = noise.shape
    tile = third // STEPS
    rest = sites - 3 * third
    rest_width = rest + -rest % LANES
    labels = labels.reshape(1, sites)
    volts = volts.T

    def kernel(noise_b, labels_b, noise_c, labels_c, noise_rest, labels_rest, volts_ref, token_ref, out_b, out_c):
        diagonal = (lax.broadcasted_iota(jnp.int32, (frames, frames), 0)
                    == lax.broadcasted_iota(jnp.int32, (frames, frames), 1))
        columns = [jnp.sum(jnp.where(diagonal, volts_ref[kind:kind + 1, :], 0.0), axis=1, keepdims=True)
                   for kind in range(volts_ref.shape[0])]

        def potential(noise, labels):
            value = jnp.broadcast_to(columns[0], noise.shape)
            for kind in range(1, len(columns)):
                value = jnp.where(labels == kind, columns[kind], value)
            return value + noise.astype(jnp.float32)

        step = pl.program_id(0)
        at = pl.multiple_of(step * tile, LANES)
        out_b[:, pl.ds(at, tile)] = potential(noise_b[...], labels_b[...]).astype(jnp.bfloat16)
        out_c[...] = potential(noise_c[...], labels_c[...]).astype(jnp.bfloat16)

        @pl.when(step == 0)
        def _():
            column = lax.broadcasted_iota(jnp.int32, (frames, rest_width), 1)
            value = jnp.where(column < rest, potential(noise_rest[...], labels_rest[...]), 0.0)
            out_b[:, third:] = value.astype(jnp.bfloat16)

    last = 3 * third // rest_width
    return pl.pallas_call(
        kernel,
        grid=(STEPS,),
        in_specs=[
            pl.BlockSpec((frames, tile), lambda i: (0, STEPS + i)),
            pl.BlockSpec((1, tile), lambda i: (0, STEPS + i)),
            pl.BlockSpec((frames, tile), lambda i: (0, 2 * STEPS + i)),
            pl.BlockSpec((1, tile), lambda i: (0, 2 * STEPS + i)),
            pl.BlockSpec((frames, rest_width), lambda i: (0, last)),
            pl.BlockSpec((1, rest_width), lambda i: (0, last)),
            pl.BlockSpec(volts.shape, lambda i: (0, 0)),
            pl.BlockSpec(memory_space=pl.ANY),
        ],
        out_specs=[pl.BlockSpec((frames, third + rest_width), lambda i: (0, 0)),
                   pl.BlockSpec((frames, tile), lambda i: (0, i))],
        out_shape=[jax.ShapeDtypeStruct((frames, third + rest_width), jnp.bfloat16),
                   jax.ShapeDtypeStruct((frames, third), jnp.bfloat16)],
        compiler_params=PARAMS,
        cost_estimate=SMALL,
    )(noise, labels, noise, labels, noise, labels, volts, token)


def route(place, whole, sources, outer, inner, start, width, tokens):
    tile = whole // STEPS
    count = len(sources)

    def kernel(place_ref, *refs):
        out_x, out_y = refs[count + len(tokens):]
        z = place_ref[0]

        @pl.when(is_end(z))
        def _():
            out_x[...] = refs[outer[0]][...]

        @pl.when(is_mid(z))
        def _():
            out_x[...] = refs[outer[1]][...]
            out_y[...] = refs[inner][...]

    def spec(number):
        array, row, column = sources[number]
        last = (array.shape[1] - 1) // tile if column == 0 else column + STEPS - 1

        def index(i, s):
            used = is_end(s[0]) if number == outer[0] else is_mid(s[0])
            return row, jnp.where(used, jnp.minimum(column + start + i, last), column)

        return pl.BlockSpec((ROWS, tile), index)

    return pl.pallas_call(
        kernel,
        grid_spec=pltpu.PrefetchScalarGridSpec(
            num_scalar_prefetch=1, grid=(pl.cdiv(width, tile),),
            in_specs=[spec(n) for n in range(count)] + [pl.BlockSpec(memory_space=pl.ANY)] * len(tokens),
            out_specs=[pl.BlockSpec((ROWS, tile), lambda i, s: (0, i)),
                       pl.BlockSpec((ROWS, tile), lambda i, s: (0, jnp.where(is_mid(s[0]), i, 0)))]),
        out_shape=[jax.ShapeDtypeStruct((ROWS, width), jnp.bfloat16)] * 2,
        compiler_params=PARAMS,
        cost_estimate=SMALL,
    )(place, *[s[0] for s in sources], *tokens)


def absorb(place, whole, streams, work, sums_shape, sums, first=None, profile=None, tiles=(0, STEPS)):
    start, count = tiles
    tile = whole // STEPS
    names = list(streams)
    slab = streams["slab"][0]
    nrows, sites = slab.shape
    rest = sites - 3 * whole
    rest_width = rest + -rest % LANES
    long = [n for n in ("own", "x", "y") if n in names and streams[n][0].shape[1] % tile == rest_width] if first else []
    blocks, frames, width = sums_shape

    def kernel(place_ref, *refs):
        now = dict(zip(names, refs))
        refs = refs[len(names):]
        if sums is not None:
            sums_ref, refs = refs[0], refs[1:]
        if first:
            slab_rest, refs = refs[0], refs[1:]
            rests = dict(zip(long, refs))
            refs = refs[len(long):]
        if profile is None:
            acc, = refs
        else:
            profile_ref, outs, acc = refs[0], refs[1:-1], refs[-1]
        z, k = place_ref[0], place_ref[1]
        step = pl.program_id(0)

        def add(block, lane, value):
            acc[block, :, lane:lane + value.shape[1]] += value

        @pl.when(step == 0)
        def _():
            acc[...] = jnp.zeros(acc.shape, acc.dtype) if sums is None else sums_ref[...]
            if first:
                column = lax.broadcasted_iota(jnp.int32, (nrows, rest_width), 1)
                piece = jnp.where(column < rest, slab_rest[...].astype(jnp.float32), 0.0).astype(jnp.bfloat16)
                first(z, dict(rests, slab=piece), add)


        work(z, now, add)

        if profile is not None:
            @pl.when(step == count - 1)
            def _():
                weight = jnp.sum(profile_ref[...])
                lane = lax.broadcasted_iota(jnp.int32, (frames, width), 1)
                for turn, out in enumerate(outs):
                    value = acc[k ^ turn]
                    moved = pltpu.roll(value, width // 2 + nrows, axis=1)
                    out[:frames, :] = jnp.where(lane < nrows, value, moved)[:, :2 * nrows]
                    out[frames:, :] = jnp.full((8, 2 * nrows), weight, jnp.float32)

    def base(array):
        return 0 if array.shape[1] <= count * tile + rest_width else start

    def spec(array, needed, third):
        return pl.BlockSpec(
            (array.shape[0], tile),
            lambda i, s: (0, third(s[0]) * STEPS + jnp.where(needed(s[0]), base(array) + i, 0)))

    in_specs = [spec(*streams[n]) for n in names]
    operands = [streams[n][0] for n in names]
    if sums is not None:
        in_specs.append(pl.BlockSpec(sums_shape, lambda i, s: (0, 0, 0)))
        operands.append(sums)
    if first:
        in_specs.append(pl.BlockSpec((nrows, rest_width), lambda i, s: (0, 3 * whole // rest_width)))
        in_specs += [pl.BlockSpec((frames, rest_width), lambda i, s, n=streams[n][0].shape[1]: (0, n // rest_width - 1)) for n in long]
        operands += [slab] + [streams[n][0] for n in long]
    if profile is None:
        out_shape = jax.ShapeDtypeStruct(sums_shape, jnp.float32)
        out_specs = pl.BlockSpec(sums_shape, lambda i, s: (0, 0, 0))
        scratch = []
    else:
        in_specs.append(pl.BlockSpec(profile.shape, lambda i, s: (0, 0)))
        operands.append(profile)
        message = (frames + 8, 2 * nrows)
        out_shape = [jax.ShapeDtypeStruct(message, jnp.float32)] * blocks
        out_specs = [pl.BlockSpec(message, lambda i, s: (0, 0))] * blocks
        scratch = [pltpu.VMEM(sums_shape, jnp.float32)]
    return pl.pallas_call(
        kernel,
        grid_spec=pltpu.PrefetchScalarGridSpec(
            num_scalar_prefetch=1, grid=(count,), in_specs=in_specs, out_specs=out_specs, scratch_shapes=scratch),
        out_shape=out_shape,
        compiler_params=PARAMS,
        cost_estimate=SMALL,
    )(place, *operands)


def line_plan(slab, noise, volts, labels, profile, sizes):
    wide, owners = sizes
    panels, rows, sites = slab.shape
    frames = noise.shape[0]
    nrows = panels * rows
    third = sites // 3 // LANES * LANES
    z = lax.axis_index("wide")
    k = lax.axis_index(SITES)
    place = jnp.stack([z, k]).astype(jnp.int32)
    slab = slab.reshape(nrows, sites)
    outer = [(0, 1), (1, 0), (2, 3), (3, 2)]
    inner = [(1, 2), (2, 1)]

    def send(pair):
        return lax.ppermute(pair[0], "wide", outer), lax.ppermute(pair[1], "wide", inner)

    def routed(sources, to_outer, to_inner, width, tokens, start=0):
        sources = [s if isinstance(s, tuple) else (s, 0, 0) for s in sources]
        pair = route(place, third, sources, to_outer, to_inner, start, width, tokens)
        return send(pair), pair[0]

    def spare(i):
        return (slab, i, 2 * STEPS)

    rest = sites - 3 * third
    long = third + rest + -rest % LANES
    own_a = potential_of(noise[:, :long], volts, labels[:long])
    r1 = send((own_a, own_a))
    own_b, own_c = later_potentials(noise, volts, labels, third, own_a)
    r2 = send((own_b, own_b))

    sums_shape = (wide, frames, WIDTH)

    def at(number):
        return lambda z: number

    def thirds(end, mid):
        return lambda z: jnp.where(is_mid(z), mid, end)

    def far(z, refs, name):
        return jnp.where(is_end(z), refs[name + "x"][...], refs[name + "y"][...])

    def both(name, pair, x_needed=always):
        return {name + "x": (pair[0], x_needed, at(0)), name + "y": (pair[1], is_mid, at(0))}

    def work1(z, refs, add):
        add(z, 0, dot(refs["own"][...], refs["slab"][...]))
        add(z ^ 1, 0, dot(refs["x"][...], refs["slab"][...]))

        @pl.when(is_mid(z))
        def _():
            add(3 - z, 0, dot(refs["y"][...], refs["slab"][...]))

    def work3(z, refs, add):
        add(z, 0, dot(refs["own"][...], refs["slab2"][...]))
        add((z + 2) % 4, 0, dot(far(z, refs, ""), refs["slab"][...]))

        @pl.when(is_mid(z))
        def _():
            add(z ^ 1, 0, dot(refs["x"][...], refs["slab2"][...]))

    def work4(z, refs, add):
        add((z + 2) % 4, 0, dot(far(z, refs, ""), refs["slab"][...]))

    def work5(z, refs, add):
        came = far(z, refs, "")
        add(3 - z, 0, dot(came, refs["slab"][...]))

        @pl.when(is_mid(z))
        def _():
            brought = jnp.concatenate([refs["4"][...], refs["x"][...]], axis=0)
            add(z, 2 * LANES, dot(refs["own"][...], brought))
            add(3 - z, 2 * LANES, dot(came, brought))

    def first4(z, refs, add):
        add((z + 2) % 4, 0, dot(far(z, refs, ""), refs["slab"]))

    def first6(z, refs, add):
        @pl.when(is_end(z))
        def _():
            add(3 - z, 0, dot(far(z, refs, ""), refs["slab"]))

    def work6(z, refs, add):
        came = far(z, refs, "")
        block = jnp.where(z < 2, 3, 0)
        add(block, 0, dot(came, refs["slab"][...]))

        @pl.when(is_mid(z))
        def _():
            newest = refs["x"][...]
            brought = jnp.concatenate([refs["4"][...], refs["5x"][...], newest], axis=0)
            add(block, 2 * LANES, dot(came, brought))
            both = dot(jnp.concatenate([refs["own"][...], refs["5y"][...]], axis=0), newest)
            add(z, 3 * LANES, both[:frames])
            add(3 - z, 3 * LANES, both[frames:])

    r3, sent = routed([own_c, r1[1], r1[0]], (0, 1), 2, long, [])
    r4, sent = routed([spare(0), r2[1], r2[0]], (0, 1), 2, long, [sent])
    sums = absorb(
        place, third, dict(both("", r1), slab=(slab, always, at(0)), own=(own_a, always, at(0))), work1, sums_shape, None)
    sums = absorb(
        place, third, dict(both("", r2), slab=(slab, always, at(1)), own=(own_b, always, at(0))), work1, sums_shape, sums,
        first=work1)
    r5, sent = routed([spare(1), r3[1], own_c], (0, 1), 2, long, [sent, sums])
    sums = absorb(
        place, third,
        dict(both("", r3), slab=(slab, always, at(0)), slab2=(slab, always, at(2)), own=(own_c, always, at(0))),
        work3, sums_shape, sums)
    tile = third // STEPS
    r6_sources = [spare(2), r4[1], r3[0]]
    r6, sent = routed(r6_sources, (0, 1), 2, third - tile, [sent, sums])
    r7, sent = routed(r6_sources, (0, 1), 2, long - third + tile, [sent], STEPS - 1)
    sums = absorb(
        place, third, dict(both("", r4), slab=(slab, always, at(1))), work4, sums_shape, sums, first=first4)
    middle = {"4": (r4[0], is_mid, at(0)), "own": (own_c, is_mid, at(0))}
    sums = absorb(place, third, dict(both("", r5), slab=(slab, always, thirds(0, 2)), **middle), work5, sums_shape, sums)
    middle.update(both("5", r5, is_mid))
    sums = absorb(
        place, third, dict(both("", r6), slab=(slab, always, thirds(1, 2)), **middle), work6, sums_shape, sums,
        tiles=(0, STEPS - 1))
    messages = absorb(
        place, third, dict(both("", r7), slab=(slab, always, thirds(1, 2)), **middle), work6, sums_shape, sums,
        first=first6, profile=profile, tiles=(STEPS - 1, 1))

    summed = messages[0]
    for turn in range(1, owners):
        summed += lax.ppermute(messages[turn], SITES, [(i, i ^ turn) for i in range(owners)])
    half = WIDTH // 2
    weights, summed = summed[frames:frames + 1], summed[:frames]
    frame_sum = jnp.sum(summed, axis=1)
    lane = jnp.arange(half)[None, :]
    skip = 2 * nrows - half
    mine = jnp.where(lane == FREE - 1, weights[:, :half], summed[:, :half])
    mine = jnp.where(lane == FREE, frame_sum[:, None], mine)
    extra = jnp.where(lane == 0, frame_sum[:, None], summed[:, skip:])
    def flip(turn):
        return [(a * owners + b, b * owners + (a ^ turn)) for a in range(wide) for b in range(owners)]

    mine, extra = lax.ppermute(mine, ALL, flip(0)), lax.ppermute(extra, ALL, flip(1))
    total = mine[:, FREE] + extra[:, 0] + lax.ppermute(frame_sum, ALL, flip(2)) + lax.ppermute(frame_sum, ALL, flip(3))
    weight_sum = mine[:, FREE - 1]
    charges = (mine[:, :nrows] + extra[:, nrows - skip:]).reshape(frames, panels, rows).transpose(1, 2, 0)
    return finish(charges, total, weight_sum, profile)


def solution(mesh):
    wide = mesh.shape["wide"]
    owners = mesh.shape["narrow"] * mesh.shape["sub"]
    plan = line_plan if wide == owners == 4 else gather_plan

    def local(slab, noise, volts, labels, profile):
        return plan(slab, noise, volts, labels, profile, (wide, owners))

    return jax.shard_map(
        local,
        mesh=mesh,
        in_specs=(
            P(None, "wide", ("narrow", "sub")),
            P(("grp", "wide"), ("narrow", "sub")),
            P(("grp", "wide"), None),
            P(("narrow", "sub")),
            P(None, ("narrow", "sub")),
        ),
        out_specs=P(None, ("narrow", "sub"), ("grp", "wide")),
        check_vma=False,
    )
```
